32 devices in a mesh: tp: 4 (over y, x), dp: 8 (over z, core).
Axes of the slice: x: 2, y: 2, z: 4, core: 2. Of those that a mesh axis runs over, the one named last changes fastest.
Arguments:
- tokens: bfloat16 [8, 1024, 1152], P('dp', 'tp'), may hold values from -6 to 6
- condition: bfloat16 [16, 1152], P('dp'), may hold values from -6 to 6
- modulator: bfloat16 [1152, 6, 1152], P(None, None, 'tp'), may hold values from -0.1875 to 0.1875
- offsets: float32 [6, 1152], replicated, may hold values from -3 to 3
- inward: bfloat16 [1152, 3, 1152], P(None, None, 'tp'), may hold values from -0.1875 to 0.1875
- query_gain: float32 [72], replicated, may hold values from 0.1 to 1.9
- key_gain: float32 [72], replicated, may hold values from 0.1 to 1.9
- outward: bfloat16 [1152, 1152], P(None, 'tp'), may hold values from -1 to 1
- expansion: bfloat16 [1152, 2, 3072], P(None, None, 'tp'), may hold values from -0.1875 to 0.1875
- contraction: bfloat16 [1152, 3072], P(None, 'tp'), may hold values from -0.109375 to 0.109375
- item_lengths: int32 [8, 4], P('dp'), may hold values from 1 to 832, 1024 in all within a row
- item_condition: int32 [8, 4], P('dp'), may hold values from 0 to 1
- patch_rows: int32 [8, 1024], P('dp'), may hold values from 0 to 63
- patch_columns: int32 [8, 1024], P('dp'), may hold values from 0 to 63
- cotangent: bfloat16 [8, 1024, 1152], P('dp', 'tp'), may hold values from -6 to 6
Outputs:
- layer_output: bfloat16 [8, 1024, 1152], P('dp', 'tp')
- token_gradient: float32 [8, 1024, 1152], P('dp', 'tp')
- modulator_gradient: float32 [1152, 6, 1152], P('dp', None, 'tp')
- bias_gradient: float32 [6, 1152], replicated
- inward_gradient: float32 [1152, 3, 1152], P('dp', None, 'tp')
- query_gradient: float32 [72], replicated
- key_gradient: float32 [72], replicated
- outward_gradient: float32 [1152, 1152], P('dp', 'tp')
- expansion_gradient: float32 [1152, 2, 3072], P('dp', None, 'tp')
- contraction_gradient: float32 [1152, 3072], P('dp', 'tp')
The draws below stay inside these ranges and needn't reach their ends.
Inputs may be any that keep to these rules, and one draw needn't show every extreme that they name: `item_lengths`: the 4 lengths of each sequence sum to 1024; the largest of each sequence is exactly 832.
All inputs are finite; a program needn't handle non-finite values.
Results may differ from the reference program's by a relative error of at most 0.017.
Values may be sent and summed in bfloat16 or wider, within the bound.
No kernel may reach another device: no remote copies, remote signals or barrier semaphores. Data moves between devices by JAX's collectives and lax.ppermute only.
A program may use at most 192 MiB of HBM per device.

```python
import math
import jax
import jax.numpy as jnp
import numpy as np
from jax import lax

D = 1152
HEADS = 16
HEAD_DIM = 72
FF = 3072
SEQ_LEN = 1024
ITEMS = 4
SEQS = 1
COND_GRP = 2
BATCH = 8
CONDS = 16


def touch_ends(values, key, least, largest):
    longest = values.shape.index(max(values.shape))
    spots = []
    for shift in (0, 1):
        where = [jax.random.randint(jax.random.fold_in(key, axis), (), 0, length) for axis, length in enumerate(values.shape)]
        where[longest] = (where[longest] + shift) % values.shape[longest]
        spots.append(tuple(where))
    return values.at[spots[0]].set(least).at[spots[1]].set(largest)


def level_of(key, extent, shards, least, high):
    def one(dim, blocks):
        heights = jax.random.uniform(jax.random.fold_in(jax.random.fold_in(key, 6), dim), (blocks,), jnp.float32, least / len(shards), high / len(shards))
        return jnp.repeat(jnp.exp(heights), extent[dim] // blocks).reshape((-1,) + (1,) * (len(extent) - dim - 1))

    gain = one(*shards[0])
    for cut in shards[1:]:
        gain = gain * one(*cut)
    return gain


def split_up(count, total, limit, slope):
    loads = [(1 << 20) // math.isqrt(grade ** slope) + 1 for grade in range(2, count + 1)]
    rest, counts = total - limit - (count - 1), [1] * (count - 1)
    while rest > 0:
        free = [i for i in range(count - 1) if counts[i] < limit]
        whole, left = sum([loads[i] for i in free]), rest
        for i in free:
            addition = min(limit - counts[i], max(1, left * loads[i] // whole), rest)
            counts[i] = counts[i] + addition
            rest = rest - addition
    return np.array([limit] + counts)


def ragged(own_key, count, total, bound, lean):
    if count == 2:
        one = jax.random.randint(own_key, (), max(1, total - bound), min(bound, total - 1) + 1)
        return jnp.stack([one, total - one])
    tallies = jnp.asarray(split_up(count, total, bound, lean), jnp.int32)
    pairs = (count - 1) // 2
    donor, taker = tallies[1:1 + 2 * pairs:2], tallies[2:2 + 2 * pairs:2]
    room = jnp.minimum(donor - 1, bound - taker)
    shifted = jax.random.randint(jax.random.fold_in(own_key, 1), (pairs,), 0, 1 << 20) % (room + 1)
    tallies = tallies.at[1:1 + 2 * pairs:2].set(donor - shifted).at[2:2 + 2 * pairs:2].set(taker + shifted)
    return tallies[jax.random.permutation(jax.random.fold_in(own_key, 2), count)]


def normal_values(rng, shape, spread, most, cuts=(), held_as=jnp.bfloat16):
    drawn = jax.random.normal(rng, shape, jnp.float32) * spread
    if len(cuts) > 0:
        drawn = level_of(rng, shape, cuts, -0.22, 0.18) * drawn
    return jnp.clip(drawn, min=-most, max=most).astype(held_as)


def setup_inputs(seed: int = 0) -> dict:
    arg_keys = jax.random.split(jax.random.key(seed), 16)
    return {
        "tokens": normal_values(arg_keys[0], (BATCH, SEQ_LEN, D), 1.0, 6.0, ((0, 8), (1, 4))),
        "condition": normal_values(arg_keys[1], (CONDS, D), 1.0, 6.0, ((0, 8),)),
        "modulator": normal_values(arg_keys[2], (D, 6, D), D ** -0.5, 0.1875, ((2, 4),)),
        "offsets": normal_values(arg_keys[3], (6, D), 0.5, 3.0, (), jnp.float32),
        "inward": normal_values(arg_keys[4], (D, 3, D), D ** -0.5, 0.1875, ((2, 4),)),
        "query_gain": jnp.clip(1.0 + 0.18 * jax.random.normal(arg_keys[5], (HEAD_DIM,), jnp.float32), 0.1, 1.9),
        "key_gain": jnp.clip(1.0 + 0.18 * jax.random.normal(arg_keys[6], (HEAD_DIM,), jnp.float32), 0.1, 1.9),
        "outward": normal_values(arg_keys[7], (D, D), (D // 32) ** -0.5, 1.0, ((1, 4),)),
        "expansion": normal_values(arg_keys[8], (D, 2, FF), D ** -0.5, 0.1875, ((2, 4),)),
        "contraction": normal_values(arg_keys[9], (D, FF), FF ** -0.5, 0.109375, ((1, 4),)),
        "item_lengths": jax.vmap(lambda own: ragged(own, ITEMS, SEQ_LEN, 13 * SEQ_LEN // 16, 2))(jax.random.split(arg_keys[10], BATCH)).reshape((BATCH, ITEMS)).astype(jnp.int32),
        "item_condition": touch_ends(jax.random.randint(arg_keys[11], (BATCH, ITEMS), 0, COND_GRP), jax.random.fold_in(arg_keys[11], 1), 0, COND_GRP - 1).astype(jnp.int32),
        "patch_rows": touch_ends(jax.random.randint(arg_keys[12], (BATCH, SEQ_LEN), 0, 64), jax.random.fold_in(arg_keys[12], 1), 0, 63).astype(jnp.int32),
        "patch_columns": touch_ends(jax.random.randint(arg_keys[13], (BATCH, SEQ_LEN), 0, 64), jax.random.fold_in(arg_keys[13], 1), 0, 63).astype(jnp.int32),
        "cotangent": normal_values(arg_keys[14], (BATCH, SEQ_LEN, D), 1.0, 6.0, ((0, 8), (1, 4))),
    }


@jax.custom_vjp
def low(v):
    return lax.optimization_barrier(v.astype(jnp.bfloat16)).astype(jnp.float32)

@jax.custom_vjp
def low_back(v):
    return v

def low_keep(v):
    return (low(v), None)

def low_pass(kept, grad):
    return (grad,)

def back_keep(v):
    return (v, None)

def back_low(kept, grad):
    return (low(grad),)
low.defvjp(low_keep, low_pass)
low_back.defvjp(back_keep, back_low)

def layer_norm(values):
    center = values - lax.optimization_barrier(jnp.mean(values, axis=-1, keepdims=True))
    variance = lax.optimization_barrier(jnp.mean(center * center, axis=-1, keepdims=True))
    return center * lax.rsqrt(variance + 1e-06)

def modulate(values, shift, scaling):
    return layer_norm(values) * (1.0 + scaling) + shift

def rope_tables(patch_rows, patch_columns, head_dim):
    quarter = head_dim // 4
    frequency = 10000.0 ** (-jnp.arange(quarter, dtype=jnp.float32) / quarter)
    along_rows = patch_rows.astype(jnp.float32)[..., None] * frequency
    along_columns = patch_columns.astype(jnp.float32)[..., None] * frequency
    angles = jnp.concatenate([along_rows, along_rows, along_columns, along_columns], axis=-1)
    return (jnp.cos(angles), jnp.sin(angles))

def turn_half(values):
    quarter = values.shape[-1] // 4
    part_one = values[..., :quarter]
    part_two = values[..., quarter:2 * quarter]
    part_three = values[..., 2 * quarter:3 * quarter]
    part_four = values[..., 3 * quarter:]
    return jnp.concatenate([-part_two, part_one, -part_four, part_three], axis=-1)

def prepare(projected_rows, scaling, cosine, sine_table):
    normed = projected_rows * lax.rsqrt(lax.optimization_barrier(jnp.mean(projected_rows * projected_rows, axis=-1, keepdims=True)) + 1e-06) * scaling
    return normed * cosine + turn_half(normed) * sine_table

def item_number(lengths, full_len):
    item_ends = jnp.cumsum(lengths, axis=-1)
    positions = jnp.arange(full_len, dtype=jnp.int32)
    return lax.optimization_barrier(jnp.sum((positions[None, :, None] >= item_ends[:, None, :]).astype(jnp.int32), axis=-1))

def attend(queries, key_rows, values, owning_sequences):
    factor = 1.0 / math.sqrt(queries.shape[-1])
    scores = jnp.einsum('qhe,khe->hqk', queries, key_rows, precision=lax.Precision.HIGHEST) * factor
    scores = low_back(scores)
    same_item = (owning_sequences[:, None] == owning_sequences[None, :])[None]
    scores = jnp.where(same_item, scores, -1e+30)
    row_top = lax.optimization_barrier(jnp.max(scores, axis=-1, keepdims=True))
    weights = jnp.exp(scores - row_top)
    weights = weights / lax.optimization_barrier(jnp.sum(weights, axis=-1, keepdims=True))
    return jnp.einsum('hqk,khe->qhe', low(weights), values, precision=lax.Precision.HIGHEST)

def reference(tokens, condition, modulator, offsets, inward, query_gain, key_gain, outward, expansion, contraction, item_lengths, item_condition, patch_rows, patch_columns, cotangent):
    seq_count, full_len, width = tokens.shape
    exact = lax.Precision.HIGHEST
    owning_sequences = item_number(item_lengths, full_len)
    group_base = (jnp.arange(seq_count, dtype=jnp.int32) // SEQS * COND_GRP)[:, None]
    cond_slot = (jnp.take_along_axis(item_condition, owning_sequences, axis=1) + group_base).astype(jnp.int32)
    cosine, sine_table = rope_tables(patch_rows, patch_columns, HEAD_DIM)
    cosine = cosine[:, :, None, :]
    sine_table = sine_table[:, :, None, :]
    cond_low = low(jax.nn.silu(condition.astype(jnp.float32)))
    attend_block = jax.checkpoint(attend)

    def forward(stream, modulator_w, offsets_w, inward_w, query_scale, key_scale, outward_w, expansion_w, contraction_w):
        portion_shares = jnp.einsum('cd,dje->cje', cond_low, modulator_w, precision=exact) + offsets_w
        per_token = jnp.take(portion_shares, cond_slot, axis=0)
        shift_one, scale_one, gate_one, shift_two, scale_two, gate_two = [per_token[:, :, column] for column in range(6)]
        first_in = low(modulate(stream, shift_one, scale_one))
        projected_rows = low_back(jnp.einsum('bld,dje->blje', first_in, inward_w, precision=exact))
        head_shape = (seq_count, full_len, HEADS, HEAD_DIM)
        queries = low(prepare(projected_rows[:, :, 0].reshape(head_shape), query_scale, cosine, sine_table))
        key_rows = low(prepare(projected_rows[:, :, 1].reshape(head_shape), key_scale, cosine, sine_table))
        values = low(projected_rows[:, :, 2].reshape(head_shape))
        mixed = lax.map(lambda parts: attend_block(*parts), (queries, key_rows, values, owning_sequences))
        mixed = low(low_back(mixed.reshape(seq_count, full_len, width)))
        attended = low_back(jnp.einsum('bli,oi->blo', mixed, outward_w, precision=exact))
        middle = stream + gate_one * attended
        second_in = low(modulate(middle, shift_two, scale_two))
        gate_lifting_pair = low_back(jnp.einsum('bld,djf->bljf', second_in, expansion_w, precision=exact))
        hidden = low(jax.nn.silu(gate_lifting_pair[:, :, 0]) * gate_lifting_pair[:, :, 1])
        fed = low_back(jnp.einsum('blf,of->blo', hidden, contraction_w, precision=exact))
        return middle + gate_two * fed
    inputs = (tokens.astype(jnp.float32), modulator.astype(jnp.float32), offsets.astype(jnp.float32), inward.astype(jnp.float32), query_gain.astype(jnp.float32), key_gain.astype(jnp.float32), outward.astype(jnp.float32), expansion.astype(jnp.float32), contraction.astype(jnp.float32))
    result, pullback = jax.vjp(forward, *inputs)
    grads = pullback(cotangent.astype(jnp.float32))
    return (result.astype(jnp.bfloat16), grads[0], grads[1], grads[2], grads[3], grads[4], grads[5], grads[6], grads[7], grads[8])
```

```python
import math

import jax
import jax.numpy as jnp
from jax import lax
from jax.sharding import PartitionSpec as P

BF = jnp.bfloat16
F32 = jnp.float32


def dot(left, right, dims):
    return lax.dot_general(left, right, (dims, ((), ())), preferred_element_type=F32)


def flip(value, by):
    return lax.ppermute(value, "tp", [(i, i ^ by) for i in range(4)])


def gather_tp(own):
    half = own.shape[0] // 2
    one, two = flip(own, 1), flip(own, 2)
    three = (flip(one[:half], 2), flip(two[half:], 1))
    return [own, one, two, jnp.concatenate(three, axis=0)]


def scatter_tp(parts):
    half = parts[0].shape[0] // 2
    low = [part.astype(BF) for part in parts[1:]]
    via_one, via_two = flip(low[2][:half], 1), flip(low[2][half:], 2)
    for_one = jnp.concatenate([low[0][:half], low[0][half:] + via_two], axis=0)
    for_two = jnp.concatenate([low[1][:half] + via_one, low[1][half:]], axis=0)
    return parts[0].astype(F32) + flip(for_one, 1).astype(F32) + flip(for_two, 2).astype(F32)


def gather_small(own, dp):
    if dp != 8:
        return lax.all_gather(own, "dp", axis=0)
    me = lax.axis_index("dp")

    def swap(value, by):
        return lax.ppermute(value, "dp", [(i, i ^ by) for i in range(dp)])

    other = swap(own, 1)
    core = me % 2
    pair = jnp.where(core == 0, jnp.stack([own, other]), jnp.stack([other, own]))
    pairs = jnp.stack([pair, swap(pair, 2), swap(pair, 4), swap(pair, 6)])
    place = me // 2
    ordered = jnp.take(pairs, jnp.arange(4) ^ place, axis=0)
    return ordered.reshape((dp,) + own.shape)


def sum_tp_columns(values):
    cut = values.shape[-1] // 4
    me = lax.axis_index("tp")

    def piece(k):
        return lax.dynamic_slice_in_dim(values, (me ^ k) * cut, cut, values.ndim - 1)

    return piece(0) + flip(piece(1), 1) + flip(piece(2), 2) + flip(piece(3), 3)


def gather_tp_columns(own):
    me = lax.axis_index("tp")
    rel = jnp.stack([own, flip(own, 1), flip(own, 2), flip(own, 3)])
    ordered = jnp.take(rel, jnp.arange(4) ^ me, axis=0)
    return jnp.moveaxis(ordered, 0, -2).reshape(own.shape[:-1] + (4 * own.shape[-1],))


def norm(values):
    center = values - jnp.mean(values, axis=-1, keepdims=True)
    inverse = lax.rsqrt(jnp.mean(center * center, axis=-1, keepdims=True) + 1e-06)
    return center * inverse, inverse


def norm_back(grad, normed, inverse):
    return inverse * (
        grad
        - jnp.mean(grad, axis=-1, keepdims=True)
        - normed * jnp.mean(grad * normed, axis=-1, keepdims=True)
    )


def turn_half(values):
    quarter = values.shape[-1] // 4
    a, b, c, d = [values[..., i * quarter : (i + 1) * quarter] for i in range(4)]
    return jnp.concatenate([-b, a, -d, c], axis=-1)


def prepare(raw, gain, cosine, sine):
    normed = raw * lax.rsqrt(jnp.mean(raw * raw, axis=-1, keepdims=True) + 1e-06) * gain
    return normed * cosine + turn_half(normed) * sine


def masked_scores(queries, keys, owners):
    factor = 1.0 / math.sqrt(queries.shape[-1])
    scores = jnp.einsum("qhe,khe->hqk", queries, keys, preferred_element_type=F32) * factor
    return jnp.where((owners[:, None] == owners[None, :])[None], scores, -1e30)


def shards(
    tokens,
    condition,
    modulator,
    offsets,
    inward,
    query_gain,
    key_gain,
    outward,
    expansion,
    contraction,
    item_lengths,
    item_condition,
    patch_rows,
    patch_columns,
    cotangent,
):
    _, rows, width = tokens.shape
    full = patch_rows.shape[1]
    head = query_gain.shape[0]
    heads = inward.shape[2] // head
    part = inward.shape[2]
    dp = lax.axis_size("dp")
    me = lax.axis_index("tp")
    dp_me = lax.axis_index("dp")
    lanes = width // dp

    x = tokens[0]
    x_all = gather_tp(x)
    cond_low = jax.nn.silu(condition.astype(F32)).astype(BF)
    share = dot(cond_low, modulator, ((1,), (0,)))
    table = gather_tp_columns(share) + offsets
    dy = cotangent[0]
    dy_all = gather_tp(dy)
    cond_all = gather_small(cond_low, dp).reshape(2 * dp, width)

    order = jnp.arange(4) ^ me

    def relative(values):
        return jnp.take(values.reshape(4, rows), order, axis=0).reshape(full)

    ends = jnp.cumsum(item_lengths[0])
    owners = jnp.sum((jnp.arange(full)[:, None] >= ends[None, :]).astype(jnp.int32), axis=-1)
    owners = relative(owners)
    item_hot = owners[:, None] == jnp.arange(item_lengths.shape[1])
    second = jnp.sum(jnp.where(item_hot, item_condition[0][None, :], 0), axis=-1) == 1
    second = second[:, None]

    def per_token(column, k):
        pick = second[k * rows : (k + 1) * rows]
        return jnp.where(pick, table[1, column], table[0, column])

    quarter = head // 4
    frequency = 10000.0 ** (-jnp.arange(quarter, dtype=F32) / quarter)
    along_rows = relative(patch_rows[0]).astype(F32)[:, None] * frequency
    along_columns = relative(patch_columns[0]).astype(F32)[:, None] * frequency
    angles = jnp.concatenate([along_rows, along_rows, along_columns, along_columns], axis=-1)
    cosine, sine = jnp.cos(angles)[:, None], jnp.sin(angles)[:, None]

    inward_flat = inward.reshape(width, 3 * part)
    expansion_flat = expansion.reshape(width, -1)
    first_in, first_normed, first_inverse, projected = [], [], [], []
    for k in range(4):
        normed, inverse = norm(x_all[k].astype(F32))
        low = (normed * (1.0 + per_token(1, k)) + per_token(0, k)).astype(BF)
        first_in.append(low)
        if k == 0:
            first_normed, first_inverse = normed, inverse
        projected.append(dot(low, inward_flat, ((1,), (0,))))
    first_in = jnp.concatenate(first_in, axis=0)
    projected = jnp.concatenate(projected, axis=0).reshape(full, 3, heads, head)
    query_raw, key_raw = projected[:, 0], projected[:, 1]
    queries = prepare(query_raw, query_gain, cosine, sine).astype(BF)
    keys = prepare(key_raw, key_gain, cosine, sine).astype(BF)
    values = projected[:, 2].astype(BF)

    scores = masked_scores(queries, keys, owners)
    top = jnp.max(scores, axis=-1, keepdims=True)
    weights = jnp.exp(scores - top)
    total = jnp.sum(weights, axis=-1, keepdims=True)
    rounded = (weights / total).astype(BF)
    mixed = jnp.einsum("hqk,khe->qhe", rounded, values, preferred_element_type=F32)
    log_total = top + jnp.log(total)
    mixed_low = mixed.reshape(full, part).astype(BF)

    def cut(array, k):
        return array[k * rows : (k + 1) * rows]

    attended = scatter_tp([dot(cut(mixed_low, k), outward, ((1,), (1,))) for k in (0, 1, 2, 3)])
    stream = x.astype(F32)
    gate_one = per_token(2, 0)
    middle = stream + gate_one * attended
    second_normed, second_inverse = norm(middle)
    second_scale = 1.0 + per_token(4, 0)
    second_own = (second_normed * second_scale + per_token(3, 0)).astype(BF)
    second_all = gather_tp(second_own)
    fed_grad = jnp.concatenate(
        [(per_token(5, k) * dy_all[k].astype(F32)).astype(BF) for k in range(4)], axis=0
    )
    hidden_grad = dot(fed_grad, contraction, ((1,), (0,)))
    hidden, widening, second_parts, fed_parts = [], [], [], []
    units = contraction.shape[1]
    for k in range(4):
        both = dot(second_all[k], expansion_flat, ((1,), (0,)))
        gate, up = both[:, :units], both[:, units:]
        sigmoid = jax.nn.sigmoid(gate)
        active = gate * sigmoid
        hidden.append((active * up).astype(BF))
        grad = cut(hidden_grad, k)
        gate_grad = grad * up * (sigmoid + active * (1.0 - sigmoid))
        widening.append(jnp.concatenate([gate_grad, grad * active], axis=1).astype(BF))
        second_parts.append(dot(widening[k], expansion_flat, ((1,), (1,))))
    second_grad = scatter_tp(second_parts)
    fed_parts = [dot(hidden[k], contraction, ((1,), (1,))) for k in range(4)]
    fed = scatter_tp(fed_parts)
    upstream = dy.astype(F32)
    layer_output = (middle + per_token(5, 0) * fed).astype(BF)
    hidden = jnp.concatenate(hidden, axis=0)
    widening = jnp.concatenate(widening, axis=0)
    second_in = jnp.concatenate(second_all, axis=0)
    wide = jnp.concatenate(
        [
            dot(second_in, widening, ((0,), (0,))).astype(BF),
            dot(fed_grad, hidden, ((0,), (0,))).astype(BF),
        ],
        axis=1,
    )
    wide = lax.psum_scatter(wide, "dp", scatter_dimension=0, tiled=True)

    middle_grad = upstream + norm_back(second_grad * second_scale, second_normed, second_inverse)
    attended_grad = jnp.concatenate(gather_tp((gate_one * middle_grad).astype(BF)), axis=0)
    mixed_grad = dot(attended_grad, outward, ((1,), (0,))).astype(BF)
    outward_grad = dot(attended_grad, mixed_low, ((0,), (0,)))
    mixed_grad = mixed_grad.reshape(full, heads, head)

    factor = 1.0 / math.sqrt(head)
    weights = jnp.exp(masked_scores(queries, keys, owners) - log_total)
    value_grad = jnp.einsum("hqk,qhe->khe", weights.astype(BF), mixed_grad, preferred_element_type=F32)
    weight_grad = jnp.einsum("qhe,khe->hqk", mixed_grad, values, preferred_element_type=F32)
    centre = jnp.sum(weights * weight_grad, axis=-1, keepdims=True)
    score_grad = (weights * (weight_grad - centre)).astype(BF)
    query_grad = jnp.einsum("hqk,khe->qhe", score_grad, keys, preferred_element_type=F32) * factor
    key_grad = jnp.einsum("hqk,qhe->khe", score_grad, queries, preferred_element_type=F32) * factor

    def both_heads(query_in, key_in, query_scale, key_scale):
        return (
            prepare(query_in, query_scale, cosine, sine),
            prepare(key_in, key_scale, cosine, sine),
        )

    _, pull = jax.vjp(both_heads, query_raw, key_raw, query_gain, key_gain)
    query_raw_grad, key_raw_grad, query_gain_grad, key_gain_grad = pull((query_grad, key_grad))
    projected_grad = jnp.stack([query_raw_grad, key_raw_grad, value_grad], axis=1)
    projected_grad = projected_grad.reshape(full, 3 * part).astype(BF)
    inward_grad = dot(first_in, projected_grad, ((0,), (0,)))
    narrow = jnp.concatenate([inward_grad.astype(BF), outward_grad.astype(BF)], axis=1)
    narrow = lax.psum_scatter(narrow, "dp", scatter_dimension=0, tiled=True)
    first_grad = scatter_tp([dot(cut(projected_grad, k), inward_flat, ((1,), (1,))) for k in range(4)])
    token_gradient = middle_grad + norm_back(
        first_grad * (1.0 + per_token(1, 0)), first_normed, first_inverse
    )

    pick = second[:rows]

    def slots(values):
        return jnp.stack([jnp.sum(jnp.where(pick, 0.0, values), axis=0), jnp.sum(jnp.where(pick, values, 0.0), axis=0)])

    mod = jnp.stack(
        [
            slots(first_grad),
            slots(first_grad * first_normed),
            slots(middle_grad * attended),
            slots(second_grad),
            slots(second_grad * second_normed),
            slots(upstream * fed),
        ],
        axis=1,
    )
    gains = jnp.concatenate([query_gain_grad, key_gain_grad])
    gains = jnp.pad(gains, (0, part - 2 * head))
    gains = jnp.broadcast_to(gains, (1, 4, part)).reshape(1, 4 * part)
    flat = jnp.concatenate([mod.reshape(12, width), gains], axis=0)
    every = gather_small(sum_tp_columns(flat), dp)
    gain_sum = jnp.sum(every[:, 12], axis=0)
    slot_share = every[:, :12].reshape(2 * dp, 6, part)
    bias_gradient = gather_tp_columns(jnp.sum(slot_share, axis=0))
    cond_rows = lax.dynamic_slice_in_dim(cond_all, dp_me * lanes, lanes, 1).astype(F32)
    modulator_gradient = jnp.einsum("cd,cje->dje", cond_rows, slot_share, precision=lax.Precision.HIGHEST)

    wide, narrow = wide.astype(F32), narrow.astype(F32)
    return (
        layer_output[None],
        token_gradient[None],
        modulator_gradient,
        bias_gradient,
        narrow[:, : 3 * part].reshape(lanes, 3, part),
        gain_sum[:head],
        gain_sum[head : 2 * head],
        narrow[:, 3 * part :],
        wide[:, : 2 * units].reshape(lanes, 2, units),
        wide[:, 2 * units :],
    )


def solution(mesh):
    placed = (
        P("dp", "tp", None),
        P("dp", None),
        P(None, None, "tp"),
        P(),
        P(None, None, "tp"),
        P(),
        P(),
        P(None, "tp"),
        P(None, None, "tp"),
        P(None, "tp"),
        P("dp", None),
        P("dp", None),
        P("dp", None),
        P("dp", None),
        P("dp", "tp", None),
    )
    return jax.shard_map(
        shards,
        mesh=mesh,
        in_specs=placed,
        out_specs=(
            P("dp", "tp", None),
            P("dp", "tp", None),
            P("dp", None, "tp"),
            P(),
            P("dp", None, "tp"),
            P(),
            P(),
            P("dp", "tp"),
            P("dp", None, "tp"),
            P("dp", "tp"),
        ),
        check_vma=False,
    )
```

```python
import functools
import math

import jax
import jax.numpy as jnp
from jax import lax
from jax.experimental import pallas as pl
from jax.experimental.pallas import tpu as pltpu
from jax.sharding import PartitionSpec as P

BF = jnp.bfloat16
F32 = jnp.float32
LANES = 128
EPS = 1e-06
NN = ((1,), (0,))
NT = ((1,), (1,))
TN = ((0,), (0,))
MASKED = -30000.0


def dot(left, right, dims):
    return lax.dot_general(left, right, (dims, ((), ())), preferred_element_type=F32)


def flip(value, by):
    return lax.ppermute(value, "tp", [(i, i ^ by) for i in range(4)])


def relay(one, two):
    half = one.shape[0] // 2
    return flip(one[:half], 2), flip(two[half:], 1)


def scatter_first(far):
    half = far.shape[0] // 2
    return flip(far[:half], 1), flip(far[half:], 2)


def join_kernel(near_ref, via_one_ref, via_two_ref, one_ref, two_ref):
    rows = one_ref.shape[0]
    half = rows // 2
    one_ref[:half, :] = near_ref[:half, :]
    one_ref[half:, :] = near_ref[half:rows, :] + via_two_ref[...]
    two_ref[:half, :] = near_ref[rows : rows + half, :] + via_one_ref[...]
    two_ref[half:, :] = near_ref[rows + half :, :]


def scatter_second(near, got):
    out = like(near.shape[0] // 2, near.shape[1], dtype=near.dtype)
    one, two = kernel_call(join_kernel, [out, out], near, *got, name="join")
    return flip(one, 1), flip(two, 2)


def gather_small(own, dp):
    if dp != 8:
        return lax.all_gather(own, "dp", axis=0)
    me = lax.axis_index("dp")

    def swap(value, by):
        return lax.ppermute(value, "dp", [(i, i ^ by) for i in range(dp)])

    other = swap(own, 1)
    core = me % 2
    pair = jnp.where(core == 0, jnp.stack([own, other]), jnp.stack([other, own]))
    pairs = jnp.stack([pair, swap(pair, 2), swap(pair, 4), swap(pair, 6)])
    ordered = jnp.take(pairs, jnp.arange(4) ^ (me // 2), axis=0)
    return ordered.reshape((dp,) + own.shape)


def sum_tp_columns(values):
    cut = values.shape[-1] // 4
    me = lax.axis_index("tp")

    def piece(k):
        return lax.dynamic_slice_in_dim(values, (me ^ k) * cut, cut, values.ndim - 1)

    return piece(0) + flip(piece(1), 1) + flip(piece(2), 2) + flip(piece(3), 3)


def columns_kernel(pieces, order_ref, *refs):
    add_ref, out_ref = refs[pieces:]
    stacked = jnp.stack([ref[...] for ref in refs[:pieces]])
    parts = []
    for j in range(pieces):
        part = stacked[0]
        for k in range(1, pieces):
            part = jnp.where(order_ref[j] == k, stacked[k], part)
        parts.append(part)
    out_ref[...] = jnp.concatenate(parts, axis=1) + add_ref[...]


def gather_tp_columns(own, add):
    order = jnp.arange(4, dtype=jnp.int32) ^ lax.axis_index("tp")
    (out,) = kernel_call(
        functools.partial(columns_kernel, 4),
        [like(own.shape[0], 4 * own.shape[1])],
        order, own, flip(own, 1), flip(own, 2), flip(own, 3), add,
        scalars=1,
        name="columns",
    )
    return out


def kernel_call(body, outs, *args, aliases=None, name=None, scalars=0, us=1.0):
    spec = pl.BlockSpec(memory_space=pltpu.VMEM)
    given = [pl.BlockSpec(memory_space=pltpu.SMEM)] * scalars + [spec] * (len(args) - scalars)
    return pl.pallas_call(
        body,
        out_shape=outs,
        in_specs=given,
        out_specs=[spec] * len(outs),
        input_output_aliases=aliases or {},
        compiler_params=pltpu.CompilerParams(vmem_limit_bytes=24 * 1024 * 1024),
        cost_estimate=pl.CostEstimate(flops=int(us * 1.15e9), bytes_accessed=1, transcendentals=0),
        name=name,
    )(*args)


def like(*shape, dtype=F32):
    return jax.ShapeDtypeStruct(shape, dtype)


def norm(values):
    count = values.shape[-1]
    center = values - jnp.sum(values, axis=-1, keepdims=True) * (1.0 / count)
    inverse = lax.rsqrt(jnp.sum(center * center, axis=-1, keepdims=True) * (1.0 / count) + EPS)
    return center * inverse, inverse


def norm_back(grad, normed, inverse):
    count = grad.shape[-1]
    middle = jnp.sum(grad, axis=-1, keepdims=True) * (1.0 / count)
    slope = jnp.sum(grad * normed, axis=-1, keepdims=True) * (1.0 / count)
    return inverse * (grad - middle - normed * slope)


def choose(pick, table_ref, column):
    return jnp.where(pick, table_ref[6 + column : 7 + column, :], table_ref[column : column + 1, :])


def slot_sums(pick, values):
    zero = jnp.zeros_like(values)
    return [
        jnp.sum(jnp.where(pick, zero, values), axis=0, keepdims=True),
        jnp.sum(jnp.where(pick, values, zero), axis=0, keepdims=True),
    ]


def picks(pick_ref, width):
    return jnp.broadcast_to(pick_ref[:, 0:1], (pick_ref.shape[0], width)) > 0.5


def widen(values):
    return jnp.concatenate(
        [values, jnp.zeros((values.shape[0], LANES - values.shape[1]), values.dtype)], axis=1
    )


def stack_rows(refs):
    return refs[0][...] if len(refs) == 1 else jnp.concatenate([ref[...] for ref in refs], axis=0)


def setup_kernel(head, items, spans, ends_ref, conds_ref, order_ref, places_ref, *out_refs):
    rows = places_ref.shape[0] // 4
    quarter = head // 4
    for s, (low, high) in enumerate(spans):
        count = high - low
        shape = (count, LANES)
        lane = lax.broadcasted_iota(jnp.int32, shape, 1)
        row = lax.broadcasted_iota(jnp.int32, shape, 0)
        start = jnp.full(shape, order_ref[low // rows] * rows, jnp.int32)
        if count > rows:
            start = jnp.where(row >= rows, order_ref[low // rows + 1] * rows - rows, start)
        token = start + row
        owner = jnp.zeros(shape, jnp.int32)
        for j in range(items):
            owner = owner + (token >= ends_ref[j]).astype(jnp.int32)
        pick = jnp.zeros(shape, jnp.int32)
        for j in range(items):
            pick = jnp.where(owner == j, conds_ref[j], pick)
        place = jnp.where(
            lane < 2 * quarter,
            jnp.broadcast_to(places_ref[low:high, 0:1], shape),
            jnp.broadcast_to(places_ref[low:high, 1:2], shape),
        )
        phase = lane
        for j in range(1, 4):
            phase = jnp.where(lane >= j * quarter, lane - j * quarter, phase)
        angles = place * jnp.exp(phase.astype(F32) * (-math.log(10000.0) / quarter))
        real = lane < head
        sine = jnp.sin(angles)
        lower = (lane < quarter) | ((lane >= 2 * quarter) & (lane < 3 * quarter))
        zero = jnp.zeros(shape, F32)
        rot_ref, aux_ref, pick_ref = out_refs[3 * s : 3 * s + 3]
        rot_ref[0] = jnp.where(real, jnp.cos(angles), zero)
        rot_ref[1] = jnp.where(real & lower, -sine, zero)
        rot_ref[2] = jnp.where(real & ~lower, sine, zero)
        base = head + 8
        mine = jnp.where(lane == owner + base, 1.0, 0.0)
        aux_ref[0] = mine
        marks = jnp.where((lane >= head + 4) & (lane < head + 7), 1.0, zero)
        slots = (lane >= base) & (lane < base + items)
        aux_ref[1] = jnp.where(slots, MASKED * (1.0 - mine), marks)
        pick_ref[...] = pick.astype(F32)


def enter_kernel(head, count, *refs):
    x = stack_rows(refs[:count])
    pick_ref, table_ref, rot_ref, aux_ref, gain_ref, weight_ref = refs[count : count + 6]
    first_ref, query_ref, key_ref, value_ref, raw_ref = refs[count + 6 :]
    rows, width = x.shape
    part = weight_ref.shape[0] // 3
    heads = part // head
    pick = picks(pick_ref, width)
    normed, _ = norm(x.astype(F32))
    low = (normed * (1.0 + choose(pick, table_ref, 1)) + choose(pick, table_ref, 0)).astype(BF)
    first_ref[...] = low
    raw = dot(low, weight_ref[...], NT)
    cosine, near, far = rot_ref[0], rot_ref[1], rot_ref[2]
    scale = math.log2(math.e) / math.sqrt(head)
    for kind in range(2):
        gain = gain_ref[kind : kind + 1, :]
        if kind == 0:
            gain = gain * scale
        target = (query_ref, key_ref)[kind]
        for h in range(heads):
            at = kind * part + h * head
            own = widen(raw[:, at : at + head])
            place = pl.ds((kind * heads + h) * LANES, LANES)
            raw_ref[:, place] = own
            inverse = lax.rsqrt(jnp.sum(own * own, axis=-1, keepdims=True) * (1.0 / head) + EPS)
            own = own * inverse * gain
            turned = (
                own * cosine
                + pltpu.roll(own, LANES - head // 4, 1) * near
                + pltpu.roll(own, head // 4, 1) * far
            )
            target[:, pl.ds(h * LANES, LANES)] = (turned + aux_ref[kind]).astype(BF)
    lane = lax.broadcasted_iota(jnp.int32, (rows, LANES), 1)
    ones = ((lane >= head) & (lane < head + 3)).astype(F32)
    for h in range(heads):
        at = 2 * part + h * head
        value_ref[:, pl.ds(h * LANES, LANES)] = (widen(raw[:, at : at + head]) + ones).astype(BF)


def split_three(value):
    one = value.astype(BF).astype(F32)
    rest = value - one
    two = rest.astype(BF).astype(F32)
    return one, two, rest - two


def forward_kernel(head, pieces, query_ref, *refs):
    keys, values = refs[:pieces], refs[pieces : 2 * pieces]
    outward_ref, partial_ref, mixed_ref, again_ref = refs[2 * pieces :]
    rows = query_ref.shape[0]
    heads = query_ref.shape[1] // LANES
    lane = lax.broadcasted_iota(jnp.int32, (rows, LANES), 1)
    mixed = []
    for h in range(heads):
        place = pl.ds(h * LANES, LANES)
        query = query_ref[:, place]
        out = None
        for key_ref, value_ref in zip(keys, values):
            weights = jnp.exp2(dot(query, key_ref[:, place], NT)).astype(BF)
            term = dot(weights, value_ref[:, place], NN)
            out = term if out is None else out + term
        total = out[:, head : head + 1]
        mixed.append((out[:, :head] * (1.0 / total)).astype(BF))
        one, two, three = split_three(-jnp.log2(total))
        marks = jnp.where(lane == head + 4, one, 0.0)
        marks = jnp.where(lane == head + 5, two, marks)
        marks = jnp.where(lane == head + 6, three, marks)
        again_ref[:, place] = (query.astype(F32) + marks).astype(BF)
    mixed = jnp.concatenate(mixed, axis=1)
    mixed_ref[...] = mixed
    partial_ref[...] = dot(mixed, outward_ref[...], NN).astype(partial_ref.dtype)


def backward_kernel(head, pieces, first, count, *refs):
    sent = stack_rows(refs[:count])
    outward_ref, mixed_ref, query_ref = refs[count : count + 3]
    refs = refs[count + 3 :]
    keys, values = refs[:pieces], refs[pieces : 2 * pieces]
    refs = refs[2 * pieces :]
    if not first:
        key_in, value_in = refs[:pieces], refs[pieces : 2 * pieces]
        refs = refs[2 * pieces :]
    query_out = refs[0]
    key_out, value_out = refs[1 : 1 + pieces], refs[1 + pieces :]
    rows = query_ref.shape[0]
    heads = query_ref.shape[1] // LANES
    lane = lax.broadcasted_iota(jnp.int32, (rows, LANES), 1)
    grads = dot(sent, outward_ref[...], NT).astype(BF).astype(F32)
    mixed = mixed_ref[...].astype(F32)
    for h in range(heads):
        place = pl.ds(h * LANES, LANES)
        cut = slice(h * head, (h + 1) * head)
        grad = grads[:, cut]
        centre = jnp.sum(grad * mixed[:, cut], axis=-1, keepdims=True)
        one, two, three = split_three(-centre)
        grad = widen(grad)
        grad = jnp.where(lane == head, one, grad)
        grad = jnp.where(lane == head + 1, two, grad)
        grad = jnp.where(lane == head + 2, three, grad).astype(BF)
        query = query_ref[:, place]
        query_grad = None
        for j in range(pieces):
            key, value = keys[j][:, place], values[j][:, place]
            weights = jnp.exp2(dot(key, query, NT))
            score_grad = (weights * dot(value, grad, NT)).astype(BF)
            value_grad = dot(weights.astype(BF), grad, NN)
            key_grad = dot(score_grad, query, NN)
            if not first:
                value_grad += value_in[j][:, place]
                key_grad += key_in[j][:, place]
            value_out[j][:, place] = value_grad
            key_out[j][:, place] = key_grad
            term = dot(score_grad, key, TN)
            query_grad = term if query_grad is None else query_grad + term
        query_out[:, place] = query_grad


def leave_kernel(head, count, *refs):
    x = stack_rows(refs[:count])
    query_grad_ref, key_grad_ref, value_grad_ref, raw_ref, rot_ref, gain_ref = refs[count : count + 6]
    weight_ref, pick_ref, projected_ref, partial_ref, slots_ref, gains_ref = refs[count + 6 :]
    rows, width = x.shape
    part = weight_ref.shape[0] // 3
    heads = part // head
    cosine, near, far = rot_ref[0], rot_ref[1], rot_ref[2]
    pieces = []
    for kind in range(2):
        gain = gain_ref[kind : kind + 1, :]
        source = (query_grad_ref, key_grad_ref)[kind]
        scale = (1.0 / math.sqrt(head), math.log(2.0))[kind]
        gain_grad = None
        for h in range(heads):
            grad = source[:, pl.ds(h * LANES, LANES)] * scale
            grad = (
                grad * cosine
                + pltpu.roll(grad * near, head // 4, 1)
                + pltpu.roll(grad * far, LANES - head // 4, 1)
            )
            own = raw_ref[:, pl.ds((kind * heads + h) * LANES, LANES)]
            inverse = lax.rsqrt(jnp.sum(own * own, axis=-1, keepdims=True) * (1.0 / head) + EPS)
            own = own * inverse
            term = jnp.sum(grad * own, axis=0, keepdims=True)
            gain_grad = term if gain_grad is None else gain_grad + term
            grad = grad * gain
            slope = jnp.sum(grad * own, axis=-1, keepdims=True) * (1.0 / head)
            pieces.append((inverse * (grad - own * slope))[:, :head].astype(BF))
        gains_ref[kind : kind + 1, :] = gain_grad
    for h in range(heads):
        pieces.append(value_grad_ref[:, pl.ds(h * LANES, head)].astype(BF))
    projected = jnp.concatenate(pieces, axis=1)
    projected_ref[...] = projected
    grad = dot(projected, weight_ref[...], NN)
    partial_ref[...] = grad.astype(partial_ref.dtype)
    pick = picks(pick_ref, width)
    normed, _ = norm(x.astype(F32))
    slots_ref[...] = jnp.concatenate(slot_sums(pick, grad) + slot_sums(pick, grad * normed), axis=0)


def middle_kernel(x_ref, own_ref, one_ref, two_ref, pick_ref, table_ref,
                  attended_ref, middle_ref, second_ref):
    attended = own_ref[...] + one_ref[...].astype(F32) + two_ref[...].astype(F32)
    attended_ref[...] = attended
    pick = picks(pick_ref, x_ref.shape[1])
    middle = x_ref[...].astype(F32) + choose(pick, table_ref, 2) * attended
    middle_ref[...] = middle
    normed, _ = norm(middle)
    second_ref[...] = (
        normed * (1.0 + choose(pick, table_ref, 4)) + choose(pick, table_ref, 3)
    ).astype(BF)


def units_kernel(count, *refs):
    second = stack_rows(refs[:count])
    grad_ref, weight_ref, hidden_ref, widening_ref, partial_ref = refs[count:]
    units = grad_ref.shape[1]
    both = dot(second, weight_ref[...], NN)
    gate, up = both[:, :units], both[:, units:]
    sigmoid = 1.0 / (1.0 + jnp.exp(-gate))
    active = gate * sigmoid
    hidden_ref[...] = (active * up).astype(BF)
    grad = grad_ref[...]
    gate_grad = (grad * up * (sigmoid + active * (1.0 - sigmoid))).astype(BF)
    widening = jnp.concatenate([gate_grad, (grad * active).astype(BF)], axis=1)
    widening_ref[...] = widening
    partial_ref[...] = dot(widening, weight_ref[...], NT).astype(partial_ref.dtype)


def hidden_grad_kernel(count, *refs):
    dy = stack_rows(refs[:count])
    pick_ref, table_ref, weight_ref, fed_ref, out_ref = refs[count:]
    pick = picks(pick_ref, dy.shape[1])
    fed = (choose(pick, table_ref, 5) * dy.astype(F32)).astype(BF)
    fed_ref[...] = fed
    out_ref[...] = dot(fed, weight_ref[...], NN)


def fed_part_kernel(hidden_ref, weight_ref, out_ref):
    out_ref[...] = dot(hidden_ref[...], weight_ref[...], NT).astype(out_ref.dtype)


def weights_kernel(counts, *refs):
    out_ref = refs[-1]
    at = 0
    for lefts, rights in counts:
        left, refs = stack_rows(refs[:lefts]), refs[lefts:]
        right, refs = stack_rows(refs[:rights]), refs[rights:]
        out_ref[:, at : at + right.shape[1]] = dot(left, right, TN).astype(BF)
        at += right.shape[1]


def weights_call(pairs, name):
    args, counts = [], []
    for lefts, rights in pairs:
        args += [*lefts, *rights]
        counts.append((len(lefts), len(rights)))
    height = pairs[0][0][0].shape[1]
    total = sum(rights[0].shape[1] for _, rights in pairs)
    (out,) = kernel_call(
        functools.partial(weights_kernel, counts), [like(height, total, dtype=BF)], *args, name=name, us=6.0
    )
    return out


def middle_back_kernel(own_ref, one_ref, two_ref, middle_ref, attended_ref, dy_ref, pick_ref, table_ref,
                       grad_ref, send_ref, slots_ref):
    pick = picks(pick_ref, dy_ref.shape[1])
    second_grad = own_ref[...] + one_ref[...].astype(F32) + two_ref[...].astype(F32)
    normed, inverse = norm(middle_ref[...])
    grad = dy_ref[...].astype(F32) + norm_back(
        second_grad * (1.0 + choose(pick, table_ref, 4)), normed, inverse
    )
    grad_ref[...] = grad
    send_ref[...] = (choose(pick, table_ref, 2) * grad).astype(BF)
    slots_ref[...] = jnp.concatenate(
        slot_sums(pick, grad * attended_ref[...])
        + slot_sums(pick, second_grad)
        + slot_sums(pick, second_grad * normed),
        axis=0,
    )


def fed_kernel(own_ref, one_ref, two_ref, middle_ref, dy_ref, pick_ref, table_ref, out_ref, slots_ref):
    pick = picks(pick_ref, dy_ref.shape[1])
    fed = own_ref[...] + one_ref[...].astype(F32) + two_ref[...].astype(F32)
    out_ref[...] = (middle_ref[...] + choose(pick, table_ref, 5) * fed).astype(BF)
    slots_ref[...] = jnp.concatenate(slot_sums(pick, dy_ref[...].astype(F32) * fed), axis=0)


def token_kernel(own_ref, one_ref, two_ref, x_ref, grad_ref, pick_ref, table_ref, out_ref):
    pick = picks(pick_ref, x_ref.shape[1])
    first_grad = own_ref[...] + one_ref[...].astype(F32) + two_ref[...].astype(F32)
    normed, inverse = norm(x_ref[...].astype(F32))
    out_ref[...] = grad_ref[...] + norm_back(
        first_grad * (1.0 + choose(pick, table_ref, 1)), normed, inverse
    )


def sync(*values):
    return lax.optimization_barrier(values)


def shards(
    tokens,
    condition,
    modulator,
    offsets,
    inward,
    query_gain,
    key_gain,
    outward,
    expansion,
    contraction,
    item_lengths,
    item_condition,
    patch_rows,
    patch_columns,
    cotangent,
):
    _, rows, width = tokens.shape
    full = patch_rows.shape[1]
    head = query_gain.shape[0]
    part = inward.shape[2]
    heads = part // head
    units = contraction.shape[1]
    items = item_lengths.shape[1]
    dp = lax.axis_size("dp")
    me = lax.axis_index("tp")
    dp_me = lax.axis_index("dp")
    lanes = width // dp
    padded = heads * LANES
    spans = ((0, rows), (rows, 3 * rows), (3 * rows, full))
    sizes = [high - low for low, high in spans]

    x, dy = tokens[0], cotangent[0]
    x_one, x_two = flip(x, 1), flip(x, 2)
    cond_low = jax.nn.silu(condition.astype(F32)).astype(BF)
    share = dot(cond_low, jnp.transpose(modulator, (1, 2, 0)).reshape(-1, width), NT)
    table = gather_tp_columns(share.reshape(12, part), jnp.concatenate([offsets, offsets], axis=0))
    inward_rows = jnp.transpose(inward, (1, 2, 0)).reshape(3 * part, width)
    outward_rows = outward.T
    expansion_flat = expansion.reshape(width, 2 * units)
    gains = jnp.pad(jnp.stack([query_gain, key_gain]), ((0, 0), (0, LANES - head)))
    order = jnp.arange(4, dtype=jnp.int32) ^ me
    places = jnp.stack([patch_rows[0], patch_columns[0]], axis=1).astype(F32)
    places = jnp.take(places.reshape(4, rows, 2), order, axis=0).reshape(full, 2)
    side = kernel_call(
        functools.partial(setup_kernel, head, items, spans),
        [
            out
            for n in sizes
            for out in (like(3, n, LANES), like(2, n, LANES), like(n, LANES))
        ],
        jnp.cumsum(item_lengths[0]), item_condition[0], order, places,
        scalars=3,
        name="setup", us=3.0,
    )
    x_one, x_two, dy, table, expansion_flat, *side = sync(
        x_one, x_two, dy, table, expansion_flat, *side
    )
    rot, aux, pick = side[0::3], side[1::3], side[2::3]

    x_far = relay(x_one, x_two)
    dy_one, dy_two = flip(dy, 1), flip(dy, 2)
    x_parts = [[x], [x_one, x_two], list(x_far)]

    def enter(k, parts):
        n = sizes[k]
        return kernel_call(
            functools.partial(enter_kernel, head, len(parts)),
            [
                like(n, width, dtype=BF),
                like(n, padded, dtype=BF),
                like(n, padded, dtype=BF),
                like(n, padded, dtype=BF),
                like(n, 2 * padded),
            ],
            *parts, pick[k], table, rot[k], aux[k], gains, inward_rows,
            name="enter", us=3.3 * n / rows,
        )

    entered = [list(enter(0, x_parts[0])), list(enter(1, x_parts[1]))]
    *x_far, entered[0][1], entered[1][1] = sync(*x_far, entered[0][1], entered[1][1])
    x_parts[2] = x_far

    entered.append(enter(2, x_far))
    first_in, queries, keys, values, raws = zip(*entered)

    def attend(k, query):
        n = sizes[k]
        return kernel_call(
            functools.partial(forward_kernel, head, 3),
            [
                like(n, width, dtype=F32 if k == 0 else BF),
                like(n, part, dtype=BF),
                like(n, padded, dtype=BF),
            ],
            query, *keys, *values, outward_rows,
            name="attend", us=2.0 * n / rows,
        )

    attended = [None, None, attend(2, queries[2])]
    far, query_near, dy_one, dy_two = sync(attended[2][0], queries[1], dy_one, dy_two)

    got = scatter_first(far)
    dy_far = relay(dy_one, dy_two)
    attended[1] = attend(1, query_near)
    near, query_own, *got = sync(attended[1][0], queries[0], *got)

    sums = scatter_second(near, got)
    attended[0] = attend(0, query_own)
    own, *both = sync(attended[0][0], *sums, *dy_far)
    sums, dy_far = both[:2], both[2:]

    attended_own, middle, second = kernel_call(
        middle_kernel,
        [like(rows, width), like(rows, width), like(rows, width, dtype=BF)],
        x, own, *sums, pick[0], table,
        name="middle", us=1.0,
    )
    second_one, second_two = flip(second, 1), flip(second, 2)
    dy_parts = [[dy], [dy_one, dy_two], dy_far]
    fed_grad, hidden_grad = [], []
    for k in range(3):
        outs = kernel_call(
            functools.partial(hidden_grad_kernel, len(dy_parts[k])),
            [like(sizes[k], width, dtype=BF), like(sizes[k], units)],
            *dy_parts[k], pick[k], table, contraction,
            name="hidden_grad", us=0.8 * sizes[k] / rows,
        )
        fed_grad.append(outs[0])
        hidden_grad.append(outs[1])
    cond_all = gather_small(cond_low, dp).reshape(2 * dp, width)
    second_one, second_two, cond_all, *hidden_grad = sync(
        second_one, second_two, cond_all, *hidden_grad
    )

    second_far = relay(second_one, second_two)
    second_parts = [[second], [second_one, second_two], list(second_far)]

    def through(k, parts):
        n = sizes[k]
        return kernel_call(
            functools.partial(units_kernel, len(parts)),
            [
                like(n, units, dtype=BF),
                like(n, 2 * units, dtype=BF),
                like(n, width, dtype=F32 if k == 0 else BF),
            ],
            *parts, hidden_grad[k], expansion_flat,
            name="units", us=2.5 * n / rows,
        )

    passed = [through(0, second_parts[0]), through(1, second_parts[1])]
    *second_far, near, own = sync(*second_far, passed[1][2], passed[0][2])
    second_parts[2] = second_far
    passed.append(through(2, second_far))
    hidden, widening, back = zip(*passed)
    far, hidden_far = sync(back[2], hidden[2])

    got = scatter_first(far)
    fed_parts = [None] * 3
    for k, source in ((2, hidden_far), (1, hidden[1]), (0, hidden[0])):
        (fed_parts[k],) = kernel_call(
            fed_part_kernel,
            [like(sizes[k], width, dtype=F32 if k == 0 else BF)],
            source, contraction,
            name="fed_part", us=0.7 * sizes[k] / rows,
        )
    *got, near, fed_far, fed_near, widening_far = sync(
        *got, near, fed_parts[2], fed_parts[1], widening[2]
    )

    sums = scatter_second(near, got)
    wide = weights_call(
        [
            (sum(second_parts, []), [*widening[:2], widening_far]),
            (fed_grad, hidden),
        ],
        "wide",
    )
    own, *sums, wide, fed_far = sync(own, *sums, wide, fed_far)
    wide = lax.psum_scatter(wide, "dp", scatter_dimension=0, tiled=True)

    fed_got = scatter_first(fed_far)
    middle_grad, send, slots_two = kernel_call(
        middle_back_kernel,
        [like(rows, width), like(rows, width, dtype=BF), like(6, width)],
        own, *sums, middle, attended_own, dy, pick[0], table,
        name="middle_back", us=1.7,
    )
    send_one, send_two = flip(send, 1), flip(send, 2)

    def attend_back(k, parts, sums):
        n = sizes[k]
        given = (*parts, outward_rows, attended[k][1], attended[k][2], *keys, *values)
        out = kernel_call(
            functools.partial(backward_kernel, head, 3, not sums, len(parts)),
            [like(n, padded)] + [like(a.shape[0], padded) for a in keys + values],
            *given, *sums,
            aliases={len(given) + i: 1 + i for i in range(len(sums))},
            name="attend_back", us=4.3 * n / rows,
        )
        return out[0], tuple(out[1:])

    query_grads = [None] * 3
    query_grads[0], totals = attend_back(0, [send], ())
    send_one, send_two, totals, fed_near, *fed_got = sync(
        send_one, send_two, totals, fed_near, *fed_got
    )

    send_far = relay(send_one, send_two)
    query_grads[1], totals = attend_back(1, [send_one, send_two], totals)
    *send_far, totals, fed_near = sync(*send_far, totals, fed_near)

    fed_sums = scatter_second(fed_near, fed_got)
    send_parts = [[send], [send_one, send_two], send_far]
    query_grads[2], totals = attend_back(2, send_far, totals)
    key_grads, value_grads = totals[:3], totals[3:]

    def leave(k, query_grad):
        n = sizes[k]
        return kernel_call(
            functools.partial(leave_kernel, head, len(x_parts[k])),
            [
                like(n, 3 * part, dtype=BF),
                like(n, width, dtype=F32 if k == 0 else BF),
                like(4, width),
                like(2, LANES),
            ],
            *x_parts[k], query_grad, key_grads[k], value_grads[k], raws[k], rot[k], gains,
            inward_rows, pick[k],
            name="leave", us=3.8 * n / rows,
        )

    left = [None, None, leave(2, query_grads[2])]
    far, query_near, *fed_sums = sync(left[2][1], query_grads[1], *fed_sums)

    got = scatter_first(far)
    left[1] = leave(1, query_near)
    near, query_own, *got = sync(left[1][1], query_grads[0], *got)

    sums = scatter_second(near, got)
    left[0] = leave(0, query_own)
    narrow = weights_call(
        [
            (first_in, [left[k][0] for k in range(3)]),
            (sum(send_parts, []), [attended[k][1] for k in range(3)]),
        ],
        "narrow",
    )
    layer_output, slots_fed = kernel_call(
        fed_kernel,
        [like(rows, width, dtype=BF), like(2, width)],
        fed_parts[0], *fed_sums, middle, dy, pick[0], table,
        name="fed", us=1.5,
    )
    own, *sums, wide, narrow, slots_fed = sync(left[0][1], *sums, wide, narrow, slots_fed)
    narrow = lax.psum_scatter(narrow, "dp", scatter_dimension=0, tiled=True)
    (token_gradient,) = kernel_call(
        token_kernel,
        [like(rows, width)],
        own, *sums, x, middle_grad, pick[0], table,
        name="token", us=2.0,
    )

    slots_one = left[0][2] + left[1][2] + left[2][2]
    gains_sum = left[0][3] + left[1][3] + left[2][3]
    mod = jnp.concatenate([slots_one, slots_two, slots_fed], axis=0)
    mod = jnp.transpose(mod.reshape(6, 2, width), (1, 0, 2)).reshape(12, width)
    gain_row = jnp.pad(gains_sum[:, :head].reshape(1, 2 * head), ((0, 0), (0, part - 2 * head)))
    flat = jnp.concatenate([mod, jnp.tile(gain_row, (1, 4))], axis=0)
    every = gather_small(sum_tp_columns(flat), dp)
    gain_sum = jnp.sum(every[:, 12], axis=0)
    slot_share = every[:, :12].reshape(2 * dp, 6, part)
    bias_gradient = gather_tp_columns(jnp.sum(slot_share, axis=0), jnp.zeros((6, width), F32))
    cond_rows = lax.dynamic_slice_in_dim(cond_all, dp_me * lanes, lanes, 1).astype(F32)
    modulator_gradient = jnp.einsum(
        "cd,cje->dje", cond_rows, slot_share, precision=lax.Precision.HIGHEST
    )

    wide, narrow = wide.astype(F32), narrow.astype(F32)
    return (
        layer_output[None],
        token_gradient[None],
        modulator_gradient,
        bias_gradient,
        narrow[:, : 3 * part].reshape(lanes, 3, part),
        gain_sum[:head],
        gain_sum[head : 2 * head],
        narrow[:, 3 * part :],
        wide[:, : 2 * units].reshape(lanes, 2, units),
        wide[:, 2 * units :],
    )


def solution(mesh):
    placed = (
        P("dp", "tp", None),
        P("dp", None),
        P(None, None, "tp"),
        P(),
        P(None, None, "tp"),
        P(),
        P(),
        P(None, "tp"),
        P(None, None, "tp"),
        P(None, "tp"),
        P("dp", None),
        P("dp", None),
        P("dp", None),
        P("dp", None),
        P("dp", "tp", None),
    )
    return jax.shard_map(
        shards,
        mesh=mesh,
        in_specs=placed,
        out_specs=(
            P("dp", "tp", None),
            P("dp", "tp", None),
            P("dp", None, "tp"),
            P(),
            P("dp", None, "tp"),
            P(),
            P(),
            P("dp", "tp"),
            P("dp", None, "tp"),
            P("dp", "tp"),
        ),
        check_vma=False,
    )
```

```python
import functools
import math

import jax
import jax.numpy as jnp
from jax import lax
from jax.experimental import pallas as pl
from jax.experimental.pallas import tpu as pltpu
from jax.sharding import PartitionSpec as P

BF = jnp.bfloat16
F32 = jnp.float32
LANES = 128
EPS = 1e-06
NN = ((1,), (0,))
NT = ((1,), (1,))
TN = ((0,), (0,))
MASKED = -30000.0


def dot(left, right, dims):
    return lax.dot_general(left, right, (dims, ((), ())), preferred_element_type=F32)


def flip(value, by):
    return lax.ppermute(value, "tp", [(i, i ^ by) for i in range(4)])


def halves(one, two):
    half = one.shape[0] // 2
    return one[:half], two[half:]


def relay(one, two):
    low, high = halves(one, two)
    return flip(low, 2), flip(high, 1)


def scatter_first(far):
    half = far.shape[0] // 2
    return flip(far[:half], 1), flip(far[half:], 2)


def total(*refs):
    return sum(ref[...].astype(F32) for ref in refs)


def join_kernel(near_ref, via_one_ref, via_two_ref, one_ref, two_ref):
    rows = one_ref.shape[0]
    half = rows // 2
    one_ref[:half, :] = near_ref[:half, :]
    one_ref[half:, :] = near_ref[half:rows, :] + via_two_ref[...]
    two_ref[:half, :] = near_ref[rows : rows + half, :] + via_one_ref[...]
    two_ref[half:, :] = near_ref[rows + half :, :]


def scatter_second(near, got):
    out = like(near.shape[0] // 2, near.shape[1], dtype=near.dtype)
    one, two = kernel_call(join_kernel, [out, out], near, *got, name="join")
    return flip(one, 1), flip(two, 2)


def gather_core(own, dp):
    return jnp.stack([own, swap(own, 1)]) if dp == 8 else own


def gather_chips(pair, dp):
    if dp != 8:
        return lax.all_gather(pair, "dp", axis=0)
    return jnp.concatenate([pair, swap(pair, 2), swap(pair, 4), swap(pair, 6)], axis=0)


def gather_small(own, dp):
    return gather_chips(gather_core(own, dp), dp)


def pack_kernel(order_ref, *refs):
    first, two_ref, fed, gains, out_refs = refs[:3], refs[3], refs[4:7], refs[7:10], refs[10:]
    cut = out_refs[0].shape[1]
    tall = jnp.concatenate([total(*first), two_ref[...], total(*fed)], axis=0)
    gain = total(*gains)
    gain = jnp.concatenate([gain, jnp.zeros((1, cut - gain.shape[1]), F32)], axis=1)
    parts = [tall[:, j * cut : (j + 1) * cut] for j in range(4)]
    for k in range(4):
        part = parts[0]
        for j in range(1, 4):
            part = jnp.where(order_ref[k] == j, parts[j], part)
        out_refs[k][...] = jnp.concatenate([part, gain], axis=0)


def slots_kernel(rows, conds_ref, every_ref, grad_ref, bias_ref, gain_ref):
    conds = conds_ref[...]
    gain_ref[...] = jnp.sum(every_ref[:, every_ref.shape[1] - 1, :], axis=0, keepdims=True)
    for j in range(6):
        both = [every_ref[:, rows[j][c], :] for c in range(2)]
        grad_ref[j] = lax.dot_general(
            conds,
            jnp.concatenate(both, axis=0),
            (TN, ((), ())),
            precision=lax.Precision.HIGHEST,
            preferred_element_type=F32,
        )
        bias_ref[j : j + 1, :] = jnp.sum(both[0] + both[1], axis=0, keepdims=True)


def columns_kernel(pieces, order_ref, *refs):
    add_ref, out_ref = refs[pieces:]
    stacked = jnp.stack([ref[...] for ref in refs[:pieces]])
    parts = []
    for j in range(pieces):
        part = stacked[0]
        for k in range(1, pieces):
            part = jnp.where(order_ref[j] == k, stacked[k], part)
        parts.append(part)
    out = jnp.concatenate(parts, axis=1)
    add = add_ref[...]
    if add.shape[0] < out.shape[0]:
        add = jnp.concatenate([add, add], axis=0)
    out_ref[...] = out + add


def gather_tp_columns(own, add):
    order = jnp.arange(4, dtype=jnp.int32) ^ lax.axis_index("tp")
    (out,) = kernel_call(
        functools.partial(columns_kernel, 4),
        [like(own.shape[0], 4 * own.shape[1])],
        order, own, flip(own, 1), flip(own, 2), flip(own, 3), add,
        scalars=1,
        name="columns",
    )
    return out


def kernel_call(body, outs, *args, aliases=None, name=None, scalars=0, us=1.0, mib=16, hbm=()):
    spec = pl.BlockSpec(memory_space=pltpu.VMEM)
    given = [pl.BlockSpec(memory_space=pltpu.SMEM)] * scalars + [spec] * (len(args) - scalars)
    return pl.pallas_call(
        body,
        out_shape=[pltpu.HBM(o.shape, o.dtype) if i in hbm else o for i, o in enumerate(outs)],
        in_specs=given,
        out_specs=[spec] * len(outs),
        input_output_aliases=aliases or {},
        compiler_params=pltpu.CompilerParams(vmem_limit_bytes=mib * 1024 * 1024),
        cost_estimate=pl.CostEstimate(flops=int(us * 1.15e9), bytes_accessed=1, transcendentals=0),
        name=name,
    )(*args)


def like(*shape, dtype=F32):
    return jax.ShapeDtypeStruct(shape, dtype)


def norm(values):
    count = values.shape[-1]
    center = values - jnp.sum(values, axis=-1, keepdims=True) * (1.0 / count)
    inverse = lax.rsqrt(jnp.sum(center * center, axis=-1, keepdims=True) * (1.0 / count) + EPS)
    return center * inverse, inverse


def norm_back(grad, normed, inverse):
    count = grad.shape[-1]
    middle = jnp.sum(grad, axis=-1, keepdims=True) * (1.0 / count)
    slope = jnp.sum(grad * normed, axis=-1, keepdims=True) * (1.0 / count)
    return inverse * (grad - middle - normed * slope)


def choose(pick, table_ref, column):
    return jnp.where(pick, table_ref[6 + column : 7 + column, :], table_ref[column : column + 1, :])


def slot_sums(pick, values):
    zero = jnp.zeros_like(values)
    return [
        jnp.sum(jnp.where(pick, zero, values), axis=0, keepdims=True),
        jnp.sum(jnp.where(pick, values, zero), axis=0, keepdims=True),
    ]


def picks(side_ref, width):
    return jnp.broadcast_to(side_ref[5][:, 0:1], (side_ref.shape[1], width)) > 0.5


def widen(values):
    return jnp.concatenate(
        [values, jnp.zeros((values.shape[0], LANES - values.shape[1]), values.dtype)], axis=1
    )


def stack_rows(refs):
    return refs[0][...] if len(refs) == 1 else jnp.concatenate([ref[...] for ref in refs], axis=0)


def setup_kernel(head, items, spans, ends_ref, conds_ref, order_ref, places_ref, *out_refs):
    rows = places_ref.shape[0] // 4
    quarter = head // 4
    for s, (low, high) in enumerate(spans):
        count = high - low
        shape = (count, LANES)
        lane = lax.broadcasted_iota(jnp.int32, shape, 1)
        row = lax.broadcasted_iota(jnp.int32, shape, 0)
        start = jnp.full(shape, order_ref[low // rows] * rows, jnp.int32)
        if count > rows:
            start = jnp.where(row >= rows, order_ref[low // rows + 1] * rows - rows, start)
        token = start + row
        owner = jnp.zeros(shape, jnp.int32)
        for j in range(items):
            owner = owner + (token >= ends_ref[j]).astype(jnp.int32)
        pick = jnp.zeros(shape, jnp.int32)
        for j in range(items):
            pick = jnp.where(owner == j, conds_ref[j], pick)
        place = jnp.where(
            lane < 2 * quarter,
            jnp.broadcast_to(places_ref[low:high, 0:1], shape),
            jnp.broadcast_to(places_ref[low:high, 1:2], shape),
        )
        phase = lane
        for j in range(1, 4):
            phase = jnp.where(lane >= j * quarter, lane - j * quarter, phase)
        angles = place * jnp.exp(phase.astype(F32) * (-math.log(10000.0) / quarter))
        real = lane < head
        sine = jnp.sin(angles)
        lower = (lane < quarter) | ((lane >= 2 * quarter) & (lane < 3 * quarter))
        zero = jnp.zeros(shape, F32)
        out_ref = out_refs[s]
        out_ref[0] = jnp.where(real, jnp.cos(angles), zero)
        out_ref[1] = jnp.where(real & lower, -sine, zero)
        out_ref[2] = jnp.where(real & ~lower, sine, zero)
        base = head + 8
        mine = jnp.where(lane == owner + base, 1.0, 0.0)
        out_ref[3] = mine
        marks = jnp.where((lane >= head + 4) & (lane < head + 7), 1.0, zero)
        slots = (lane >= base) & (lane < base + items)
        out_ref[4] = jnp.where(slots, MASKED * (1.0 - mine), marks)
        out_ref[5] = pick.astype(F32)


def enter_kernel(head, count, *refs):
    x = stack_rows(refs[:count])
    side_ref, table_ref, gain_ref, weight_ref = refs[count : count + 4]
    first_ref, query_ref, key_ref, value_ref, raw_ref = refs[count + 4 :]
    rows, width = x.shape
    part = weight_ref.shape[0] // 3
    heads = part // head
    pick = picks(side_ref, width)
    normed, _ = norm(x.astype(F32))
    low = (normed * (1.0 + choose(pick, table_ref, 1)) + choose(pick, table_ref, 0)).astype(BF)
    first_ref[...] = low
    raw = dot(low, weight_ref[...], NT)
    raw_ref[...] = raw[:, : 2 * part].astype(BF)
    cosine, near, far = side_ref[0], side_ref[1], side_ref[2]
    scale = math.log2(math.e) / math.sqrt(head)
    for kind in range(2):
        gain = gain_ref[kind : kind + 1, :]
        if kind == 0:
            gain = gain * scale
        target = (query_ref, key_ref)[kind]
        for h in range(heads):
            at = kind * part + h * head
            own = widen(raw[:, at : at + head])
            inverse = lax.rsqrt(jnp.sum(own * own, axis=-1, keepdims=True) * (1.0 / head) + EPS)
            own = own * inverse * gain
            turned = (
                own * cosine
                + pltpu.roll(own, LANES - head // 4, 1) * near
                + pltpu.roll(own, head // 4, 1) * far
            )
            target[:, pl.ds(h * LANES, LANES)] = (turned + side_ref[3 + kind]).astype(BF)
    lane = lax.broadcasted_iota(jnp.int32, (rows, LANES), 1)
    ones = ((lane >= head) & (lane < head + 3)).astype(F32)
    for h in range(heads):
        at = 2 * part + h * head
        value_ref[:, pl.ds(h * LANES, LANES)] = (widen(raw[:, at : at + head]) + ones).astype(BF)


def split_three(value):
    one = value.astype(BF).astype(F32)
    rest = value - one
    two = rest.astype(BF).astype(F32)
    return one, two, rest - two


def forward_kernel(head, pieces, query_ref, *refs):
    keys, values = refs[:pieces], refs[pieces : 2 * pieces]
    outward_ref, partial_ref, mixed_ref, again_ref = refs[2 * pieces :]
    rows = query_ref.shape[0]
    heads = query_ref.shape[1] // LANES
    lane = lax.broadcasted_iota(jnp.int32, (rows, LANES), 1)
    mixed = []
    for h in range(heads):
        place = pl.ds(h * LANES, LANES)
        query = query_ref[:, place]
        out = None
        for key_ref, value_ref in zip(keys, values):
            weights = jnp.exp2(dot(query, key_ref[:, place], NT)).astype(BF)
            term = dot(weights, value_ref[:, place], NN)
            out = term if out is None else out + term
        total = out[:, head : head + 1]
        mixed.append((out[:, :head] * (1.0 / total)).astype(BF))
        one, two, three = split_three(-jnp.log2(total))
        marks = jnp.where(lane == head + 4, one, 0.0)
        marks = jnp.where(lane == head + 5, two, marks)
        marks = jnp.where(lane == head + 6, three, marks)
        again_ref[:, place] = (query.astype(F32) + marks).astype(BF)
    mixed = jnp.concatenate(mixed, axis=1)
    mixed_ref[...] = mixed
    partial_ref[...] = dot(mixed, outward_ref[...], NN).astype(partial_ref.dtype)


def backward_kernel(head, pieces, first, count, *refs):
    sent = stack_rows(refs[:count])
    outward_ref, mixed_ref, query_ref = refs[count : count + 3]
    refs = refs[count + 3 :]
    keys, values = refs[:pieces], refs[pieces : 2 * pieces]
    refs = refs[2 * pieces :]
    if not first:
        key_in, value_in = refs[:pieces], refs[pieces : 2 * pieces]
        refs = refs[2 * pieces :]
    query_out = refs[0]
    key_out, value_out = refs[1 : 1 + pieces], refs[1 + pieces :]
    rows = query_ref.shape[0]
    heads = query_ref.shape[1] // LANES
    lane = lax.broadcasted_iota(jnp.int32, (rows, LANES), 1)
    grads = dot(sent, outward_ref[...], NT).astype(BF).astype(F32)
    mixed = mixed_ref[...].astype(F32)
    for h in range(heads):
        place = pl.ds(h * LANES, LANES)
        cut = slice(h * head, (h + 1) * head)
        grad = grads[:, cut]
        centre = jnp.sum(grad * mixed[:, cut], axis=-1, keepdims=True)
        one, two, three = split_three(-centre)
        grad = widen(grad)
        grad = jnp.where(lane == head, one, grad)
        grad = jnp.where(lane == head + 1, two, grad)
        grad = jnp.where(lane == head + 2, three, grad).astype(BF)
        query = query_ref[:, place]
        query_grad = None
        for j in range(pieces):
            key, value = keys[j][:, place], values[j][:, place]
            weights = jnp.exp2(dot(key, query, NT))
            score_grad = (weights * dot(value, grad, NT)).astype(BF)
            value_grad = dot(weights.astype(BF), grad, NN)
            key_grad = dot(score_grad, query, NN)
            if not first:
                value_grad += value_in[j][:, place]
                key_grad += key_in[j][:, place]
            value_out[j][:, place] = value_grad
            key_out[j][:, place] = key_grad
            term = dot(score_grad, key, TN)
            query_grad = term if query_grad is None else query_grad + term
        query_out[:, place] = query_grad


def leave_kernel(head, count, *refs):
    x = stack_rows(refs[:count])
    query_grad_ref, key_grad_ref, value_grad_ref, raw_ref, side_ref, gain_ref = refs[count : count + 6]
    weight_ref, projected_ref, partial_ref, slots_ref, gains_ref = refs[count + 6 :]
    rows, width = x.shape
    part = weight_ref.shape[0] // 3
    heads = part // head
    cosine, near, far = side_ref[0], side_ref[1], side_ref[2]
    raw = raw_ref[...].astype(F32)
    pieces = []
    gain_grads = []
    for kind in range(2):
        gain = gain_ref[kind : kind + 1, :]
        source = (query_grad_ref, key_grad_ref)[kind]
        scale = (1.0 / math.sqrt(head), math.log(2.0))[kind]
        gain_grad = None
        for h in range(heads):
            grad = source[:, pl.ds(h * LANES, LANES)] * scale
            grad = (
                grad * cosine
                + pltpu.roll(grad * near, head // 4, 1)
                + pltpu.roll(grad * far, LANES - head // 4, 1)
            )
            at = kind * part + h * head
            own = widen(raw[:, at : at + head])
            inverse = lax.rsqrt(jnp.sum(own * own, axis=-1, keepdims=True) * (1.0 / head) + EPS)
            own = own * inverse
            term = jnp.sum(grad * own, axis=0, keepdims=True)
            gain_grad = term if gain_grad is None else gain_grad + term
            grad = grad * gain
            slope = jnp.sum(grad * own, axis=-1, keepdims=True) * (1.0 / head)
            pieces.append((inverse * (grad - own * slope))[:, :head].astype(BF))
        gain_grads.append(gain_grad[:, :head])
    gains_ref[...] = jnp.concatenate(gain_grads, axis=1)
    for h in range(heads):
        pieces.append(value_grad_ref[:, pl.ds(h * LANES, head)].astype(BF))
    projected = jnp.concatenate(pieces, axis=1)
    projected_ref[...] = projected
    grad = dot(projected, weight_ref[...], NN)
    partial_ref[...] = grad.astype(partial_ref.dtype)
    pick = picks(side_ref, width)
    normed, _ = norm(x.astype(F32))
    slots_ref[...] = jnp.concatenate(slot_sums(pick, grad) + slot_sums(pick, grad * normed), axis=0)


def middle_kernel(x_ref, own_ref, one_ref, two_ref, side_ref, table_ref,
                  attended_ref, middle_ref, second_ref):
    attended = total(own_ref, one_ref, two_ref)
    attended_ref[...] = attended.astype(BF)
    pick = picks(side_ref, x_ref.shape[1])
    middle = x_ref[...].astype(F32) + choose(pick, table_ref, 2) * attended
    middle_ref[...] = middle
    normed, _ = norm(middle)
    second_ref[...] = (
        normed * (1.0 + choose(pick, table_ref, 4)) + choose(pick, table_ref, 3)
    ).astype(BF)


def units_kernel(count, *refs):
    second = stack_rows(refs[:count])
    grad_ref, weight_ref, hidden_ref, widening_ref, partial_ref = refs[count:]
    units = grad_ref.shape[1]
    both = dot(second, weight_ref[...], NN)
    gate, up = both[:, :units], both[:, units:]
    sigmoid = 1.0 / (1.0 + jnp.exp(-gate))
    active = gate * sigmoid
    hidden_ref[...] = (active * up).astype(BF)
    grad = grad_ref[...]
    gate_grad = (grad * up * (sigmoid + active * (1.0 - sigmoid))).astype(BF)
    widening = jnp.concatenate([gate_grad, (grad * active).astype(BF)], axis=1)
    widening_ref[...] = widening
    partial_ref[...] = dot(widening, weight_ref[...], NT).astype(partial_ref.dtype)


def hidden_grad_kernel(count, *refs):
    dy = stack_rows(refs[:count])
    side_ref, table_ref, weight_ref, fed_ref, out_ref = refs[count:]
    pick = picks(side_ref, dy.shape[1])
    fed = (choose(pick, table_ref, 5) * dy.astype(F32)).astype(BF)
    fed_ref[...] = fed
    out_ref[...] = dot(fed, weight_ref[...], NN)


def fed_part_kernel(count, *refs):
    dy = stack_rows(refs[:count])
    hidden_ref, side_ref, weight_ref, out_ref, slots_ref = refs[count:]
    fed = dot(hidden_ref[...], weight_ref[...], NT)
    out_ref[...] = fed.astype(BF)
    slots_ref[...] = jnp.concatenate(
        slot_sums(picks(side_ref, dy.shape[1]), dy.astype(F32) * fed), axis=0
    )


def weights_kernel(counts, cuts, core_ref, *refs):
    *refs, room_ref, sems = refs
    pairs = []
    for lefts, rights in counts:
        pairs.append((refs[:lefts], stack_rows(refs[lefts : lefts + rights])))
        refs = refs[lefts + rights :]
    outs = refs
    height = room_ref.shape[0]
    blocks = len(outs) * outs[0].shape[0]
    size = height // blocks
    copies = []
    step = height // cuts
    for low in range(0, height, step):
        at = 0
        for lefts, right in pairs:
            left = [ref[:, low : low + step] for ref in lefts]
            left = left[0] if len(left) == 1 else jnp.concatenate(left, axis=0)
            high = at + right.shape[1]
            room_ref[low : low + step, at:high] = dot(left, right, TN).astype(BF)
            at = high
        while len(copies) < blocks and (len(copies) + 1) * size <= low + step:
            j = len(copies)
            rows = room_ref.at[j * size : (j + 1) * size, :]
            to = [pltpu.make_async_copy(rows, out.at[j // len(outs)], sems.at[j]) for out in outs]
            if len(outs) == 1:
                to[0].start()
            else:

                @pl.when(core_ref[0] == j % 2)
                def _(copy=to[0]):
                    copy.start()

                @pl.when(core_ref[0] != j % 2)
                def _(copy=to[1]):
                    copy.start()

            copies.append(to[0])
    for copy in copies:
        copy.wait()


def weights_call(pairs, dp, name, us, mib):
    args, counts = [], []
    for lefts, rights in pairs:
        args += [*lefts, *rights]
        counts.append((len(lefts), len(rights)))
    height = pairs[0][0][0].shape[1]
    wide = sum(rights[0].shape[1] for _, rights in pairs)
    outs = 2 if dp == 8 else 1
    blocks = dp if outs == 2 else 1
    return pl.pallas_call(
        functools.partial(weights_kernel, counts, 3),
        out_shape=[pltpu.HBM((blocks // outs, height // blocks, wide), BF)] * outs,
        in_specs=[pl.BlockSpec(memory_space=pltpu.SMEM)]
        + [pl.BlockSpec(memory_space=pltpu.VMEM)] * len(args),
        out_specs=[pl.BlockSpec(memory_space=pltpu.HBM)] * outs,
        scratch_shapes=[pltpu.VMEM((height, wide), BF), pltpu.SemaphoreType.DMA((blocks,))],
        compiler_params=pltpu.CompilerParams(vmem_limit_bytes=mib * 1024 * 1024),
        cost_estimate=pl.CostEstimate(flops=int(us * 1.15e9), bytes_accessed=1, transcendentals=0),
        name=name,
    )((lax.axis_index("dp") % 2).reshape(1).astype(jnp.int32), *args)


def swap(value, by):
    return None if value is None else lax.ppermute(value, "dp", [(i, i ^ by) for i in range(8)])


def merge_kernel(place_ref, keep_ref, got_ref, *out_refs):
    for k, ref in enumerate(out_refs):
        at = place_ref[0] ^ k
        ref[...] = keep_ref[at] + got_ref[at]


def sum_start(outs):
    if len(outs) == 1:
        total_sum = lax.psum_scatter(outs[0][0], "dp", scatter_dimension=0, tiled=True)
        return [total_sum, None, None, None]
    return [outs[0], swap(outs[1], 1), None, None]


def sum_merge(parts, name):
    if parts[1] is None:
        return parts
    _, size, wide = parts[0].shape
    place = (lax.axis_index("dp") // 2).reshape(1).astype(jnp.int32)
    outs = kernel_call(
        merge_kernel,
        [like(size, wide, dtype=BF)] * 4,
        place, in_hbm(parts[0]), in_hbm(parts[1]),
        scalars=1, name=name, us=3.0, hbm=(0,),
    )
    return list(outs)


def plus(left, right):
    return None if left is None else left + right


def spread(groups, outs, parts):
    parts = [part for part in parts if part is not None]
    return kernel_call(
        functools.partial(spread_kernel, groups, len(parts)), outs, *parts, name="spread"
    )


def in_hbm(value):
    return pltpu.with_memory_space_constraint(value, pltpu.HBM)


def middle_back_kernel(own_ref, one_ref, two_ref, middle_ref, attended_ref, dy_ref, side_ref, table_ref,
                       grad_ref, send_ref, slots_ref):
    pick = picks(side_ref, dy_ref.shape[1])
    second_grad = total(own_ref, one_ref, two_ref)
    normed, inverse = norm(middle_ref[...])
    grad = dy_ref[...].astype(F32) + norm_back(
        second_grad * (1.0 + choose(pick, table_ref, 4)), normed, inverse
    )
    grad_ref[...] = grad
    send_ref[...] = (choose(pick, table_ref, 2) * grad).astype(BF)
    slots_ref[...] = jnp.concatenate(
        slot_sums(pick, grad * attended_ref[...].astype(F32))
        + slot_sums(pick, second_grad)
        + slot_sums(pick, second_grad * normed),
        axis=0,
    )


def fed_kernel(own_ref, one_ref, two_ref, middle_ref, side_ref, table_ref, out_ref):
    pick = picks(side_ref, middle_ref.shape[1])
    fed = total(own_ref, one_ref, two_ref)
    out_ref[...] = (middle_ref[...] + choose(pick, table_ref, 5) * fed).astype(BF)


def spread_kernel(groups, count, *refs):
    parts, out_refs = refs[:count], refs[count:]
    at = 0
    for group, ref in zip(groups, out_refs):
        width = ref.shape[-1]
        for j in range(group):
            ref[j] = total(*[part.at[:, at : at + width] for part in parts])
            at += width


def token_kernel(own_ref, one_ref, two_ref, x_ref, grad_ref, side_ref, table_ref, out_ref):
    pick = picks(side_ref, x_ref.shape[1])
    first_grad = total(own_ref, one_ref, two_ref)
    normed, inverse = norm(x_ref[...].astype(F32))
    out_ref[...] = grad_ref[...] + norm_back(
        first_grad * (1.0 + choose(pick, table_ref, 1)), normed, inverse
    )


def sync(*values):
    return lax.optimization_barrier(values)


def shards(
    tokens,
    condition,
    modulator,
    offsets,
    inward,
    query_gain,
    key_gain,
    outward,
    expansion,
    contraction,
    item_lengths,
    item_condition,
    patch_rows,
    patch_columns,
    cotangent,
):
    _, rows, width = tokens.shape
    full = patch_rows.shape[1]
    head = query_gain.shape[0]
    part = inward.shape[2]
    heads = part // head
    units = contraction.shape[1]
    items = item_lengths.shape[1]
    dp = lax.axis_size("dp")
    me = lax.axis_index("tp")
    dp_me = lax.axis_index("dp")
    lanes = width // dp
    padded = heads * LANES
    spans = ((0, rows), (rows, 3 * rows), (3 * rows, full))
    sizes = [high - low for low, high in spans]

    x, dy = tokens[0], cotangent[0]
    x_one, x_two = flip(x, 1), flip(x, 2)
    cond_low = jax.nn.silu(condition.astype(F32)).astype(BF)
    share = dot(cond_low, jnp.transpose(modulator, (1, 2, 0)).reshape(-1, width), NT)
    share = share.reshape(12, part)
    inward_rows = jnp.transpose(inward, (1, 2, 0)).reshape(3 * part, width)
    outward_rows = outward.T
    gains = jnp.pad(jnp.stack([query_gain, key_gain]), ((0, 0), (0, LANES - head)))
    order = jnp.arange(4, dtype=jnp.int32) ^ me
    places = jnp.stack([patch_rows[0], patch_columns[0]], axis=1).astype(F32)
    places = jnp.take(places.reshape(4, rows, 2), order, axis=0).reshape(full, 2)
    ends = jnp.cumsum(item_lengths[0])
    share, order, places, ends = sync(share, order, places, ends)
    shares = [share, flip(share, 1), flip(share, 2), flip(share, 3)]
    side = kernel_call(
        functools.partial(setup_kernel, head, items, spans),
        [like(6, n, LANES) for n in sizes],
        ends, item_condition[0], order, places,
        scalars=3, name="setup", us=3.0,
    )
    order, expansion, *both = sync(order, expansion, *shares, *side)
    shares, side = both[:4], both[4:]
    (table,) = kernel_call(
        functools.partial(columns_kernel, 4),
        [like(12, width)],
        order, *shares, offsets,
        scalars=1, name="columns",
    )
    expansion_flat = expansion.reshape(width, 2 * units)
    x_halves = halves(x_one, x_two)
    x_one, x_two, dy, table, expansion_flat, *x_halves = sync(
        x_one, x_two, dy, table, expansion_flat, *x_halves
    )

    x_far = flip(x_halves[0], 2), flip(x_halves[1], 1)
    x_parts = [[x], [x_one, x_two], list(x_far)]

    def enter(k, parts):
        n = sizes[k]
        return kernel_call(
            functools.partial(enter_kernel, head, len(parts)),
            [
                like(n, width, dtype=BF),
                like(n, padded, dtype=BF),
                like(n, padded, dtype=BF),
                like(n, padded, dtype=BF),
                like(n, 2 * part, dtype=BF),
            ],
            *parts, side[k], table, gains, inward_rows,
            name="enter", hbm=(0, 4), us=3.3 * n / rows,
        )

    entered = [None, list(enter(1, x_parts[1]))]
    x_far, dy, entered[1][1], x_own = sync(x_far, dy, entered[1][1], x)
    dy_one, dy_two = flip(dy, 1), flip(dy, 2)
    entered[0] = list(enter(0, [x_own]))
    x_far = list(x_far)
    x_parts[2] = x_far

    entered.append(enter(2, x_far))
    first_in, queries, keys, values, raws = zip(*entered)

    def attend(k, query):
        n = sizes[k]
        return kernel_call(
            functools.partial(forward_kernel, head, 3),
            [like(n, width, dtype=BF), like(n, part, dtype=BF), like(n, padded, dtype=BF)],
            query, *keys, *values, outward_rows,
            name="attend", us=2.0 * n / rows,
        )

    attended = [None, None, attend(2, queries[2])]
    far, query_near, dy_one, dy_two = sync(attended[2][0], queries[1], dy_one, dy_two)

    got = scatter_first(far)
    dy_far = relay(dy_one, dy_two)
    attended[1] = attend(1, query_near)
    near, query_own, *got = sync(attended[1][0], queries[0], *got)

    sums = scatter_second(near, got)
    attended[0] = attend(0, query_own)
    own, cond_low, *both = sync(attended[0][0], cond_low, *sums, *dy_far)
    sums, dy_far = both[:2], both[2:]

    attended_own, middle, second = kernel_call(
        middle_kernel,
        [like(rows, width, dtype=BF), like(rows, width), like(rows, width, dtype=BF)],
        x, own, *sums, side[0], table,
        name="middle",
    )
    second, cond_low = sync(second, cond_low)
    second_one, second_two = flip(second, 1), flip(second, 2)
    dy_parts = [[dy], [dy_one, dy_two], dy_far]
    fed_grad, hidden_grad = [], []
    for k in range(3):
        outs = kernel_call(
            functools.partial(hidden_grad_kernel, len(dy_parts[k])),
            [like(sizes[k], width, dtype=BF), like(sizes[k], units)],
            *dy_parts[k], side[k], table, contraction,
            name="hidden_grad", us=0.8 * sizes[k] / rows,
        )
        fed_grad.append(outs[0])
        hidden_grad.append(outs[1])
    conds = jnp.transpose(gather_small(cond_low, dp), (1, 0, 2)).reshape(2 * dp, width)
    conds = lax.dynamic_slice_in_dim(conds, dp_me * lanes, lanes, 1).astype(F32)
    second_one, second_two, conds, *hidden_grad = sync(second_one, second_two, conds, *hidden_grad)

    second_far = relay(second_one, second_two)
    second_parts = [[second], [second_one, second_two], list(second_far)]

    def through(k, parts):
        n = sizes[k]
        return kernel_call(
            functools.partial(units_kernel, len(parts)),
            [
                like(n, units, dtype=BF),
                like(n, 2 * units, dtype=BF),
                like(n, width, dtype=BF),
            ],
            *parts, hidden_grad[k], expansion_flat,
            name="units", us=2.5 * n / rows,
        )

    passed = [through(0, second_parts[0]), through(1, second_parts[1])]
    *second_far, near, own = sync(*second_far, passed[1][2], passed[0][2])
    second_parts[2] = second_far
    passed.append(through(2, second_far))
    hidden, widening, back = zip(*passed)
    far, hidden_far = sync(back[2], hidden[2])

    got = scatter_first(far)
    wide = weights_call(
        [
            (sum(second_parts, []), widening),
            (fed_grad, [*hidden[:2], hidden_far]),
        ],
        dp,
        "wide",
        6.0,
        18,
    )
    wide, near, hidden_far, got = sync(wide, near, hidden_far, got)

    sums = scatter_second(near, got)
    wide = sum_start(wide)
    fed_parts, fed_slots = [None] * 3, [None] * 3
    for k, source in ((1, hidden[1]), (2, hidden_far), (0, hidden[0])):
        if k == 2:
            fed_parts[1], wide, source = sync(fed_parts[1], wide, source)
            wide = sum_merge(wide, "merge")
        if k == 0:
            fed_parts[2], wide, source = sync(fed_parts[2], wide, source)
            wide[3] = swap(wide[3], 2)
        fed_parts[k], fed_slots[k] = kernel_call(
            functools.partial(fed_part_kernel, len(dy_parts[k])),
            [like(sizes[k], width, dtype=BF), like(2, width)],
            *dy_parts[k], source, side[k], contraction,
            name="fed_part", hbm=(0, 1), us=1.0 * sizes[k] / rows,
        )
    own, sums, fed_parts[0] = sync(own, sums, fed_parts[0])

    middle_grad, send, slots_two = kernel_call(
        middle_back_kernel,
        [like(rows, width), like(rows, width, dtype=BF), like(6, width)],
        own, *sums, middle, attended_own, dy, side[0], table,
        name="middle_back", hbm=(0, 2), us=1.7,
    )
    send_one, send_two = flip(send, 1), flip(send, 2)

    def attend_back(k, parts, sums):
        n = sizes[k]
        given = (*parts, outward_rows, attended[k][1], attended[k][2], *keys, *values)
        out = kernel_call(
            functools.partial(backward_kernel, head, 3, not sums, len(parts)),
            [like(n, padded)] + [like(a.shape[0], padded) for a in keys + values],
            *given, *sums,
            aliases={len(given) + i: 1 + i for i in range(len(sums))},
            name="attend_back", us=4.3 * n / rows, mib=16,
        )
        return out[0], tuple(out[1:])

    query_grads = [None] * 3
    query_grads[0], totals = attend_back(0, [send], ())
    send_one, send_two, totals, wide[3] = sync(send_one, send_two, totals, wide[3])

    send_far = relay(send_one, send_two)
    wide[2] = swap(plus(wide[2], wide[3]), 4)
    query_grads[1], totals = attend_back(1, [send_one, send_two], totals)
    send_far, totals, fed_far = sync(send_far, totals, fed_parts[2])

    fed_got = scatter_first(fed_far)
    send_parts = [[send], [send_one, send_two], list(send_far)]
    query_grads[2], totals = attend_back(2, send_far, totals)
    key_grads, value_grads = totals[:3], totals[3:]

    def leave(k, query_grad):
        n = sizes[k]
        return kernel_call(
            functools.partial(leave_kernel, head, len(x_parts[k])),
            [
                like(n, 3 * part, dtype=BF),
                like(n, width, dtype=BF),
                like(4, width),
                like(1, 2 * head),
            ],
            *x_parts[k], query_grad, key_grads[k], value_grads[k], raws[k], side[k], gains,
            inward_rows,
            name="leave", hbm=(0, 2, 3), us=3.8 * n / rows,
        )

    left = [None, None, leave(2, query_grads[2])]
    far, query_near, fed_got, wide[1] = sync(left[2][1], query_grads[1], fed_got, wide[1])

    got = scatter_first(far)
    wide[1] = swap(wide[1], 2)
    left[1] = leave(1, query_near)
    near, query_own, got = sync(left[1][1], query_grads[0], got)

    sums = scatter_second(near, got)
    left[0], wide[1], wide[2] = sync(leave(0, query_own), wide[1], wide[2])

    packed = kernel_call(
        pack_kernel,
        [like(13, part)] * 4,
        order, left[0][2], left[1][2], left[2][2], slots_two, *fed_slots,
        left[0][3], left[1][3], left[2][3],
        scalars=1, name="pack",
    )
    packed = [packed[0]] + [flip(packed[k], k) for k in (1, 2, 3)]
    narrow = weights_call(
        [
            (first_in, [left[k][0] for k in range(3)]),
            (sum(send_parts, []), [attended[k][1] for k in range(3)]),
        ],
        dp,
        "narrow",
        5.0,
        16,
    )
    packed, narrow = sync(packed, narrow)

    narrow = sum_start(narrow)
    every = gather_core(packed[0] + packed[1] + packed[2] + packed[3], dp)
    narrow, every = sync(narrow, every)

    narrow = sum_merge(narrow, "merge")
    every = gather_chips(every, dp)
    narrow, every = sync(narrow, every)
    narrow[3] = swap(narrow[3], 2)
    (token_gradient,) = kernel_call(
        token_kernel,
        [like(rows, width)],
        left[0][1], *sums, x, middle_grad, side[0], table,
        name="token", us=2.0,
    )
    fed_near, narrow[1], narrow[2], narrow[3], every, token_gradient = sync(
        fed_parts[1], narrow[1], narrow[2], narrow[3], every, token_gradient
    )
    narrow[1] = swap(narrow[1], 2)
    narrow[2] = swap(plus(narrow[2], narrow[3]), 4)
    fed_sums = scatter_second(fed_near, fed_got)
    expansion_gradient, contraction_gradient = spread(
        [2, 1], [like(2, lanes, units), like(1, lanes, units)], wide[:3]
    )
    modulator_gradient, bias_part, gain_sum = kernel_call(
        functools.partial(slots_kernel, [(2 * j, 2 * j + 1) for j in range(6)]),
        [like(6, lanes, part), like(6, part), like(1, part)],
        conds, every,
        name="slots", us=2.0,
    )
    (bias_gradient,) = kernel_call(
        functools.partial(columns_kernel, 4),
        [like(6, width)],
        order, bias_part, flip(bias_part, 1), flip(bias_part, 2), flip(bias_part, 3),
        jnp.zeros((6, width), F32),
        scalars=1, name="columns",
    )
    (layer_output,) = kernel_call(
        fed_kernel,
        [like(rows, width, dtype=BF)],
        fed_parts[0], *fed_sums, middle, side[0], table,
        name="fed", us=1.5,
    )
    inward_gradient, outward_gradient = spread(
        [3, 1], [like(3, lanes, part), like(1, lanes, part)], narrow[:3]
    )
    return (
        layer_output[None],
        token_gradient[None],
        jnp.transpose(modulator_gradient, (1, 0, 2)),
        bias_gradient,
        jnp.transpose(inward_gradient, (1, 0, 2)),
        gain_sum[0, :head],
        gain_sum[0, head : 2 * head],
        outward_gradient[0],
        jnp.transpose(expansion_gradient, (1, 0, 2)),
        contraction_gradient[0],
    )


def solution(mesh):
    placed = (
        P("dp", "tp", None),
        P("dp", None),
        P(None, None, "tp"),
        P(),
        P(None, None, "tp"),
        P(),
        P(),
        P(None, "tp"),
        P(None, None, "tp"),
        P(None, "tp"),
        P("dp", None),
        P("dp", None),
        P("dp", None),
        P("dp", None),
        P("dp", "tp", None),
    )
    return jax.shard_map(
        shards,
        mesh=mesh,
        in_specs=placed,
        out_specs=(
            P("dp", "tp", None),
            P("dp", "tp", None),
            P("dp", None, "tp"),
            P(),
            P("dp", None, "tp"),
            P(),
            P(),
            P("dp", "tp"),
            P("dp", None, "tp"),
            P("dp", "tp"),
        ),
        check_vma=False,
    )
```

```python
import functools
import math

import jax
import jax.numpy as jnp
from jax import lax
from jax.experimental import pallas as pl
from jax.experimental.pallas import tpu as pltpu
from jax.sharding import PartitionSpec as P

BF = jnp.bfloat16
F32 = jnp.float32
LANES = 128
EPS = 1e-06
NN = ((1,), (0,))
NT = ((1,), (1,))
TN = ((0,), (0,))
MASKED = -30000.0


def dot(left, right, dims):
    return lax.dot_general(left, right, (dims, ((), ())), preferred_element_type=F32)


def flip(value, by):
    return lax.ppermute(value, "tp", [(i, i ^ by) for i in range(4)])


def halves(one, two):
    half = one.shape[0] // 2
    return one[:half], two[half:]


def relay(one, two):
    low, high = halves(one, two)
    return flip(low, 2), flip(high, 1)


def scatter_first(far):
    half = far.shape[0] // 2
    return flip(far[:half], 1), flip(far[half:], 2)


def total(*refs):
    return sum(ref[...].astype(F32) for ref in refs)


def join_kernel(near_ref, via_one_ref, via_two_ref, one_ref, two_ref):
    rows = one_ref.shape[0]
    half = rows // 2
    one_ref[:half, :] = near_ref[:half, :]
    one_ref[half:, :] = near_ref[half:rows, :] + via_two_ref[...]
    two_ref[:half, :] = near_ref[rows : rows + half, :] + via_one_ref[...]
    two_ref[half:, :] = near_ref[rows + half :, :]


def scatter_second(near, got):
    out = like(near.shape[0] // 2, near.shape[1], dtype=near.dtype)
    one, two = kernel_call(join_kernel, [out, out], near, *got, name="join")
    return flip(one, 1), flip(two, 2)


def gather_core(own, dp):
    return jnp.stack([own, swap(own, 1)]) if dp == 8 else own


def gather_chips(pair, dp):
    if dp != 8:
        return lax.all_gather(pair, "dp", axis=0)
    four = jnp.concatenate([pair, swap(pair, 2)], axis=0)
    return jnp.concatenate([four, swap(four, 4)], axis=0)


def gather_small(own, dp):
    return gather_chips(gather_core(own, dp), dp)


def pack_kernel(order_ref, *refs):
    first, two_ref, fed, gains, out_refs = refs[:3], refs[3], refs[4:7], refs[7:10], refs[10:]
    cut = out_refs[0].shape[-1]
    tall = jnp.concatenate([total(*first), two_ref[...], total(*fed)], axis=0)
    gain = total(*gains)
    gain = jnp.concatenate([gain, jnp.zeros((1, cut - gain.shape[1]), F32)], axis=1)
    parts = [tall[:, j * cut : (j + 1) * cut] for j in range(4)]
    bias = []
    for part in parts:
        bias += [part[2 * j : 2 * j + 1] + part[2 * j + 1 : 2 * j + 2] for j in range(6)]
    below = jnp.concatenate([gain, *bias], axis=0)
    for k in range(4):
        part = parts[0]
        for j in range(1, 4):
            part = jnp.where(order_ref[k] == j, parts[j], part)
        out_refs[k % 2][k // 2] = jnp.concatenate([part, below], axis=0)


def slots_kernel(conds_ref, every_ref, grad_ref, bias_ref, gain_ref):
    conds = conds_ref[...]
    cut = every_ref.shape[2]
    gain_ref[...] = jnp.sum(every_ref[:, 12, :], axis=0, keepdims=True)
    for j in range(6):
        both = [every_ref[:, 2 * j + c, :] for c in range(2)]
        grad_ref[j] = lax.dot_general(
            conds,
            jnp.concatenate(both, axis=0),
            (TN, ((), ())),
            precision=lax.Precision.HIGHEST,
            preferred_element_type=F32,
        )
        for q in range(4):
            own = every_ref[:, 13 + 6 * q + j, :]
            bias_ref[j : j + 1, q * cut : (q + 1) * cut] = jnp.sum(own, axis=0, keepdims=True)


def columns_kernel(pieces, order_ref, *refs):
    add_ref, out_ref = refs[pieces:]
    stacked = jnp.stack([ref[...] for ref in refs[:pieces]])
    parts = []
    for j in range(pieces):
        part = stacked[0]
        for k in range(1, pieces):
            part = jnp.where(order_ref[j] == k, stacked[k], part)
        parts.append(part)
    out = jnp.concatenate(parts, axis=1)
    add = add_ref[...]
    if add.shape[0] < out.shape[0]:
        add = jnp.concatenate([add, add], axis=0)
    out_ref[...] = out + add


def gather_tp_columns(own, add):
    order = jnp.arange(4, dtype=jnp.int32) ^ lax.axis_index("tp")
    (out,) = kernel_call(
        functools.partial(columns_kernel, 4),
        [like(own.shape[0], 4 * own.shape[1])],
        order, own, flip(own, 1), flip(own, 2), flip(own, 3), add,
        scalars=1,
        name="columns",
    )
    return out


def kernel_call(body, outs, *args, aliases=None, name=None, scalars=0, us=1.0, mib=16, hbm=()):
    spec = pl.BlockSpec(memory_space=pltpu.VMEM)
    given = [pl.BlockSpec(memory_space=pltpu.SMEM)] * scalars + [spec] * (len(args) - scalars)
    return pl.pallas_call(
        body,
        out_shape=[pltpu.HBM(o.shape, o.dtype) if i in hbm else o for i, o in enumerate(outs)],
        in_specs=given,
        out_specs=[spec] * len(outs),
        input_output_aliases=aliases or {},
        compiler_params=pltpu.CompilerParams(vmem_limit_bytes=mib * 1024 * 1024),
        cost_estimate=pl.CostEstimate(flops=int(us * 1.15e9), bytes_accessed=1, transcendentals=0),
        name=name,
    )(*args)


def like(*shape, dtype=F32):
    return jax.ShapeDtypeStruct(shape, dtype)


def norm(values):
    count = values.shape[-1]
    center = values - jnp.sum(values, axis=-1, keepdims=True) * (1.0 / count)
    inverse = lax.rsqrt(jnp.sum(center * center, axis=-1, keepdims=True) * (1.0 / count) + EPS)
    return center * inverse, inverse


def norm_back(grad, normed, inverse):
    count = grad.shape[-1]
    middle = jnp.sum(grad, axis=-1, keepdims=True) * (1.0 / count)
    slope = jnp.sum(grad * normed, axis=-1, keepdims=True) * (1.0 / count)
    return inverse * (grad - middle - normed * slope)


def choose(pick, table_ref, column):
    return jnp.where(pick, table_ref[6 + column : 7 + column, :], table_ref[column : column + 1, :])


def slot_sums(pick, values):
    zero = jnp.zeros_like(values)
    return [
        jnp.sum(jnp.where(pick, zero, values), axis=0, keepdims=True),
        jnp.sum(jnp.where(pick, values, zero), axis=0, keepdims=True),
    ]


def picks(pick_ref, width):
    return jnp.broadcast_to(pick_ref[:, 0:1], (pick_ref.shape[0], width)) > 0.5


def widen(values):
    return jnp.concatenate(
        [values, jnp.zeros((values.shape[0], LANES - values.shape[1]), values.dtype)], axis=1
    )


def stack_rows(refs):
    return refs[0][...] if len(refs) == 1 else jnp.concatenate([ref[...] for ref in refs], axis=0)


def setup_kernel(head, items, spans, ends_ref, conds_ref, order_ref, places_ref, *out_refs):
    rows = places_ref.shape[0] // 4
    quarter = head // 4
    for s, (low, high) in enumerate(spans):
        count = high - low
        shape = (count, LANES)
        lane = lax.broadcasted_iota(jnp.int32, shape, 1)
        row = lax.broadcasted_iota(jnp.int32, shape, 0)
        start = jnp.full(shape, order_ref[low // rows] * rows, jnp.int32)
        if count > rows:
            start = jnp.where(row >= rows, order_ref[low // rows + 1] * rows - rows, start)
        token = start + row
        owner = jnp.zeros(shape, jnp.int32)
        for j in range(items):
            owner = owner + (token >= ends_ref[j]).astype(jnp.int32)
        pick = jnp.zeros(shape, jnp.int32)
        for j in range(items):
            pick = jnp.where(owner == j, conds_ref[j], pick)
        place = jnp.where(
            lane < 2 * quarter,
            jnp.broadcast_to(places_ref[low:high, 0:1], shape),
            jnp.broadcast_to(places_ref[low:high, 1:2], shape),
        )
        phase = lane
        for j in range(1, 4):
            phase = jnp.where(lane >= j * quarter, lane - j * quarter, phase)
        angles = place * jnp.exp(phase.astype(F32) * (-math.log(10000.0) / quarter))
        real = lane < head
        sine = jnp.sin(angles)
        lower = (lane < quarter) | ((lane >= 2 * quarter) & (lane < 3 * quarter))
        zero = jnp.zeros(shape, F32)
        out_ref, pick_ref = out_refs[2 * s : 2 * s + 2]
        out_ref[0] = jnp.where(real, jnp.cos(angles), zero)
        out_ref[1] = jnp.where(real & lower, -sine, zero)
        out_ref[2] = jnp.where(real & ~lower, sine, zero)
        base = head + 8
        mine = jnp.where(lane == owner + base, 1.0, 0.0)
        out_ref[3] = mine
        marks = jnp.where((lane >= head + 4) & (lane < head + 7), 1.0, zero)
        slots = (lane >= base) & (lane < base + items)
        out_ref[4] = jnp.where(slots, MASKED * (1.0 - mine), marks)
        pick_ref[...] = pick.astype(F32)


def enter_kernel(head, count, *refs):
    x = stack_rows(refs[:count])
    side_ref, pick_ref, table_ref, gain_ref, weight_ref = refs[count : count + 5]
    first_ref, query_ref, key_ref, value_ref, raw_ref = refs[count + 5 :]
    rows, width = x.shape
    part = weight_ref.shape[0] // 3
    heads = part // head
    pick = picks(pick_ref, width)
    normed, _ = norm(x.astype(F32))
    low = (normed * (1.0 + choose(pick, table_ref, 1)) + choose(pick, table_ref, 0)).astype(BF)
    first_ref[...] = low
    raw = dot(low, weight_ref[...], NT)
    raw_ref[...] = raw[:, : 2 * part].astype(BF)
    cosine, near, far = side_ref[0], side_ref[1], side_ref[2]
    scale = math.log2(math.e) / math.sqrt(head)
    for kind in range(2):
        gain = gain_ref[kind : kind + 1, :]
        if kind == 0:
            gain = gain * scale
        target = (query_ref, key_ref)[kind]
        for h in range(heads):
            at = kind * part + h * head
            own = widen(raw[:, at : at + head])
            inverse = lax.rsqrt(jnp.sum(own * own, axis=-1, keepdims=True) * (1.0 / head) + EPS)
            own = own * inverse * gain
            turned = (
                own * cosine
                + pltpu.roll(own, LANES - head // 4, 1) * near
                + pltpu.roll(own, head // 4, 1) * far
            )
            target[:, pl.ds(h * LANES, LANES)] = (turned + side_ref[3 + kind]).astype(BF)
    lane = lax.broadcasted_iota(jnp.int32, (rows, LANES), 1)
    ones = ((lane >= head) & (lane < head + 3)).astype(F32)
    for h in range(heads):
        at = 2 * part + h * head
        value_ref[:, pl.ds(h * LANES, LANES)] = (widen(raw[:, at : at + head]) + ones).astype(BF)


def split_three(value):
    one = value.astype(BF).astype(F32)
    rest = value - one
    two = rest.astype(BF).astype(F32)
    return one, two, rest - two


def forward_kernel(head, pieces, query_ref, *refs):
    keys, values = refs[:pieces], refs[pieces : 2 * pieces]
    outward_ref, partial_ref, mixed_ref, again_ref = refs[2 * pieces :]
    rows = query_ref.shape[0]
    heads = query_ref.shape[1] // LANES
    lane = lax.broadcasted_iota(jnp.int32, (rows, LANES), 1)
    mixed = []
    for h in range(heads):
        place = pl.ds(h * LANES, LANES)
        query = query_ref[:, place]
        out = None
        for key_ref, value_ref in zip(keys, values):
            weights = jnp.exp2(dot(query, key_ref[:, place], NT)).astype(BF)
            term = dot(weights, value_ref[:, place], NN)
            out = term if out is None else out + term
        total = out[:, head : head + 1]
        mixed.append((out[:, :head] * (1.0 / total)).astype(BF))
        one, two, three = split_three(-jnp.log2(total))
        marks = jnp.where(lane == head + 4, one, 0.0)
        marks = jnp.where(lane == head + 5, two, marks)
        marks = jnp.where(lane == head + 6, three, marks)
        again_ref[:, place] = (query.astype(F32) + marks).astype(BF)
    mixed = jnp.concatenate(mixed, axis=1)
    mixed_ref[...] = mixed
    partial_ref[...] = dot(mixed, outward_ref[...], NN).astype(partial_ref.dtype)


def backward_kernel(head, pieces, first, count, *refs):
    sent = stack_rows(refs[:count])
    outward_ref, mixed_ref, query_ref = refs[count : count + 3]
    refs = refs[count + 3 :]
    keys, values = refs[:pieces], refs[pieces : 2 * pieces]
    refs = refs[2 * pieces :]
    if not first:
        key_in, value_in = refs[:pieces], refs[pieces : 2 * pieces]
        refs = refs[2 * pieces :]
    query_out = refs[0]
    key_out, value_out = refs[1 : 1 + pieces], refs[1 + pieces :]
    rows = query_ref.shape[0]
    heads = query_ref.shape[1] // LANES
    lane = lax.broadcasted_iota(jnp.int32, (rows, LANES), 1)
    grads = dot(sent, outward_ref[...], NT).astype(BF).astype(F32)
    mixed = mixed_ref[...].astype(F32)
    for h in range(heads):
        place = pl.ds(h * LANES, LANES)
        cut = slice(h * head, (h + 1) * head)
        grad = grads[:, cut]
        centre = jnp.sum(grad * mixed[:, cut], axis=-1, keepdims=True)
        one, two, three = split_three(-centre)
        grad = widen(grad)
        grad = jnp.where(lane == head, one, grad)
        grad = jnp.where(lane == head + 1, two, grad)
        grad = jnp.where(lane == head + 2, three, grad).astype(BF)
        query = query_ref[:, place]
        query_grad = None
        for j in range(pieces):
            key, value = keys[j][:, place], values[j][:, place]
            weights = jnp.exp2(dot(key, query, NT))
            score_grad = (weights * dot(value, grad, NT)).astype(BF)
            value_grad = dot(weights.astype(BF), grad, NN)
            key_grad = dot(score_grad, query, NN)
            if not first:
                value_grad += value_in[j][:, place]
                key_grad += key_in[j][:, place]
            value_out[j][:, place] = value_grad
            key_out[j][:, place] = key_grad
            term = dot(score_grad, key, TN)
            query_grad = term if query_grad is None else query_grad + term
        query_out[:, place] = query_grad


def leave_kernel(head, count, *refs):
    x = stack_rows(refs[:count])
    query_grad_ref, key_grad_ref, value_grad_ref, raw_ref, side_ref, pick_ref = refs[count : count + 6]
    gain_ref, weight_ref, projected_ref, partial_ref, slots_ref, gains_ref = refs[count + 6 :]
    rows, width = x.shape
    part = weight_ref.shape[0] // 3
    heads = part // head
    cosine, near, far = side_ref[0], side_ref[1], side_ref[2]
    raw = raw_ref[...].astype(F32)
    pieces = []
    gain_grads = []
    for kind in range(2):
        gain = gain_ref[kind : kind + 1, :]
        source = (query_grad_ref, key_grad_ref)[kind]
        scale = (1.0 / math.sqrt(head), math.log(2.0))[kind]
        gain_grad = None
        for h in range(heads):
            grad = source[:, pl.ds(h * LANES, LANES)] * scale
            grad = (
                grad * cosine
                + pltpu.roll(grad * near, head // 4, 1)
                + pltpu.roll(grad * far, LANES - head // 4, 1)
            )
            at = kind * part + h * head
            own = widen(raw[:, at : at + head])
            inverse = lax.rsqrt(jnp.sum(own * own, axis=-1, keepdims=True) * (1.0 / head) + EPS)
            own = own * inverse
            term = jnp.sum(grad * own, axis=0, keepdims=True)
            gain_grad = term if gain_grad is None else gain_grad + term
            grad = grad * gain
            slope = jnp.sum(grad * own, axis=-1, keepdims=True) * (1.0 / head)
            pieces.append((inverse * (grad - own * slope))[:, :head].astype(BF))
        gain_grads.append(gain_grad[:, :head])
    gains_ref[...] = jnp.concatenate(gain_grads, axis=1)
    for h in range(heads):
        pieces.append(value_grad_ref[:, pl.ds(h * LANES, head)].astype(BF))
    projected = jnp.concatenate(pieces, axis=1)
    projected_ref[...] = projected
    grad = dot(projected, weight_ref[...], NN)
    partial_ref[...] = grad.astype(partial_ref.dtype)
    pick = picks(pick_ref, width)
    normed, _ = norm(x.astype(F32))
    slots_ref[...] = jnp.concatenate(slot_sums(pick, grad) + slot_sums(pick, grad * normed), axis=0)


def middle_kernel(x_ref, own_ref, one_ref, two_ref, side_ref, table_ref,
                  attended_ref, middle_ref, second_ref):
    attended = total(own_ref, one_ref, two_ref)
    attended_ref[...] = attended.astype(BF)
    pick = picks(side_ref, x_ref.shape[1])
    middle = x_ref[...].astype(F32) + choose(pick, table_ref, 2) * attended
    middle_ref[...] = middle
    normed, _ = norm(middle)
    second_ref[...] = (
        normed * (1.0 + choose(pick, table_ref, 4)) + choose(pick, table_ref, 3)
    ).astype(BF)


def units_kernel(count, *refs):
    second = stack_rows(refs[:count])
    grad_ref, weight_ref, hidden_ref, widening_ref, partial_ref = refs[count:]
    units = grad_ref.shape[1]
    both = dot(second, weight_ref[...], NN)
    gate, up = both[:, :units], both[:, units:]
    sigmoid = 1.0 / (1.0 + jnp.exp(-gate))
    active = gate * sigmoid
    hidden_ref[...] = (active * up).astype(BF)
    grad = grad_ref[...]
    gate_grad = (grad * up * (sigmoid + active * (1.0 - sigmoid))).astype(BF)
    widening = jnp.concatenate([gate_grad, (grad * active).astype(BF)], axis=1)
    widening_ref[...] = widening
    partial_ref[...] = dot(widening, weight_ref[...], NT).astype(partial_ref.dtype)


def hidden_grad_kernel(count, *refs):
    dy = stack_rows(refs[:count])
    side_ref, table_ref, weight_ref, fed_ref, out_ref = refs[count:]
    pick = picks(side_ref, dy.shape[1])
    fed = (choose(pick, table_ref, 5) * dy.astype(F32)).astype(BF)
    fed_ref[...] = fed
    out_ref[...] = dot(fed, weight_ref[...], NN)


def fed_part_kernel(count, *refs):
    dy = stack_rows(refs[:count])
    hidden_ref, side_ref, weight_ref, out_ref, slots_ref = refs[count:]
    fed = dot(hidden_ref[...], weight_ref[...], NT)
    out_ref[...] = fed.astype(BF)
    slots_ref[...] = jnp.concatenate(
        slot_sums(picks(side_ref, dy.shape[1]), dy.astype(F32) * fed), axis=0
    )


def weights_kernel(counts, cuts, core_ref, *refs):
    *refs, room_ref, sems = refs
    pairs = []
    for lefts, rights in counts:
        pairs.append((refs[:lefts], stack_rows(refs[lefts : lefts + rights])))
        refs = refs[lefts + rights :]
    outs = refs
    height = room_ref.shape[0]
    blocks = len(outs) * outs[0].shape[0]
    size = height // blocks
    copies = []
    step = height // cuts
    for low in range(0, height, step):
        at = 0
        for lefts, right in pairs:
            left = [ref[:, low : low + step] for ref in lefts]
            left = left[0] if len(left) == 1 else jnp.concatenate(left, axis=0)
            high = at + right.shape[1]
            room_ref[low : low + step, at:high] = dot(left, right, TN).astype(BF)
            at = high
        while len(copies) < blocks and (len(copies) + 1) * size <= low + step:
            j = len(copies)
            rows = room_ref.at[j * size : (j + 1) * size, :]
            to = [pltpu.make_async_copy(rows, out.at[j // len(outs)], sems.at[j]) for out in outs]
            if len(outs) == 1:
                to[0].start()
            else:

                @pl.when(core_ref[0] == j % 2)
                def _(copy=to[0]):
                    copy.start()

                @pl.when(core_ref[0] != j % 2)
                def _(copy=to[1]):
                    copy.start()

            copies.append(to[0])
    for copy in copies:
        copy.wait()


def weights_call(pairs, dp, name, us, mib):
    args, counts = [], []
    for lefts, rights in pairs:
        args += [*lefts, *rights]
        counts.append((len(lefts), len(rights)))
    height = pairs[0][0][0].shape[1]
    wide = sum(rights[0].shape[1] for _, rights in pairs)
    outs = 2 if dp == 8 else 1
    blocks = dp if outs == 2 else 1
    return pl.pallas_call(
        functools.partial(weights_kernel, counts, 3),
        out_shape=[pltpu.HBM((blocks // outs, height // blocks, wide), BF)] * outs,
        in_specs=[pl.BlockSpec(memory_space=pltpu.SMEM)]
        + [pl.BlockSpec(memory_space=pltpu.VMEM)] * len(args),
        out_specs=[pl.BlockSpec(memory_space=pltpu.HBM)] * outs,
        scratch_shapes=[pltpu.VMEM((height, wide), BF), pltpu.SemaphoreType.DMA((blocks,))],
        compiler_params=pltpu.CompilerParams(vmem_limit_bytes=mib * 1024 * 1024),
        cost_estimate=pl.CostEstimate(flops=int(us * 1.15e9), bytes_accessed=1, transcendentals=0),
        name=name,
    )((lax.axis_index("dp") % 2).reshape(1).astype(jnp.int32), *args)


def swap(value, by):
    return None if value is None else lax.ppermute(value, "dp", [(i, i ^ by) for i in range(8)])


def merge_kernel(place_ref, keep_ref, got_ref, *out_refs):
    for k, ref in enumerate(out_refs):
        at = place_ref[0] ^ k
        ref[...] = keep_ref[at] + got_ref[at]


def sum_start(outs):
    if len(outs) == 1:
        total_sum = lax.psum_scatter(outs[0][0], "dp", scatter_dimension=0, tiled=True)
        return [total_sum, None, None, None]
    return [outs[0], swap(outs[1], 1), None, None]


def sum_merge(parts, name):
    if parts[1] is None:
        return parts
    _, size, wide = parts[0].shape
    place = (lax.axis_index("dp") // 2).reshape(1).astype(jnp.int32)
    outs = kernel_call(
        merge_kernel,
        [like(size, wide, dtype=BF)] * 4,
        place, in_hbm(parts[0]), parts[1],
        scalars=1, name=name, us=3.0, hbm=(0,),
    )
    return list(outs)


def plus(left, right):
    return None if left is None else left + right


def spread(groups, outs, parts):
    parts = [part for part in parts if part is not None]
    return kernel_call(
        functools.partial(spread_kernel, groups, len(parts)), outs, *parts, name="spread"
    )


def in_hbm(value):
    return pltpu.with_memory_space_constraint(value, pltpu.HBM)


def middle_back_kernel(own_ref, one_ref, two_ref, middle_ref, attended_ref, dy_ref, side_ref, table_ref,
                       grad_ref, send_ref, slots_ref):
    pick = picks(side_ref, dy_ref.shape[1])
    second_grad = total(own_ref, one_ref, two_ref)
    normed, inverse = norm(middle_ref[...])
    grad = dy_ref[...].astype(F32) + norm_back(
        second_grad * (1.0 + choose(pick, table_ref, 4)), normed, inverse
    )
    grad_ref[...] = grad
    send_ref[...] = (choose(pick, table_ref, 2) * grad).astype(BF)
    slots_ref[...] = jnp.concatenate(
        slot_sums(pick, grad * attended_ref[...].astype(F32))
        + slot_sums(pick, second_grad)
        + slot_sums(pick, second_grad * normed),
        axis=0,
    )


def fed_kernel(own_ref, one_ref, two_ref, middle_ref, side_ref, table_ref, out_ref):
    pick = picks(side_ref, middle_ref.shape[1])
    fed = total(own_ref, one_ref, two_ref)
    out_ref[...] = (middle_ref[...] + choose(pick, table_ref, 5) * fed).astype(BF)


def spread_kernel(groups, count, *refs):
    parts, out_refs = refs[:count], refs[count:]
    at = 0
    for group, ref in zip(groups, out_refs):
        width = ref.shape[-1]
        for j in range(group):
            ref[j] = total(*[part.at[:, at : at + width] for part in parts])
            at += width


def token_kernel(own_ref, one_ref, two_ref, x_ref, grad_ref, side_ref, table_ref, out_ref):
    pick = picks(side_ref, x_ref.shape[1])
    first_grad = total(own_ref, one_ref, two_ref)
    normed, inverse = norm(x_ref[...].astype(F32))
    out_ref[...] = grad_ref[...] + norm_back(
        first_grad * (1.0 + choose(pick, table_ref, 1)), normed, inverse
    )


def sync(*values):
    return lax.optimization_barrier(values)


def shards(
    tokens,
    condition,
    modulator,
    offsets,
    inward,
    query_gain,
    key_gain,
    outward,
    expansion,
    contraction,
    item_lengths,
    item_condition,
    patch_rows,
    patch_columns,
    cotangent,
):
    _, rows, width = tokens.shape
    full = patch_rows.shape[1]
    head = query_gain.shape[0]
    part = inward.shape[2]
    heads = part // head
    units = contraction.shape[1]
    items = item_lengths.shape[1]
    dp = lax.axis_size("dp")
    me = lax.axis_index("tp")
    dp_me = lax.axis_index("dp")
    lanes = width // dp
    padded = heads * LANES
    spans = ((0, rows), (rows, 3 * rows), (3 * rows, full))
    sizes = [high - low for low, high in spans]

    x, dy = tokens[0], cotangent[0]
    x_one, x_two = flip(x, 1), flip(x, 2)
    cond_low = jax.nn.silu(condition.astype(F32)).astype(BF)
    share = dot(cond_low, jnp.transpose(modulator, (1, 2, 0)).reshape(-1, width), NT)
    share = share.reshape(12, part)
    inward_rows = jnp.transpose(inward, (1, 2, 0)).reshape(3 * part, width)
    outward_rows = outward.T
    gains = jnp.pad(jnp.stack([query_gain, key_gain]), ((0, 0), (0, LANES - head)))
    order = jnp.arange(4, dtype=jnp.int32) ^ me
    places = jnp.stack([patch_rows[0], patch_columns[0]], axis=1).astype(F32)
    places = jnp.take(places.reshape(4, rows, 2), order, axis=0).reshape(full, 2)
    ends = jnp.cumsum(item_lengths[0])
    share, order, places, ends = sync(share, order, places, ends)
    shares = [share, flip(share, 1), flip(share, 2), flip(share, 3)]
    side = kernel_call(
        functools.partial(setup_kernel, head, items, spans),
        [out for n in sizes for out in (like(5, n, LANES), like(n, LANES))],
        ends, item_condition[0], order, places,
        scalars=3, name="setup", us=3.0, hbm=(0, 2, 4),
    )
    order, expansion, *both = sync(order, expansion, *shares, *side)
    shares, side, pick = both[:4], both[4::2], both[5::2]
    (table,) = kernel_call(
        functools.partial(columns_kernel, 4),
        [like(12, width)],
        order, *[in_hbm(share) for share in shares], offsets,
        scalars=1, name="columns",
    )
    expansion_flat = expansion.reshape(width, 2 * units)
    x_halves = halves(x_one, x_two)
    x_one, x_two, dy, table, expansion_flat, *x_halves = sync(
        x_one, x_two, dy, table, expansion_flat, *x_halves
    )

    x_far = flip(x_halves[0], 2), flip(x_halves[1], 1)
    x_parts = [[x], [x_one, x_two], list(x_far)]

    def enter(k, parts):
        n = sizes[k]
        return kernel_call(
            functools.partial(enter_kernel, head, len(parts)),
            [
                like(n, width, dtype=BF),
                like(n, padded, dtype=BF),
                like(n, padded, dtype=BF),
                like(n, padded, dtype=BF),
                like(n, 2 * part, dtype=BF),
            ],
            *parts, side[k], pick[k], table, gains, inward_rows,
            name="enter", hbm=(0, 4), us=3.3 * n / rows,
        )

    entered = [None, list(enter(1, x_parts[1]))]
    x_far, dy, entered[1][1], x_own = sync(x_far, dy, entered[1][1], x)
    dy_one, dy_two = flip(dy, 1), flip(dy, 2)
    entered[0] = list(enter(0, [x_own]))
    x_far = list(x_far)
    x_parts[2] = x_far

    entered.append(enter(2, x_far))
    first_in, queries, keys, values, raws = zip(*entered)

    def attend(k, query):
        n = sizes[k]
        return kernel_call(
            functools.partial(forward_kernel, head, 3),
            [like(n, width, dtype=BF), like(n, part, dtype=BF), like(n, padded, dtype=BF)],
            query, *keys, *values, outward_rows,
            name="attend", hbm=(1, 2) if k == 2 else (), us=2.0 * n / rows,
        )

    attended = [None, None, attend(2, queries[2])]
    far, query_near, dy_one, dy_two = sync(attended[2][0], queries[1], dy_one, dy_two)

    got = scatter_first(far)
    attended[1] = attend(1, query_near)
    near, query_own, got, dy_one, dy_two = sync(
        attended[1][0], queries[0], got, dy_one, dy_two
    )

    sums = scatter_second(near, got)
    dy_far = relay(dy_one, dy_two)
    attended[0] = attend(0, query_own)
    own, cond_low, sums, dy_far = sync(attended[0][0], cond_low, sums, dy_far)
    dy_far = list(dy_far)

    attended_own, middle, second = kernel_call(
        middle_kernel,
        [like(rows, width, dtype=BF), like(rows, width), like(rows, width, dtype=BF)],
        x, own, *sums, pick[0], table,
        name="middle",
    )
    second, cond_low, dy, dy_one, dy_two = sync(second, cond_low, dy, dy_one, dy_two)
    second_one, second_two = flip(second, 1), flip(second, 2)
    dy_parts = [[dy], [dy_one, dy_two], dy_far]
    fed_grad, hidden_grad = [], []
    for k in range(3):
        outs = kernel_call(
            functools.partial(hidden_grad_kernel, len(dy_parts[k])),
            [like(sizes[k], width, dtype=BF), like(sizes[k], units)],
            *dy_parts[k], pick[k], table, contraction,
            name="hidden_grad", us=0.8 * sizes[k] / rows,
        )
        fed_grad.append(outs[0])
        hidden_grad.append(outs[1])
    conds = jnp.transpose(gather_small(cond_low, dp), (1, 0, 2)).reshape(2 * dp, width)
    conds = lax.dynamic_slice_in_dim(conds, dp_me * lanes, lanes, 1).astype(F32)
    second_one, second_two, conds, *hidden_grad = sync(second_one, second_two, conds, *hidden_grad)

    second_far = relay(second_one, second_two)
    second_parts = [[second], [second_one, second_two], list(second_far)]

    def through(k, parts):
        n = sizes[k]
        return kernel_call(
            functools.partial(units_kernel, len(parts)),
            [
                like(n, units, dtype=BF),
                like(n, 2 * units, dtype=BF),
                like(n, width, dtype=BF),
            ],
            *parts, hidden_grad[k], expansion_flat,
            name="units", hbm=(2,) if k == 1 else (), us=2.5 * n / rows,
        )

    passed = [through(0, second_parts[0]), through(1, second_parts[1])]
    *second_far, near, own = sync(*second_far, passed[1][2], passed[0][2])
    second_parts[2] = second_far
    passed.append(through(2, second_far))
    hidden, widening, back = zip(*passed)
    far, hidden_far = sync(back[2], hidden[2])

    got = scatter_first(far)
    wide = weights_call(
        [
            (sum(second_parts, []), widening),
            (fed_grad, [*hidden[:2], hidden_far]),
        ],
        dp,
        "wide",
        6.0,
        18,
    )
    wide, near, hidden_far, got = sync(wide, near, hidden_far, got)

    sums = scatter_second(near, got)
    wide = sum_start(wide)
    fed_parts, fed_slots = [None] * 3, [None] * 3
    for k, source in ((1, hidden[1]), (2, hidden_far), (0, hidden[0])):
        if k == 2:
            fed_parts[1], wide, source = sync(fed_parts[1], wide, source)
            wide = sum_merge(wide, "merge")
        if k == 0:
            fed_parts[2], wide, source = sync(fed_parts[2], wide, source)
            wide[3] = swap(wide[3], 2)
        fed_parts[k], fed_slots[k] = kernel_call(
            functools.partial(fed_part_kernel, len(dy_parts[k])),
            [like(sizes[k], width, dtype=BF), like(2, width)],
            *dy_parts[k], source, pick[k], contraction,
            name="fed_part", hbm=(0, 1), us=1.0 * sizes[k] / rows,
        )
    own, sums, fed_parts[0] = sync(own, sums, fed_parts[0])

    middle_grad, send, slots_two = kernel_call(
        middle_back_kernel,
        [like(rows, width), like(rows, width, dtype=BF), like(6, width)],
        own, *sums, middle, attended_own, dy, pick[0], table,
        name="middle_back", hbm=(0, 2), us=1.7,
    )
    send_one, send_two = flip(send, 1), flip(send, 2)

    def attend_back(k, parts, sums):
        n = sizes[k]
        given = (*parts, outward_rows, attended[k][1], attended[k][2], *keys, *values)
        out = kernel_call(
            functools.partial(backward_kernel, head, 3, not sums, len(parts)),
            [like(n, padded)] + [like(a.shape[0], padded) for a in keys + values],
            *given, *sums,
            aliases={len(given) + i: 1 + i for i in range(len(sums))},
            name="attend_back", us=4.3 * n / rows, mib=16,
        )
        return out[0], tuple(out[1:])

    query_grads = [None] * 3
    query_grads[0], totals = attend_back(0, [send], ())
    send_one, send_two, totals, wide = sync(send_one, send_two, totals, wide)

    send_far = relay(send_one, send_two)
    wide[2] = swap(plus(wide[2], wide[3]), 4)
    query_grads[1], totals = attend_back(1, [send_one, send_two], totals)
    send_far, totals, fed_far, wide[1] = sync(send_far, totals, fed_parts[2], wide[1])

    fed_got = scatter_first(fed_far)
    wide[1] = swap(wide[1], 2)
    send_parts = [[send], [send_one, send_two], list(send_far)]
    query_grads[2], totals = attend_back(2, send_far, totals)
    key_grads, value_grads = totals[:3], totals[3:]

    def leave(k, query_grad):
        n = sizes[k]
        return kernel_call(
            functools.partial(leave_kernel, head, len(x_parts[k])),
            [
                like(n, 3 * part, dtype=BF),
                like(n, width, dtype=BF),
                like(4, width),
                like(1, 2 * head),
            ],
            *x_parts[k], query_grad, key_grads[k], value_grads[k], raws[k], side[k], pick[k], gains,
            inward_rows,
            name="leave", hbm=(0, 2, 3), us=3.8 * n / rows,
        )

    left = [None, None, leave(2, query_grads[2])]
    far, query_near, fed_near, fed_got = sync(left[2][1], query_grads[1], fed_parts[1], fed_got)

    got = scatter_first(far)
    left[1] = leave(1, query_near)
    near, query_own, got = sync(left[1][1], query_grads[0], got)

    left[0] = sync(*leave(0, query_own))

    parts = left[0][2], left[1][2], left[2][2], slots_two, *fed_slots
    packed = kernel_call(
        pack_kernel,
        [like(2, 37, part)] * 2,
        order, *[in_hbm(v) for v in (*parts, left[0][3], left[1][3], left[2][3])],
        scalars=1, name="pack", us=1.0,
    )
    packed = packed[0] + flip(packed[1], 1)
    narrow = weights_call(
        [
            (first_in, [left[k][0] for k in range(3)]),
            (sum(send_parts, []), [attended[k][1] for k in range(3)]),
        ],
        dp,
        "narrow",
        0.1,
        16,
    )
    narrow, packed, wide[1], wide[2] = sync(narrow, packed, wide[1], wide[2])

    narrow = sum_start(narrow)
    packed = packed[0] + flip(packed[1], 2)
    narrow, packed, near, got = sync(narrow, packed, near, got)

    narrow = sum_merge(narrow, "merge")
    narrow[3] = swap(narrow[3], 2)
    sums = scatter_second(near, got)
    every = gather_small(packed, dp)
    expansion_gradient, contraction_gradient = spread(
        [2, 1], [like(2, lanes, units), like(1, lanes, units)], wide[:3]
    )
    narrow[1], narrow[2], narrow[3], sums, fed_near, expansion_gradient, every = sync(
        narrow[1], narrow[2], narrow[3], sums, fed_parts[1], expansion_gradient, every
    )

    narrow[2] = swap(plus(narrow[2], narrow[3]), 4)
    narrow[1] = swap(narrow[1], 2)
    fed_sums = scatter_second(fed_near, fed_got)
    (token_gradient,) = kernel_call(
        token_kernel,
        [like(rows, width)],
        left[0][1], *sums, x, middle_grad, pick[0], table,
        name="token", us=8.0,
    )
    (layer_output,) = kernel_call(
        fed_kernel,
        [like(rows, width, dtype=BF)],
        fed_parts[0], *fed_sums, middle, pick[0], table,
        name="fed", us=8,
    )
    expansion_gradient = jnp.transpose(expansion_gradient, (1, 0, 2))
    modulator_gradient, bias_gradient, gain_sum = kernel_call(
        slots_kernel,
        [like(6, lanes, part), like(6, width), like(1, part)],
        conds, every,
        name="slots", us=8.0,
    )
    narrow[0], expansion_gradient, token_gradient, modulator_gradient = sync(
        narrow[0], expansion_gradient, token_gradient, modulator_gradient
    )
    inward_gradient, outward_gradient = spread(
        [3, 1], [like(3, lanes, part), like(1, lanes, part)], narrow[:3]
    )
    return (
        layer_output[None],
        token_gradient[None],
        jnp.transpose(modulator_gradient, (1, 0, 2)),
        bias_gradient,
        jnp.transpose(inward_gradient, (1, 0, 2)),
        gain_sum[0, :head],
        gain_sum[0, head : 2 * head],
        outward_gradient[0],
        expansion_gradient,
        contraction_gradient[0],
    )


def solution(mesh):
    placed = (
        P("dp", "tp", None),
        P("dp", None),
        P(None, None, "tp"),
        P(),
        P(None, None, "tp"),
        P(),
        P(),
        P(None, "tp"),
        P(None, None, "tp"),
        P(None, "tp"),
        P("dp", None),
        P("dp", None),
        P("dp", None),
        P("dp", None),
        P("dp", "tp", None),
    )
    return jax.shard_map(
        shards,
        mesh=mesh,
        in_specs=placed,
        out_specs=(
            P("dp", "tp", None),
            P("dp", "tp", None),
            P("dp", None, "tp"),
            P(),
            P("dp", None, "tp"),
            P(),
            P(),
            P("dp", "tp"),
            P("dp", None, "tp"),
            P("dp", "tp"),
        ),
        check_vma=False,
    )
```

```python
import functools
import math

import jax
import jax.numpy as jnp
from jax import lax
from jax.experimental import pallas as pl
from jax.experimental.pallas import tpu as pltpu
from jax.sharding import PartitionSpec as P

BF = jnp.bfloat16
F32 = jnp.float32
LANES = 128
EPS = 1e-06
NN = ((1,), (0,))
NT = ((1,), (1,))
TN = ((0,), (0,))
MASKED = -30000.0


def dot(left, right, dims):
    return lax.dot_general(left, right, (dims, ((), ())), preferred_element_type=F32)


def flip(value, by):
    return lax.ppermute(value, "tp", [(i, i ^ by) for i in range(4)])


def halves(one, two):
    half = one.shape[0] // 2
    return one[:half], two[half:]


def relay(one, two):
    low, high = halves(one, two)
    return flip(low, 2), flip(high, 1)


def scatter_first(far):
    half = far.shape[0] // 2
    return flip(far[:half], 1), flip(far[half:], 2)


def total(*refs):
    return sum(ref[...].astype(F32) for ref in refs)


def join_kernel(near_ref, via_one_ref, via_two_ref, one_ref, two_ref):
    rows = one_ref.shape[0]
    half = rows // 2
    one_ref[:half, :] = near_ref[:half, :]
    one_ref[half:, :] = near_ref[half:rows, :] + via_two_ref[...]
    two_ref[:half, :] = near_ref[rows : rows + half, :] + via_one_ref[...]
    two_ref[half:, :] = near_ref[rows + half :, :]


def joined(near, got):
    out = like(near.shape[0] // 2, near.shape[1], dtype=near.dtype)
    return kernel_call(join_kernel, [out, out], near, *got, name="join")


def scatter_second(near, got):
    one, two = joined(near, got)
    return flip(one, 1), flip(two, 2)


def gather_core(own, dp):
    return jnp.stack([own, swap(own, 1)]) if dp == 8 else own


def gather_chips(pair, dp):
    if dp != 8:
        return lax.all_gather(pair, "dp", axis=0)
    four = jnp.concatenate([pair, swap(pair, 2)], axis=0)
    return jnp.concatenate([four, swap(four, 4)], axis=0)


def gather_small(own, dp):
    return gather_chips(gather_core(own, dp), dp)


def pack_kernel(order_ref, *refs):
    first, two_ref, fed, gains, out_refs = refs[:3], refs[3], refs[4:7], refs[7:10], refs[10:]
    cut = out_refs[0].shape[-1]
    tall = jnp.concatenate([total(*first), two_ref[...], total(*fed)], axis=0)
    gain = total(*gains)
    gain = jnp.concatenate([gain, jnp.zeros((1, cut - gain.shape[1]), F32)], axis=1)
    parts = [tall[:, j * cut : (j + 1) * cut] for j in range(4)]
    bias = []
    for part in parts:
        bias += [part[2 * j : 2 * j + 1] + part[2 * j + 1 : 2 * j + 2] for j in range(6)]
    below = jnp.concatenate([gain, *bias], axis=0)
    for k in range(4):
        part = parts[0]
        for j in range(1, 4):
            part = jnp.where(order_ref[k] == j, parts[j], part)
        out_refs[k % 2][k // 2] = jnp.concatenate([part, below], axis=0)


def slots_kernel(conds_ref, every_ref, grad_ref, bias_ref, gain_ref):
    conds = conds_ref[...]
    cut = every_ref.shape[2]
    gain_ref[...] = jnp.sum(every_ref[:, 12, :], axis=0, keepdims=True)
    for j in range(6):
        both = [every_ref[:, 2 * j + c, :] for c in range(2)]
        grad_ref[j] = lax.dot_general(
            conds,
            jnp.concatenate(both, axis=0),
            (TN, ((), ())),
            precision=lax.Precision.HIGHEST,
            preferred_element_type=F32,
        )
        for q in range(4):
            own = every_ref[:, 13 + 6 * q + j, :]
            bias_ref[j : j + 1, q * cut : (q + 1) * cut] = jnp.sum(own, axis=0, keepdims=True)


def columns_kernel(pieces, order_ref, *refs):
    add_ref, out_ref = refs[pieces:]
    stacked = jnp.stack([ref[...] for ref in refs[:pieces]])
    parts = []
    for j in range(pieces):
        part = stacked[0]
        for k in range(1, pieces):
            part = jnp.where(order_ref[j] == k, stacked[k], part)
        parts.append(part)
    out = jnp.concatenate(parts, axis=1)
    add = add_ref[...]
    if add.shape[0] < out.shape[0]:
        add = jnp.concatenate([add, add], axis=0)
    out_ref[...] = out + add


def gather_tp_columns(own, add):
    order = jnp.arange(4, dtype=jnp.int32) ^ lax.axis_index("tp")
    (out,) = kernel_call(
        functools.partial(columns_kernel, 4),
        [like(own.shape[0], 4 * own.shape[1])],
        order, own, flip(own, 1), flip(own, 2), flip(own, 3), add,
        scalars=1,
        name="columns",
    )
    return out


def kernel_call(body, outs, *args, aliases=None, name=None, scalars=0, us=1.0, mib=16, hbm=()):
    spec = pl.BlockSpec(memory_space=pltpu.VMEM)
    given = [pl.BlockSpec(memory_space=pltpu.SMEM)] * scalars + [spec] * (len(args) - scalars)
    return pl.pallas_call(
        body,
        out_shape=[pltpu.HBM(o.shape, o.dtype) if i in hbm else o for i, o in enumerate(outs)],
        in_specs=given,
        out_specs=[spec] * len(outs),
        input_output_aliases=aliases or {},
        compiler_params=pltpu.CompilerParams(vmem_limit_bytes=mib * 1024 * 1024),
        cost_estimate=pl.CostEstimate(flops=int(us * 1.15e9), bytes_accessed=1, transcendentals=0),
        name=name,
    )(*args)


def like(*shape, dtype=F32):
    return jax.ShapeDtypeStruct(shape, dtype)


def norm(values):
    count = values.shape[-1]
    center = values - jnp.sum(values, axis=-1, keepdims=True) * (1.0 / count)
    inverse = lax.rsqrt(jnp.sum(center * center, axis=-1, keepdims=True) * (1.0 / count) + EPS)
    return center * inverse, inverse


def norm_back(grad, normed, inverse):
    count = grad.shape[-1]
    middle = jnp.sum(grad, axis=-1, keepdims=True) * (1.0 / count)
    slope = jnp.sum(grad * normed, axis=-1, keepdims=True) * (1.0 / count)
    return inverse * (grad - middle - normed * slope)


def choose(pick, table_ref, column):
    return jnp.where(pick, table_ref[6 + column : 7 + column, :], table_ref[column : column + 1, :])


def slot_sums(pick, values):
    zero = jnp.zeros_like(values)
    return [
        jnp.sum(jnp.where(pick, zero, values), axis=0, keepdims=True),
        jnp.sum(jnp.where(pick, values, zero), axis=0, keepdims=True),
    ]


def picks(pick_ref, width):
    return jnp.broadcast_to(pick_ref[:, 0:1], (pick_ref.shape[0], width)) > 0.5


def lane_sums(values):
    ones = jnp.ones((values.shape[1], values.shape[1]), BF)
    high = values.astype(BF)
    low = (values - high.astype(F32)).astype(BF)
    return dot(high, ones, NN) + dot(low, ones, NN)


def widen(values):
    return jnp.concatenate(
        [values, jnp.zeros((values.shape[0], LANES - values.shape[1]), values.dtype)], axis=1
    )


def stack_rows(refs):
    return refs[0][...] if len(refs) == 1 else jnp.concatenate([ref[...] for ref in refs], axis=0)


def setup_kernel(head, items, spans, ends_ref, conds_ref, order_ref, places_ref, *out_refs):
    rows = places_ref.shape[0] // 4
    quarter = head // 4
    for s, (low, high) in enumerate(spans):
        count = high - low
        shape = (count, LANES)
        lane = lax.broadcasted_iota(jnp.int32, shape, 1)
        row = lax.broadcasted_iota(jnp.int32, shape, 0)
        start = jnp.full(shape, order_ref[low // rows] * rows, jnp.int32)
        if count > rows:
            start = jnp.where(row >= rows, order_ref[low // rows + 1] * rows - rows, start)
        token = start + row
        owner = jnp.zeros(shape, jnp.int32)
        for j in range(items):
            owner = owner + (token >= ends_ref[j]).astype(jnp.int32)
        pick = jnp.zeros(shape, jnp.int32)
        for j in range(items):
            pick = jnp.where(owner == j, conds_ref[j], pick)
        place = jnp.where(
            lane < 2 * quarter,
            jnp.broadcast_to(places_ref[low:high, 0:1], shape),
            jnp.broadcast_to(places_ref[low:high, 1:2], shape),
        )
        phase = lane
        for j in range(1, 4):
            phase = jnp.where(lane >= j * quarter, lane - j * quarter, phase)
        angles = place * jnp.exp(phase.astype(F32) * (-math.log(10000.0) / quarter))
        real = lane < head
        sine = jnp.sin(angles)
        lower = (lane < quarter) | ((lane >= 2 * quarter) & (lane < 3 * quarter))
        zero = jnp.zeros(shape, F32)
        out_ref, pick_ref = out_refs[2 * s : 2 * s + 2]
        out_ref[0] = jnp.where(real, jnp.cos(angles), zero)
        out_ref[1] = jnp.where(real & lower, -sine, zero)
        out_ref[2] = jnp.where(real & ~lower, sine, zero)
        base = head + 8
        mine = jnp.where(lane == owner + base, 1.0, 0.0)
        out_ref[3] = mine
        marks = jnp.where((lane >= head + 4) & (lane < head + 7), 1.0, zero)
        slots = (lane >= base) & (lane < base + items)
        out_ref[4] = jnp.where(slots, MASKED * (1.0 - mine), marks)
        pick_ref[...] = pick.astype(F32)


def enter_kernel(head, count, *refs):
    x = stack_rows(refs[:count])
    side_ref, pick_ref, table_ref, gain_ref, weight_ref = refs[count : count + 5]
    first_ref, query_ref, key_ref, value_ref, raw_ref = refs[count + 5 :]
    rows, width = x.shape
    part = weight_ref.shape[0] // 3
    heads = part // head
    pick = picks(pick_ref, width)
    normed, _ = norm(x.astype(F32))
    low = (normed * (1.0 + choose(pick, table_ref, 1)) + choose(pick, table_ref, 0)).astype(BF)
    first_ref[...] = low
    raw = dot(low, weight_ref[...], NT)
    raw_ref[...] = raw[:, : 2 * part].astype(BF)
    cosine, near, far = side_ref[0], side_ref[1], side_ref[2]
    scale = math.log2(math.e) / math.sqrt(head)
    for kind in range(2):
        gain = gain_ref[kind : kind + 1, :]
        if kind == 0:
            gain = gain * scale
        target = (query_ref, key_ref)[kind]
        for h in range(heads):
            at = kind * part + h * head
            own = widen(raw[:, at : at + head])
            inverse = lax.rsqrt(lane_sums(own * own) * (1.0 / head) + EPS)
            own = own * inverse * gain
            turned = (
                own * cosine
                + pltpu.roll(own, LANES - head // 4, 1) * near
                + pltpu.roll(own, head // 4, 1) * far
            )
            target[:, pl.ds(h * LANES, LANES)] = (turned + side_ref[3 + kind]).astype(BF)
    lane = lax.broadcasted_iota(jnp.int32, (rows, LANES), 1)
    ones = ((lane >= head) & (lane < head + 3)).astype(F32)
    for h in range(heads):
        at = 2 * part + h * head
        value_ref[:, pl.ds(h * LANES, LANES)] = (widen(raw[:, at : at + head]) + ones).astype(BF)


def split_three(value):
    one = value.astype(BF).astype(F32)
    rest = value - one
    two = rest.astype(BF).astype(F32)
    return one, two, rest - two


def forward_kernel(head, pieces, query_ref, *refs):
    keys, values = refs[:pieces], refs[pieces : 2 * pieces]
    outward_ref, partial_ref, mixed_ref, again_ref = refs[2 * pieces :]
    rows = query_ref.shape[0]
    heads = query_ref.shape[1] // LANES
    lane = lax.broadcasted_iota(jnp.int32, (rows, LANES), 1)
    mixed = []
    for h in range(heads):
        place = pl.ds(h * LANES, LANES)
        query = query_ref[:, place]
        out = None
        for key_ref, value_ref in zip(keys, values):
            weights = jnp.exp2(dot(query, key_ref[:, place], NT)).astype(BF)
            term = dot(weights, value_ref[:, place], NN)
            out = term if out is None else out + term
        total = out[:, head : head + 1]
        mixed.append((out[:, :head] * (1.0 / total)).astype(BF))
        one, two, three = split_three(-jnp.log2(total))
        marks = jnp.where(lane == head + 4, one, 0.0)
        marks = jnp.where(lane == head + 5, two, marks)
        marks = jnp.where(lane == head + 6, three, marks)
        again_ref[:, place] = (query.astype(F32) + marks).astype(BF)
    mixed = jnp.concatenate(mixed, axis=1)
    mixed_ref[...] = mixed
    partial_ref[...] = dot(mixed, outward_ref[...], NN).astype(partial_ref.dtype)


def backward_kernel(head, pieces, first, count, *refs):
    sent = stack_rows(refs[:count])
    outward_ref, mixed_ref, query_ref = refs[count : count + 3]
    refs = refs[count + 3 :]
    keys, values = refs[:pieces], refs[pieces : 2 * pieces]
    refs = refs[2 * pieces :]
    if not first:
        key_in, value_in = refs[:pieces], refs[pieces : 2 * pieces]
        refs = refs[2 * pieces :]
    query_out = refs[0]
    key_out, value_out = refs[1 : 1 + pieces], refs[1 + pieces :]
    rows = query_ref.shape[0]
    heads = query_ref.shape[1] // LANES
    lane = lax.broadcasted_iota(jnp.int32, (rows, LANES), 1)
    grads = dot(sent, outward_ref[...], NT).astype(BF).astype(F32)
    mixed = mixed_ref[...].astype(F32)
    for h in range(heads):
        place = pl.ds(h * LANES, LANES)
        cut = slice(h * head, (h + 1) * head)
        grad = grads[:, cut]
        centre = jnp.sum(grad * mixed[:, cut], axis=-1, keepdims=True)
        one, two, three = split_three(-centre)
        grad = widen(grad)
        grad = jnp.where(lane == head, one, grad)
        grad = jnp.where(lane == head + 1, two, grad)
        grad = jnp.where(lane == head + 2, three, grad).astype(BF)
        query = query_ref[:, place]
        query_grad = None
        for j in range(pieces):
            key, value = keys[j][:, place], values[j][:, place]
            weights = jnp.exp2(dot(key, query, NT))
            score_grad = (weights * dot(value, grad, NT)).astype(BF)
            value_grad = dot(weights.astype(BF), grad, NN)
            key_grad = dot(score_grad, query, NN)
            if not first:
                value_grad += value_in[j][:, place]
                key_grad += key_in[j][:, place]
            value_out[j][:, place] = value_grad
            key_out[j][:, place] = key_grad
            term = dot(key, score_grad, TN)
            query_grad = term if query_grad is None else query_grad + term
        query_out[:, place] = query_grad.T


def leave_kernel(head, count, *refs):
    x = stack_rows(refs[:count])
    query_grad_ref, key_grad_ref, value_grad_ref, raw_ref, side_ref, pick_ref = refs[count : count + 6]
    gain_ref, weight_ref, projected_ref, partial_ref, slots_ref, gains_ref = refs[count + 6 :]
    rows, width = x.shape
    part = weight_ref.shape[0] // 3
    heads = part // head
    cosine, near, far = side_ref[0], side_ref[1], side_ref[2]
    raw = raw_ref[...].astype(F32)
    pieces = []
    gain_grads = []
    for kind in range(2):
        gain = gain_ref[kind : kind + 1, :]
        source = (query_grad_ref, key_grad_ref)[kind]
        scale = (1.0 / math.sqrt(head), math.log(2.0))[kind]
        gain_grad = None
        for h in range(heads):
            grad = source[:, pl.ds(h * LANES, LANES)] * scale
            grad = (
                grad * cosine
                + pltpu.roll(grad * near, head // 4, 1)
                + pltpu.roll(grad * far, LANES - head // 4, 1)
            )
            at = kind * part + h * head
            own = widen(raw[:, at : at + head])
            inverse = lax.rsqrt(lane_sums(own * own) * (1.0 / head) + EPS)
            own = own * inverse
            term = grad * own
            gain_grad = term if gain_grad is None else gain_grad + term
            slope = lane_sums(term * gain) * (1.0 / head)
            pieces.append((inverse * (grad * gain - own * slope))[:, :head].astype(BF))
        gain_grad = jnp.sum(gain_grad, axis=0, keepdims=True)
        gain_grads.append(gain_grad[:, :head])
    gains_ref[...] = jnp.concatenate(gain_grads, axis=1)
    for h in range(heads):
        pieces.append(value_grad_ref[:, pl.ds(h * LANES, head)].astype(BF))
    projected = jnp.concatenate(pieces, axis=1)
    projected_ref[...] = projected
    grad = dot(projected, weight_ref[...], NN)
    partial_ref[...] = grad.astype(partial_ref.dtype)
    pick = picks(pick_ref, width)
    normed, _ = norm(x.astype(F32))
    slots_ref[...] = jnp.concatenate(slot_sums(pick, grad) + slot_sums(pick, grad * normed), axis=0)


def middle_kernel(x_ref, own_ref, one_ref, two_ref, side_ref, table_ref,
                  attended_ref, middle_ref, second_ref):
    attended = total(own_ref, one_ref, two_ref)
    attended_ref[...] = attended.astype(BF)
    pick = picks(side_ref, x_ref.shape[1])
    middle = x_ref[...].astype(F32) + choose(pick, table_ref, 2) * attended
    middle_ref[...] = middle
    normed, _ = norm(middle)
    second_ref[...] = (
        normed * (1.0 + choose(pick, table_ref, 4)) + choose(pick, table_ref, 3)
    ).astype(BF)


def units_kernel(count, *refs):
    second = stack_rows(refs[:count])
    grad_ref, weight_ref, hidden_ref, widening_ref, partial_ref = refs[count:]
    units = grad_ref.shape[1]
    both = dot(second, weight_ref[...], NN)
    gate, up = both[:, :units], both[:, units:]
    sigmoid = 1.0 / (1.0 + jnp.exp(-gate))
    active = gate * sigmoid
    hidden_ref[...] = (active * up).astype(BF)
    grad = grad_ref[...]
    gate_grad = (grad * up * (sigmoid + active * (1.0 - sigmoid))).astype(BF)
    widening = jnp.concatenate([gate_grad, (grad * active).astype(BF)], axis=1)
    widening_ref[...] = widening
    partial_ref[...] = dot(widening, weight_ref[...], NT).astype(partial_ref.dtype)


def hidden_grad_kernel(count, *refs):
    dy = stack_rows(refs[:count])
    side_ref, table_ref, weight_ref, fed_ref, out_ref = refs[count:]
    pick = picks(side_ref, dy.shape[1])
    fed = (choose(pick, table_ref, 5) * dy.astype(F32)).astype(BF)
    fed_ref[...] = fed
    out_ref[...] = dot(fed, weight_ref[...], NN)


def fed_part_kernel(count, *refs):
    dy = stack_rows(refs[:count])
    hidden_ref, side_ref, weight_ref, out_ref, slots_ref = refs[count:]
    fed = dot(hidden_ref[...], weight_ref[...], NT)
    out_ref[...] = fed.astype(BF)
    slots_ref[...] = jnp.concatenate(
        slot_sums(picks(side_ref, dy.shape[1]), dy.astype(F32) * fed), axis=0
    )


def weights_kernel(counts, cuts, core_ref, *refs):
    *refs, room_ref, sems = refs
    pairs = []
    for lefts, rights in counts:
        pairs.append((refs[:lefts], stack_rows(refs[lefts : lefts + rights])))
        refs = refs[lefts + rights :]
    outs = refs
    height = room_ref.shape[0]
    blocks = len(outs) * outs[0].shape[0]
    size = height // blocks
    copies = []
    step = height // cuts
    for low in range(0, height, step):
        at = 0
        for lefts, right in pairs:
            left = [ref[:, low : low + step] for ref in lefts]
            left = left[0] if len(left) == 1 else jnp.concatenate(left, axis=0)
            high = at + right.shape[1]
            room_ref[low : low + step, at:high] = dot(left, right, TN).astype(BF)
            at = high
        while len(copies) < blocks and (len(copies) + 1) * size <= low + step:
            j = len(copies)
            rows = room_ref.at[j * size : (j + 1) * size, :]
            to = [pltpu.make_async_copy(rows, out.at[j // len(outs)], sems.at[j]) for out in outs]
            if len(outs) == 1:
                to[0].start()
            else:

                @pl.when(core_ref[0] == j % 2)
                def _(copy=to[0]):
                    copy.start()

                @pl.when(core_ref[0] != j % 2)
                def _(copy=to[1]):
                    copy.start()

            copies.append(to[0])
    for copy in copies:
        copy.wait()


def weights_call(pairs, dp, name, us, mib):
    args, counts = [], []
    for lefts, rights in pairs:
        args += [*lefts, *rights]
        counts.append((len(lefts), len(rights)))
    height = pairs[0][0][0].shape[1]
    wide = sum(rights[0].shape[1] for _, rights in pairs)
    outs = 2 if dp == 8 else 1
    blocks = dp if outs == 2 else 1
    return pl.pallas_call(
        functools.partial(weights_kernel, counts, 3),
        out_shape=[pltpu.HBM((blocks // outs, height // blocks, wide), BF)] * outs,
        in_specs=[pl.BlockSpec(memory_space=pltpu.SMEM)]
        + [pl.BlockSpec(memory_space=pltpu.VMEM)] * len(args),
        out_specs=[pl.BlockSpec(memory_space=pltpu.HBM)] * outs,
        scratch_shapes=[pltpu.VMEM((height, wide), BF), pltpu.SemaphoreType.DMA((blocks,))],
        compiler_params=pltpu.CompilerParams(vmem_limit_bytes=mib * 1024 * 1024),
        cost_estimate=pl.CostEstimate(flops=int(us * 1.15e9), bytes_accessed=1, transcendentals=0),
        name=name,
    )((lax.axis_index("dp") % 2).reshape(1).astype(jnp.int32), *args)


def swap(value, by):
    return None if value is None else lax.ppermute(value, "dp", [(i, i ^ by) for i in range(8)])


def merge_kernel(place_ref, keep_ref, got_ref, *out_refs):
    for k, ref in enumerate(out_refs):
        at = place_ref[0] ^ k
        ref[...] = keep_ref[at] + got_ref[at]


def sum_start(outs):
    if len(outs) == 1:
        total_sum = lax.psum_scatter(outs[0][0], "dp", scatter_dimension=0, tiled=True)
        return [total_sum, None, None, None]
    return [outs[0], swap(outs[1], 1), None, None]


def sum_merge(parts, name):
    if parts[1] is None:
        return parts
    _, size, wide = parts[0].shape
    place = (lax.axis_index("dp") // 2).reshape(1).astype(jnp.int32)
    outs = kernel_call(
        merge_kernel,
        [like(size, wide, dtype=BF)] * 4,
        place, in_hbm(parts[0]), parts[1],
        scalars=1, name=name, us=3.0, hbm=(0,),
    )
    return list(outs)


def plus(left, right):
    return None if left is None else left + right


def spread(groups, outs, parts):
    parts = [part for part in parts if part is not None]
    return kernel_call(
        functools.partial(spread_kernel, groups, len(parts)), outs, *parts, name="spread"
    )


def in_hbm(value):
    return pltpu.with_memory_space_constraint(value, pltpu.HBM)


def middle_back_kernel(own_ref, one_ref, two_ref, middle_ref, attended_ref, dy_ref, side_ref, table_ref,
                       grad_ref, send_ref, slots_ref):
    pick = picks(side_ref, dy_ref.shape[1])
    second_grad = total(own_ref, one_ref, two_ref)
    normed, inverse = norm(middle_ref[...])
    grad = dy_ref[...].astype(F32) + norm_back(
        second_grad * (1.0 + choose(pick, table_ref, 4)), normed, inverse
    )
    grad_ref[...] = grad
    send_ref[...] = (choose(pick, table_ref, 2) * grad).astype(BF)
    slots_ref[...] = jnp.concatenate(
        slot_sums(pick, grad * attended_ref[...].astype(F32))
        + slot_sums(pick, second_grad)
        + slot_sums(pick, second_grad * normed),
        axis=0,
    )


def fed_kernel(own_ref, one_ref, two_ref, middle_ref, side_ref, table_ref, out_ref):
    pick = picks(side_ref, middle_ref.shape[1])
    fed = total(own_ref, one_ref, two_ref)
    out_ref[...] = (middle_ref[...] + choose(pick, table_ref, 5) * fed).astype(BF)


def spread_kernel(groups, count, *refs):
    parts, out_refs = refs[:count], refs[count:]
    at = 0
    for group, ref in zip(groups, out_refs):
        width = ref.shape[-1]
        for j in range(group):
            ref[j] = total(*[part.at[:, at : at + width] for part in parts])
            at += width


def token_kernel(own_ref, one_ref, two_ref, x_ref, grad_ref, side_ref, table_ref, out_ref):
    pick = picks(side_ref, x_ref.shape[1])
    first_grad = total(own_ref, one_ref, two_ref)
    normed, inverse = norm(x_ref[...].astype(F32))
    out_ref[...] = grad_ref[...] + norm_back(
        first_grad * (1.0 + choose(pick, table_ref, 1)), normed, inverse
    )


def sync(*values):
    return lax.optimization_barrier(values)


def shards(
    tokens,
    condition,
    modulator,
    offsets,
    inward,
    query_gain,
    key_gain,
    outward,
    expansion,
    contraction,
    item_lengths,
    item_condition,
    patch_rows,
    patch_columns,
    cotangent,
):
    _, rows, width = tokens.shape
    full = patch_rows.shape[1]
    head = query_gain.shape[0]
    part = inward.shape[2]
    heads = part // head
    units = contraction.shape[1]
    items = item_lengths.shape[1]
    dp = lax.axis_size("dp")
    me = lax.axis_index("tp")
    dp_me = lax.axis_index("dp")
    lanes = width // dp
    padded = heads * LANES
    spans = ((0, rows), (rows, 3 * rows), (3 * rows, full))
    sizes = [high - low for low, high in spans]

    x, dy = tokens[0], cotangent[0]
    x_one, x_two = flip(x, 1), flip(x, 2)
    cond_low = jax.nn.silu(condition.astype(F32)).astype(BF)
    share = dot(cond_low, jnp.transpose(modulator, (1, 2, 0)).reshape(-1, width), NT)
    share = share.reshape(12, part)
    inward_rows = jnp.transpose(inward, (1, 2, 0)).reshape(3 * part, width)
    outward_rows = outward.T
    gains = jnp.pad(jnp.stack([query_gain, key_gain]), ((0, 0), (0, LANES - head)))
    order = jnp.arange(4, dtype=jnp.int32) ^ me
    places = jnp.stack([patch_rows[0], patch_columns[0]], axis=1).astype(F32)
    places = jnp.take(places.reshape(4, rows, 2), order, axis=0).reshape(full, 2)
    ends = jnp.cumsum(item_lengths[0])
    share, order, places, ends = sync(share, order, places, ends)
    shares = [share, flip(share, 1), flip(share, 2), flip(share, 3)]
    side = kernel_call(
        functools.partial(setup_kernel, head, items, spans),
        [out for n in sizes for out in (like(5, n, LANES), like(n, LANES))],
        ends, item_condition[0], order, places,
        scalars=3, name="setup", us=3.0, hbm=(0, 2, 4),
    )
    order, expansion, *both = sync(order, expansion, *shares, *side)
    shares, side, pick = both[:4], both[4::2], both[5::2]
    (table,) = kernel_call(
        functools.partial(columns_kernel, 4),
        [like(12, width)],
        order, *[in_hbm(share) for share in shares], offsets,
        scalars=1, name="columns",
    )
    expansion_flat = expansion.reshape(width, 2 * units)
    x_halves = halves(x_one, x_two)
    x_one, x_two, dy, table, expansion_flat, *x_halves = sync(
        x_one, x_two, dy, table, expansion_flat, *x_halves
    )

    x_far = flip(x_halves[0], 2), flip(x_halves[1], 1)
    x_parts = [[x], [x_one, x_two], list(x_far)]

    def enter(k, parts):
        n = sizes[k]
        return kernel_call(
            functools.partial(enter_kernel, head, len(parts)),
            [
                like(n, width, dtype=BF),
                like(n, padded, dtype=BF),
                like(n, padded, dtype=BF),
                like(n, padded, dtype=BF),
                like(n, 2 * part, dtype=BF),
            ],
            *parts, side[k], pick[k], table, gains, inward_rows,
            name="enter", hbm=(0, 1, 4) if k == 0 else (0, 4), us=3.3 * n / rows,
        )

    entered = [None, list(enter(1, x_parts[1]))]
    x_far, dy, entered[1][1], x_own = sync(x_far, dy, entered[1][1], x)
    dy_one, dy_two = flip(dy, 1), flip(dy, 2)
    entered[0] = list(enter(0, [x_own]))
    x_far = list(x_far)
    x_parts[2] = x_far

    entered.append(enter(2, x_far))
    first_in, queries, keys, values, raws = zip(*entered)

    def attend(k, query):
        n = sizes[k]
        return kernel_call(
            functools.partial(forward_kernel, head, 3),
            [like(n, width, dtype=BF), like(n, part, dtype=BF), like(n, padded, dtype=BF)],
            query, *keys, *values, outward_rows,
            name="attend", hbm=(1, 2) if k == 2 else (), us=2.0 * n / rows,
        )

    attended = [None, None, attend(2, queries[2])]
    far, query_near, dy_one, dy_two = sync(attended[2][0], queries[1], dy_one, dy_two)

    got = scatter_first(far)
    attended[1] = attend(1, query_near)
    dy_halves = halves(dy_one, dy_two)
    near, query_own, got, dy_halves = sync(attended[1][0], queries[0], got, dy_halves)

    both, dy_halves = sync(joined(near, got), dy_halves)
    sums = flip(both[0], 1), flip(both[1], 2)
    dy_far = flip(dy_halves[0], 2), flip(dy_halves[1], 1)
    attended[0] = attend(0, query_own)
    own, cond_low, sums, dy_far = sync(attended[0][0], cond_low, sums, dy_far)
    dy_far = list(dy_far)

    attended_own, middle, second = kernel_call(
        middle_kernel,
        [like(rows, width, dtype=BF), like(rows, width), like(rows, width, dtype=BF)],
        x, own, *sums, pick[0], table,
        name="middle", hbm=(0, 1),
    )
    second, cond_low, dy, dy_one, dy_two = sync(second, cond_low, dy, dy_one, dy_two)
    second_one, second_two = flip(second, 1), flip(second, 2)
    dy_parts = [[dy], [dy_one, dy_two], dy_far]
    fed_grad, hidden_grad = [], []
    for k in range(3):
        outs = kernel_call(
            functools.partial(hidden_grad_kernel, len(dy_parts[k])),
            [like(sizes[k], width, dtype=BF), like(sizes[k], units)],
            *dy_parts[k], pick[k], table, contraction,
            name="hidden_grad", us=0.8 * sizes[k] / rows,
        )
        fed_grad.append(outs[0])
        hidden_grad.append(outs[1])
    conds = jnp.transpose(gather_small(cond_low, dp), (1, 0, 2)).reshape(2 * dp, width)
    conds = lax.dynamic_slice_in_dim(conds, dp_me * lanes, lanes, 1).astype(F32)
    second_one, second_two, conds, *hidden_grad = sync(second_one, second_two, conds, *hidden_grad)

    second_far = relay(second_one, second_two)
    second_parts = [[second], [second_one, second_two], list(second_far)]

    def through(k, parts):
        n = sizes[k]
        return kernel_call(
            functools.partial(units_kernel, len(parts)),
            [
                like(n, units, dtype=BF),
                like(n, 2 * units, dtype=BF),
                like(n, width, dtype=BF),
            ],
            *parts, hidden_grad[k], expansion_flat,
            name="units", hbm=() if k == 2 else (2,), us=2.5 * n / rows,
        )

    passed = [through(0, second_parts[0]), through(1, second_parts[1])]
    *second_far, near, own = sync(*second_far, passed[1][2], passed[0][2])
    second_parts[2] = second_far
    passed.append(through(2, second_far))
    hidden, widening, back = zip(*passed)
    far, hidden_far = sync(back[2], hidden[2])

    got = scatter_first(far)
    wide = weights_call(
        [
            (sum(second_parts, []), widening),
            (fed_grad, [*hidden[:2], hidden_far]),
        ],
        dp,
        "wide",
        6.0,
        18,
    )
    wide, near, hidden_far, got = sync(wide, near, hidden_far, got)

    sums = scatter_second(in_hbm(near), got)
    wide = sum_start(wide)
    fed_parts, fed_slots = [None] * 3, [None] * 3
    for k, source in ((1, hidden[1]), (2, hidden_far), (0, hidden[0])):
        if k == 2:
            fed_parts[1], wide, source = sync(fed_parts[1], wide, source)
            wide = sum_merge(wide, "merge")
        if k == 0:
            fed_parts[2], wide, source = sync(fed_parts[2], wide, source)
            wide[3] = swap(wide[3], 2)
        fed_parts[k], fed_slots[k] = kernel_call(
            functools.partial(fed_part_kernel, len(dy_parts[k])),
            [like(sizes[k], width, dtype=BF), like(2, width)],
            *dy_parts[k], source, pick[k], contraction,
            name="fed_part", hbm=(0, 1), us=1.0 * sizes[k] / rows,
        )
    own, sums, fed_parts[0] = sync(own, sums, fed_parts[0])

    middle_grad, send, slots_two = kernel_call(
        middle_back_kernel,
        [like(rows, width), like(rows, width, dtype=BF), like(6, width)],
        own, *sums, middle, attended_own, dy, pick[0], table,
        name="middle_back", hbm=(0, 2), us=1.7,
    )
    send_one, send_two = flip(send, 1), flip(send, 2)

    def attend_back(k, parts, sums):
        n = sizes[k]
        given = (*parts, outward_rows, attended[k][1], attended[k][2], *keys, *values)
        out = kernel_call(
            functools.partial(backward_kernel, head, 3, not sums, len(parts)),
            [like(n, padded)] + [like(a.shape[0], padded) for a in keys + values],
            *given, *sums,
            aliases={len(given) + i: 1 + i for i in range(len(sums))},
            name="attend_back", us=4.3 * n / rows, mib=16,
        )
        return out[0], tuple(out[1:])

    query_grads = [None] * 3
    query_grads[0], totals = attend_back(0, [send], ())
    send_one, send_two, totals, wide = sync(send_one, send_two, totals, wide)

    send_far = relay(send_one, send_two)
    wide[2] = swap(plus(wide[2], wide[3]), 4)
    query_grads[1], totals = attend_back(1, [send_one, send_two], totals)
    send_far, totals, fed_far, wide[1] = sync(send_far, totals, fed_parts[2], wide[1])

    fed_got = scatter_first(fed_far)
    wide[1] = swap(wide[1], 2)
    send_parts = [[send], [send_one, send_two], list(send_far)]
    query_grads[2], totals = attend_back(2, send_far, totals)
    key_grads, value_grads = totals[:3], totals[3:]

    def leave(k, query_grad):
        n = sizes[k]
        return kernel_call(
            functools.partial(leave_kernel, head, len(x_parts[k])),
            [
                like(n, 3 * part, dtype=BF),
                like(n, width, dtype=BF),
                like(4, width),
                like(1, 2 * head),
            ],
            *x_parts[k], query_grad, key_grads[k], value_grads[k], raws[k], side[k], pick[k], gains,
            inward_rows,
            name="leave", hbm=(0, 2, 3), us=3.8 * n / rows,
        )

    left = [None, None, leave(2, query_grads[2])]
    far, query_near, fed_near, fed_got = sync(left[2][1], query_grads[1], fed_parts[1], fed_got)

    got = scatter_first(far)
    left[1] = leave(1, query_near)
    near, query_own, got = sync(left[1][1], query_grads[0], got)

    left[0] = sync(*leave(0, query_own))

    parts = left[0][2], left[1][2], left[2][2], slots_two, *fed_slots
    packed = kernel_call(
        pack_kernel,
        [like(2, 37, part)] * 2,
        order, *[in_hbm(v) for v in (*parts, left[0][3], left[1][3], left[2][3])],
        scalars=1, name="pack", us=1.0,
    )
    packed = packed[0] + flip(packed[1], 1)
    narrow = weights_call(
        [
            (first_in, [left[k][0] for k in range(3)]),
            (sum(send_parts, []), [attended[k][1] for k in range(3)]),
        ],
        dp,
        "narrow",
        0.1,
        16,
    )
    narrow, packed, wide[1], wide[2] = sync(narrow, packed, wide[1], wide[2])

    narrow = sum_start(narrow)
    packed = packed[0] + flip(packed[1], 2)
    narrow, packed, near, got = sync(narrow, packed, near, got)

    narrow = sum_merge(narrow, "merge")
    narrow[3] = swap(narrow[3], 2)
    sums = scatter_second(near, got)
    every = gather_small(packed, dp)
    expansion_gradient, contraction_gradient = spread(
        [2, 1], [like(2, lanes, units), like(1, lanes, units)], wide[:3]
    )
    narrow[1], narrow[2], narrow[3], sums, fed_near, expansion_gradient, every = sync(
        narrow[1], narrow[2], narrow[3], sums, fed_parts[1], expansion_gradient, every
    )

    narrow[2] = swap(plus(narrow[2], narrow[3]), 4)
    narrow[1] = swap(narrow[1], 2)
    fed_sums = scatter_second(in_hbm(fed_near), fed_got)
    (token_gradient,) = kernel_call(
        token_kernel,
        [like(rows, width)],
        left[0][1], *sums, x, middle_grad, pick[0], table,
        name="token", us=8.0,
    )
    (layer_output,) = kernel_call(
        fed_kernel,
        [like(rows, width, dtype=BF)],
        fed_parts[0], *fed_sums, middle, pick[0], table,
        name="fed", us=8,
    )
    expansion_gradient = jnp.transpose(expansion_gradient, (1, 0, 2))
    modulator_gradient, bias_gradient, gain_sum = kernel_call(
        slots_kernel,
        [like(6, lanes, part), like(6, width), like(1, part)],
        conds, every,
        name="slots", us=8.0,
    )
    narrow[0], expansion_gradient, token_gradient, modulator_gradient = sync(
        narrow[0], expansion_gradient, token_gradient, modulator_gradient
    )
    inward_gradient, outward_gradient = spread(
        [3, 1], [like(3, lanes, part), like(1, lanes, part)], narrow[:3]
    )
    return (
        layer_output[None],
        token_gradient[None],
        jnp.transpose(modulator_gradient, (1, 0, 2)),
        bias_gradient,
        jnp.transpose(inward_gradient, (1, 0, 2)),
        gain_sum[0, :head],
        gain_sum[0, head : 2 * head],
        outward_gradient[0],
        expansion_gradient,
        contraction_gradient[0],
    )


def solution(mesh):
    placed = (
        P("dp", "tp", None),
        P("dp", None),
        P(None, None, "tp"),
        P(),
        P(None, None, "tp"),
        P(),
        P(),
        P(None, "tp"),
        P(None, None, "tp"),
        P(None, "tp"),
        P("dp", None),
        P("dp", None),
        P("dp", None),
        P("dp", None),
        P("dp", "tp", None),
    )
    return jax.shard_map(
        shards,
        mesh=mesh,
        in_specs=placed,
        out_specs=(
            P("dp", "tp", None),
            P("dp", "tp", None),
            P("dp", None, "tp"),
            P(),
            P("dp", None, "tp"),
            P(),
            P(),
            P("dp", "tp"),
            P("dp", None, "tp"),
            P("dp", "tp"),
        ),
        check_vma=False,
    )
```

```python
import functools
import math

import jax
import jax.numpy as jnp
from jax import lax
from jax.experimental import pallas as pl
from jax.experimental.pallas import tpu as pltpu
from jax.sharding import PartitionSpec as P

BF = jnp.bfloat16
F32 = jnp.float32
LANES = 128
EPS = 1e-06
NN = ((1,), (0,))
NT = ((1,), (1,))
TN = ((0,), (0,))
MASKED = -30000.0


def dot(left, right, dims):
    return lax.dot_general(left, right, (dims, ((), ())), preferred_element_type=F32)


def flip(value, by):
    return lax.ppermute(value, "tp", [(i, i ^ by) for i in range(4)])


def halves(one, two):
    half = one.shape[0] // 2
    return one[:half], two[half:]


def relay(one, two):
    low, high = halves(one, two)
    return flip(low, 2), flip(high, 1)


def scatter_first(far):
    half = far.shape[0] // 2
    return flip(far[:half], 1), flip(far[half:], 2)


def total(*refs):
    return sum(ref[...].astype(F32) for ref in refs)


def join_kernel(near_ref, via_one_ref, via_two_ref, one_ref, two_ref):
    rows = one_ref.shape[0]
    half = rows // 2
    one_ref[:half, :] = near_ref[:half, :]
    one_ref[half:, :] = near_ref[half:rows, :] + via_two_ref[...]
    two_ref[:half, :] = near_ref[rows : rows + half, :] + via_one_ref[...]
    two_ref[half:, :] = near_ref[rows + half :, :]


def joined(near, got):
    out = like(near.shape[0] // 2, near.shape[1], dtype=near.dtype)
    return kernel_call(join_kernel, [out, out], near, *got, name="join")


def scatter_second(near, got):
    one, two = joined(near, got)
    return flip(one, 1), flip(two, 2)


def gather_core(own, dp):
    return jnp.stack([own, swap(own, 1)]) if dp == 8 else own


def gather_chips(pair, dp):
    if dp != 8:
        return lax.all_gather(pair, "dp", axis=0)
    four = jnp.concatenate([pair, swap(pair, 2)], axis=0)
    return jnp.concatenate([four, swap(four, 4)], axis=0)


def gather_small(own, dp):
    return gather_chips(gather_core(own, dp), dp)


def pack_kernel(order_ref, *refs):
    first, two_ref, fed, gains, out_refs = refs[:3], refs[3], refs[4:7], refs[7:10], refs[10:]
    cut = out_refs[0].shape[-1]
    tall = jnp.concatenate([total(*first), two_ref[...], total(*fed)], axis=0)
    gain = total(*gains)
    gain = jnp.concatenate([gain, jnp.zeros((1, cut - gain.shape[1]), F32)], axis=1)
    parts = [tall[:, j * cut : (j + 1) * cut] for j in range(4)]
    bias = []
    for part in parts:
        bias += [part[2 * j : 2 * j + 1] + part[2 * j + 1 : 2 * j + 2] for j in range(6)]
    below = jnp.concatenate([gain, *bias], axis=0)
    for k in range(4):
        part = parts[0]
        for j in range(1, 4):
            part = jnp.where(order_ref[k] == j, parts[j], part)
        out_refs[k % 2][k // 2] = jnp.concatenate([part, below], axis=0)


def slots_kernel(conds_ref, every_ref, grad_ref, bias_ref, gain_ref):
    conds = conds_ref[...]
    cut = every_ref.shape[2]
    gain_ref[...] = jnp.sum(every_ref[:, 12, :], axis=0, keepdims=True)
    for j in range(6):
        both = [every_ref[:, 2 * j + c, :] for c in range(2)]
        grad_ref[j] = lax.dot_general(
            conds,
            jnp.concatenate(both, axis=0),
            (TN, ((), ())),
            precision=lax.Precision.HIGHEST,
            preferred_element_type=F32,
        )
        for q in range(4):
            own = every_ref[:, 13 + 6 * q + j, :]
            bias_ref[j : j + 1, q * cut : (q + 1) * cut] = jnp.sum(own, axis=0, keepdims=True)


def columns_kernel(pieces, order_ref, *refs):
    add_ref, out_ref = refs[pieces:]
    stacked = jnp.stack([ref[...] for ref in refs[:pieces]])
    parts = []
    for j in range(pieces):
        part = stacked[0]
        for k in range(1, pieces):
            part = jnp.where(order_ref[j] == k, stacked[k], part)
        parts.append(part)
    out = jnp.concatenate(parts, axis=1)
    add = add_ref[...]
    if add.shape[0] < out.shape[0]:
        add = jnp.concatenate([add, add], axis=0)
    out_ref[...] = out + add


def gather_tp_columns(own, add):
    order = jnp.arange(4, dtype=jnp.int32) ^ lax.axis_index("tp")
    (out,) = kernel_call(
        functools.partial(columns_kernel, 4),
        [like(own.shape[0], 4 * own.shape[1])],
        order, own, flip(own, 1), flip(own, 2), flip(own, 3), add,
        scalars=1,
        name="columns",
    )
    return out


def kernel_call(body, outs, *args, aliases=None, name=None, scalars=0, us=1.0, mib=16, hbm=()):
    spec = pl.BlockSpec(memory_space=pltpu.VMEM)
    given = [pl.BlockSpec(memory_space=pltpu.SMEM)] * scalars + [spec] * (len(args) - scalars)
    return pl.pallas_call(
        body,
        out_shape=[pltpu.HBM(o.shape, o.dtype) if i in hbm else o for i, o in enumerate(outs)],
        in_specs=given,
        out_specs=[spec] * len(outs),
        input_output_aliases=aliases or {},
        compiler_params=pltpu.CompilerParams(vmem_limit_bytes=mib * 1024 * 1024),
        cost_estimate=pl.CostEstimate(flops=int(us * 1.15e9), bytes_accessed=1, transcendentals=0),
        name=name,
    )(*args)


def like(*shape, dtype=F32):
    return jax.ShapeDtypeStruct(shape, dtype)


def norm(values):
    count = values.shape[-1]
    center = values - jnp.sum(values, axis=-1, keepdims=True) * (1.0 / count)
    inverse = lax.rsqrt(jnp.sum(center * center, axis=-1, keepdims=True) * (1.0 / count) + EPS)
    return center * inverse, inverse


def norm_back(grad, normed, inverse):
    count = grad.shape[-1]
    middle = jnp.sum(grad, axis=-1, keepdims=True) * (1.0 / count)
    slope = jnp.sum(grad * normed, axis=-1, keepdims=True) * (1.0 / count)
    return inverse * (grad - middle - normed * slope)


def choose(pick, table_ref, column):
    return jnp.where(pick, table_ref[6 + column : 7 + column, :], table_ref[column : column + 1, :])


def slot_sums(pick, values):
    zero = jnp.zeros_like(values)
    return [
        jnp.sum(jnp.where(pick, zero, values), axis=0, keepdims=True),
        jnp.sum(jnp.where(pick, values, zero), axis=0, keepdims=True),
    ]


def picks(pick_ref, width):
    return jnp.broadcast_to(pick_ref[:, 0:1], (pick_ref.shape[0], width)) > 0.5


def lane_sums(values):
    ones = jnp.ones((values.shape[1], values.shape[1]), BF)
    high = values.astype(BF)
    low = (values - high.astype(F32)).astype(BF)
    return dot(high, ones, NN) + dot(low, ones, NN)


def widen(values):
    return jnp.concatenate(
        [values, jnp.zeros((values.shape[0], LANES - values.shape[1]), values.dtype)], axis=1
    )


def stack_rows(refs):
    return refs[0][...] if len(refs) == 1 else jnp.concatenate([ref[...] for ref in refs], axis=0)


def setup_kernel(head, items, spans, ends_ref, conds_ref, order_ref, places_ref, *out_refs):
    rows = places_ref.shape[0] // 4
    quarter = head // 4
    for s, (low, high) in enumerate(spans):
        count = high - low
        shape = (count, LANES)
        lane = lax.broadcasted_iota(jnp.int32, shape, 1)
        row = lax.broadcasted_iota(jnp.int32, shape, 0)
        start = jnp.full(shape, order_ref[low // rows] * rows, jnp.int32)
        if count > rows:
            start = jnp.where(row >= rows, order_ref[low // rows + 1] * rows - rows, start)
        token = start + row
        owner = jnp.zeros(shape, jnp.int32)
        for j in range(items):
            owner = owner + (token >= ends_ref[j]).astype(jnp.int32)
        pick = jnp.zeros(shape, jnp.int32)
        for j in range(items):
            pick = jnp.where(owner == j, conds_ref[j], pick)
        place = jnp.where(
            lane < 2 * quarter,
            jnp.broadcast_to(places_ref[low:high, 0:1], shape),
            jnp.broadcast_to(places_ref[low:high, 1:2], shape),
        )
        phase = lane
        for j in range(1, 4):
            phase = jnp.where(lane >= j * quarter, lane - j * quarter, phase)
        angles = place * jnp.exp(phase.astype(F32) * (-math.log(10000.0) / quarter))
        real = lane < head
        sine = jnp.sin(angles)
        lower = (lane < quarter) | ((lane >= 2 * quarter) & (lane < 3 * quarter))
        zero = jnp.zeros(shape, F32)
        out_ref, pick_ref = out_refs[2 * s : 2 * s + 2]
        out_ref[0] = jnp.where(real, jnp.cos(angles), zero)
        out_ref[1] = jnp.where(real & lower, -sine, zero)
        out_ref[2] = jnp.where(real & ~lower, sine, zero)
        base = head + 8
        mine = jnp.where(lane == owner + base, 1.0, 0.0)
        out_ref[3] = mine
        marks = jnp.where((lane >= head + 4) & (lane < head + 7), 1.0, zero)
        slots = (lane >= base) & (lane < base + items)
        out_ref[4] = jnp.where(slots, MASKED * (1.0 - mine), marks)
        pick_ref[...] = pick.astype(F32)


def enter_kernel(head, count, *refs):
    x = stack_rows(refs[:count])
    side_ref, pick_ref, table_ref, gain_ref, weight_ref = refs[count : count + 5]
    first_ref, query_ref, key_ref, value_ref, raw_ref = refs[count + 5 :]
    rows, width = x.shape
    part = weight_ref.shape[0] // 3
    heads = part // head
    pick = picks(pick_ref, width)
    normed, _ = norm(x.astype(F32))
    low = (normed * (1.0 + choose(pick, table_ref, 1)) + choose(pick, table_ref, 0)).astype(BF)
    first_ref[...] = low
    raw = dot(low, weight_ref[...], NT)
    raw_ref[...] = raw[:, : 2 * part].astype(BF)
    cosine, near, far = side_ref[0], side_ref[1], side_ref[2]
    scale = math.log2(math.e) / math.sqrt(head)
    for kind in range(2):
        gain = gain_ref[kind : kind + 1, :]
        if kind == 0:
            gain = gain * scale
        target = (query_ref, key_ref)[kind]
        for h in range(heads):
            at = kind * part + h * head
            own = widen(raw[:, at : at + head])
            inverse = lax.rsqrt(lane_sums(own * own) * (1.0 / head) + EPS)
            own = own * inverse * gain
            turned = (
                own * cosine
                + pltpu.roll(own, LANES - head // 4, 1) * near
                + pltpu.roll(own, head // 4, 1) * far
            )
            target[:, pl.ds(h * LANES, LANES)] = (turned + side_ref[3 + kind]).astype(BF)
    lane = lax.broadcasted_iota(jnp.int32, (rows, LANES), 1)
    ones = ((lane >= head) & (lane < head + 3)).astype(F32)
    for h in range(heads):
        at = 2 * part + h * head
        value_ref[:, pl.ds(h * LANES, LANES)] = (widen(raw[:, at : at + head]) + ones).astype(BF)


def split_three(value):
    one = value.astype(BF).astype(F32)
    rest = value - one
    two = rest.astype(BF).astype(F32)
    return one, two, rest - two


def forward_kernel(head, pieces, query_ref, *refs):
    keys, values = refs[:pieces], refs[pieces : 2 * pieces]
    outward_ref, partial_ref, mixed_ref, again_ref = refs[2 * pieces :]
    rows = query_ref.shape[0]
    heads = query_ref.shape[1] // LANES
    lane = lax.broadcasted_iota(jnp.int32, (rows, LANES), 1)
    mixed = []
    for h in range(heads):
        place = pl.ds(h * LANES, LANES)
        query = query_ref[:, place]
        out = None
        for key_ref, value_ref in zip(keys, values):
            weights = jnp.exp2(dot(query, key_ref[:, place], NT)).astype(BF)
            term = dot(weights, value_ref[:, place], NN)
            out = term if out is None else out + term
        total = out[:, head : head + 1]
        mixed.append((out[:, :head] * (1.0 / total)).astype(BF))
        one, two, three = split_three(-jnp.log2(total))
        marks = jnp.where(lane == head + 4, one, 0.0)
        marks = jnp.where(lane == head + 5, two, marks)
        marks = jnp.where(lane == head + 6, three, marks)
        again_ref[:, place] = (query.astype(F32) + marks).astype(BF)
    mixed = jnp.concatenate(mixed, axis=1)
    mixed_ref[...] = mixed
    partial_ref[...] = dot(mixed, outward_ref[...], NN).astype(partial_ref.dtype)


def backward_kernel(head, pieces, first, count, *refs):
    sent = stack_rows(refs[:count])
    outward_ref, mixed_ref, query_ref = refs[count : count + 3]
    refs = refs[count + 3 :]
    keys, values = refs[:pieces], refs[pieces : 2 * pieces]
    refs = refs[2 * pieces :]
    if not first:
        key_in, value_in = refs[:pieces], refs[pieces : 2 * pieces]
        refs = refs[2 * pieces :]
    query_out = refs[0]
    key_out, value_out = refs[1 : 1 + pieces], refs[1 + pieces :]
    rows = query_ref.shape[0]
    heads = query_ref.shape[1] // LANES
    lane = lax.broadcasted_iota(jnp.int32, (rows, LANES), 1)
    grads = dot(sent, outward_ref[...], NT).astype(BF).astype(F32)
    mixed = mixed_ref[...].astype(F32)
    for h in range(heads):
        place = pl.ds(h * LANES, LANES)
        cut = slice(h * head, (h + 1) * head)
        grad = grads[:, cut]
        centre = jnp.sum(grad * mixed[:, cut], axis=-1, keepdims=True)
        one, two, three = split_three(-centre)
        grad = widen(grad)
        grad = jnp.where(lane == head, one, grad)
        grad = jnp.where(lane == head + 1, two, grad)
        grad = jnp.where(lane == head + 2, three, grad).astype(BF)
        query = query_ref[:, place]
        query_grad = None
        for j in range(pieces):
            key, value = keys[j][:, place], values[j][:, place]
            weights = jnp.exp2(dot(key, query, NT))
            score_grad = (weights * dot(value, grad, NT)).astype(BF)
            value_grad = dot(weights.astype(BF), grad, NN)
            key_grad = dot(score_grad, query, NN)
            if not first:
                value_grad += value_in[j][:, place]
                key_grad += key_in[j][:, place]
            value_out[j][:, place] = value_grad
            key_out[j][:, place] = key_grad
            term = dot(key, score_grad, TN)
            query_grad = term if query_grad is None else query_grad + term
        query_out[:, place] = query_grad.T


def leave_kernel(head, count, *refs):
    x = stack_rows(refs[:count])
    query_grad_ref, key_grad_ref, value_grad_ref, raw_ref, side_ref, pick_ref = refs[count : count + 6]
    gain_ref, weight_ref, projected_ref, partial_ref, slots_ref, gains_ref = refs[count + 6 :]
    rows, width = x.shape
    part = weight_ref.shape[0] // 3
    heads = part // head
    cosine, near, far = side_ref[0], side_ref[1], side_ref[2]
    raw = raw_ref[...].astype(F32)
    pieces = []
    gain_grads = []
    for kind in range(2):
        gain = gain_ref[kind : kind + 1, :]
        source = (query_grad_ref, key_grad_ref)[kind]
        scale = (1.0 / math.sqrt(head), math.log(2.0))[kind]
        gain_grad = None
        for h in range(heads):
            grad = source[:, pl.ds(h * LANES, LANES)] * scale
            grad = (
                grad * cosine
                + pltpu.roll(grad * near, head // 4, 1)
                + pltpu.roll(grad * far, LANES - head // 4, 1)
            )
            at = kind * part + h * head
            own = widen(raw[:, at : at + head])
            inverse = lax.rsqrt(lane_sums(own * own) * (1.0 / head) + EPS)
            own = own * inverse
            term = grad * own
            gain_grad = term if gain_grad is None else gain_grad + term
            slope = lane_sums(term * gain) * (1.0 / head)
            pieces.append((inverse * (grad * gain - own * slope))[:, :head].astype(BF))
        gain_grad = jnp.sum(gain_grad, axis=0, keepdims=True)
        gain_grads.append(gain_grad[:, :head])
    gains_ref[...] = jnp.concatenate(gain_grads, axis=1)
    for h in range(heads):
        pieces.append(value_grad_ref[:, pl.ds(h * LANES, head)].astype(BF))
    projected = jnp.concatenate(pieces, axis=1)
    projected_ref[...] = projected
    grad = dot(projected, weight_ref[...], NN)
    partial_ref[...] = grad.astype(partial_ref.dtype)
    pick = picks(pick_ref, width)
    normed, _ = norm(x.astype(F32))
    slots_ref[...] = jnp.concatenate(slot_sums(pick, grad) + slot_sums(pick, grad * normed), axis=0)


def middle_kernel(x_ref, own_ref, one_ref, two_ref, side_ref, table_ref,
                  attended_ref, middle_ref, second_ref):
    attended = total(own_ref, one_ref, two_ref)
    attended_ref[...] = attended.astype(BF)
    pick = picks(side_ref, x_ref.shape[1])
    middle = x_ref[...].astype(F32) + choose(pick, table_ref, 2) * attended
    middle_ref[...] = middle
    normed, _ = norm(middle)
    second_ref[...] = (
        normed * (1.0 + choose(pick, table_ref, 4)) + choose(pick, table_ref, 3)
    ).astype(BF)


def units_kernel(count, *refs):
    second = stack_rows(refs[:count])
    grad_ref, weight_ref, hidden_ref, widening_ref, partial_ref = refs[count:]
    units = grad_ref.shape[1]
    both = dot(second, weight_ref[...], NN)
    gate, up = both[:, :units], both[:, units:]
    sigmoid = 1.0 / (1.0 + jnp.exp(-gate))
    active = gate * sigmoid
    hidden_ref[...] = (active * up).astype(BF)
    grad = grad_ref[...]
    gate_grad = (grad * up * (sigmoid + active * (1.0 - sigmoid))).astype(BF)
    widening = jnp.concatenate([gate_grad, (grad * active).astype(BF)], axis=1)
    widening_ref[...] = widening
    partial_ref[...] = dot(widening, weight_ref[...], NT).astype(partial_ref.dtype)


def hidden_grad_kernel(count, *refs):
    dy = stack_rows(refs[:count])
    side_ref, table_ref, weight_ref, fed_ref, out_ref = refs[count:]
    pick = picks(side_ref, dy.shape[1])
    fed = (choose(pick, table_ref, 5) * dy.astype(F32)).astype(BF)
    fed_ref[...] = fed
    out_ref[...] = dot(fed, weight_ref[...], NN)


def fed_part_kernel(count, *refs):
    dy = stack_rows(refs[:count])
    hidden_ref, side_ref, weight_ref, out_ref, slots_ref = refs[count:]
    fed = dot(hidden_ref[...], weight_ref[...], NT)
    out_ref[...] = fed.astype(BF)
    slots_ref[...] = jnp.concatenate(
        slot_sums(picks(side_ref, dy.shape[1]), dy.astype(F32) * fed), axis=0
    )


def weights_kernel(counts, cuts, core_ref, *refs):
    *refs, room_ref, sems = refs
    pairs = []
    for lefts, rights in counts:
        pairs.append((refs[:lefts], stack_rows(refs[lefts : lefts + rights])))
        refs = refs[lefts + rights :]
    outs = refs
    height = room_ref.shape[0]
    blocks = len(outs) * outs[0].shape[0]
    size = height // blocks
    copies = []
    step = height // cuts
    for low in range(0, height, step):
        at = 0
        for lefts, right in pairs:
            left = [ref[:, low : low + step] for ref in lefts]
            left = left[0] if len(left) == 1 else jnp.concatenate(left, axis=0)
            high = at + right.shape[1]
            room_ref[low : low + step, at:high] = dot(left, right, TN).astype(BF)
            at = high
        while len(copies) < blocks and (len(copies) + 1) * size <= low + step:
            j = len(copies)
            rows = room_ref.at[j * size : (j + 1) * size, :]
            to = [pltpu.make_async_copy(rows, out.at[j // len(outs)], sems.at[j]) for out in outs]
            if len(outs) == 1:
                to[0].start()
            else:

                @pl.when(core_ref[0] == j % 2)
                def _(copy=to[0]):
                    copy.start()

                @pl.when(core_ref[0] != j % 2)
                def _(copy=to[1]):
                    copy.start()

            copies.append(to[0])
    for copy in copies:
        copy.wait()


def weights_call(pairs, dp, name, us, mib):
    args, counts = [], []
    for lefts, rights in pairs:
        args += [*lefts, *rights]
        counts.append((len(lefts), len(rights)))
    height = pairs[0][0][0].shape[1]
    wide = sum(rights[0].shape[1] for _, rights in pairs)
    outs = 2 if dp == 8 else 1
    blocks = dp if outs == 2 else 1
    return pl.pallas_call(
        functools.partial(weights_kernel, counts, 3),
        out_shape=[pltpu.HBM((blocks // outs, height // blocks, wide), BF)] * outs,
        in_specs=[pl.BlockSpec(memory_space=pltpu.SMEM)]
        + [pl.BlockSpec(memory_space=pltpu.VMEM)] * len(args),
        out_specs=[pl.BlockSpec(memory_space=pltpu.HBM)] * outs,
        scratch_shapes=[pltpu.VMEM((height, wide), BF), pltpu.SemaphoreType.DMA((blocks,))],
        compiler_params=pltpu.CompilerParams(vmem_limit_bytes=mib * 1024 * 1024),
        cost_estimate=pl.CostEstimate(flops=int(us * 1.15e9), bytes_accessed=1, transcendentals=0),
        name=name,
    )((lax.axis_index("dp") % 2).reshape(1).astype(jnp.int32), *args)


def swap(value, by):
    return None if value is None else lax.ppermute(value, "dp", [(i, i ^ by) for i in range(8)])


def merge_kernel(place_ref, keep_ref, got_ref, *out_refs):
    for k, ref in enumerate(out_refs):
        at = place_ref[0] ^ k
        ref[...] = keep_ref[at] + got_ref[at]


def sum_start(outs):
    if len(outs) == 1:
        total_sum = lax.psum_scatter(outs[0][0], "dp", scatter_dimension=0, tiled=True)
        return [total_sum, None, None, None]
    return [outs[0], swap(outs[1], 1), None, None]


def sum_merge(parts, name):
    if parts[1] is None:
        return parts
    _, size, wide = parts[0].shape
    place = (lax.axis_index("dp") // 2).reshape(1).astype(jnp.int32)
    outs = kernel_call(
        merge_kernel,
        [like(size, wide, dtype=BF)] * 4,
        place, in_hbm(parts[0]), parts[1],
        scalars=1, name=name, us=3.0, hbm=(0,),
    )
    return list(outs)


def plus(left, right):
    return None if left is None else left + right


def spread(groups, outs, parts):
    parts = [part for part in parts if part is not None]
    return kernel_call(
        functools.partial(spread_kernel, groups, len(parts)), outs, *parts, name="spread"
    )


def in_hbm(value):
    return pltpu.with_memory_space_constraint(value, pltpu.HBM)


def middle_back_kernel(own_ref, one_ref, two_ref, middle_ref, attended_ref, dy_ref, side_ref, table_ref,
                       grad_ref, send_ref, slots_ref):
    pick = picks(side_ref, dy_ref.shape[1])
    second_grad = total(own_ref, one_ref, two_ref)
    normed, inverse = norm(middle_ref[...])
    grad = dy_ref[...].astype(F32) + norm_back(
        second_grad * (1.0 + choose(pick, table_ref, 4)), normed, inverse
    )
    grad_ref[...] = grad
    send_ref[...] = (choose(pick, table_ref, 2) * grad).astype(BF)
    slots_ref[...] = jnp.concatenate(
        slot_sums(pick, grad * attended_ref[...].astype(F32))
        + slot_sums(pick, second_grad)
        + slot_sums(pick, second_grad * normed),
        axis=0,
    )


def fed_kernel(own_ref, one_ref, two_ref, middle_ref, side_ref, table_ref, out_ref):
    pick = picks(side_ref, middle_ref.shape[1])
    fed = total(own_ref, one_ref, two_ref)
    out_ref[...] = (middle_ref[...] + choose(pick, table_ref, 5) * fed).astype(BF)


def spread_kernel(groups, count, *refs):
    parts, out_refs = refs[:count], refs[count:]
    at = 0
    for group, ref in zip(groups, out_refs):
        width = ref.shape[-1]
        for j in range(group):
            ref[j] = total(*[part.at[:, at : at + width] for part in parts])
            at += width


def last_kernel(groups, count, *refs):
    outs = len(groups)
    spread_kernel(groups, count, *refs[:count], *refs[count + 6 : count + 6 + outs])
    fed_kernel(*refs[count : count + 6], refs[-1])


def token_kernel(own_ref, one_ref, two_ref, x_ref, grad_ref, side_ref, table_ref, out_ref):
    pick = picks(side_ref, x_ref.shape[1])
    first_grad = total(own_ref, one_ref, two_ref)
    normed, inverse = norm(x_ref[...].astype(F32))
    out_ref[...] = grad_ref[...] + norm_back(
        first_grad * (1.0 + choose(pick, table_ref, 1)), normed, inverse
    )


def sync(*values):
    return lax.optimization_barrier(values)


def shards(
    tokens,
    condition,
    modulator,
    offsets,
    inward,
    query_gain,
    key_gain,
    outward,
    expansion,
    contraction,
    item_lengths,
    item_condition,
    patch_rows,
    patch_columns,
    cotangent,
):
    _, rows, width = tokens.shape
    full = patch_rows.shape[1]
    head = query_gain.shape[0]
    part = inward.shape[2]
    heads = part // head
    units = contraction.shape[1]
    items = item_lengths.shape[1]
    dp = lax.axis_size("dp")
    me = lax.axis_index("tp")
    dp_me = lax.axis_index("dp")
    lanes = width // dp
    padded = heads * LANES
    spans = ((0, rows), (rows, 3 * rows), (3 * rows, full))
    sizes = [high - low for low, high in spans]

    x, dy = tokens[0], cotangent[0]
    x_one, x_two = flip(x, 1), flip(x, 2)
    cond_low = jax.nn.silu(condition.astype(F32)).astype(BF)
    share = dot(cond_low, jnp.transpose(modulator, (1, 2, 0)).reshape(-1, width), NT)
    share = share.reshape(12, part)
    inward_rows = jnp.transpose(inward, (1, 2, 0)).reshape(3 * part, width)
    outward_rows = outward.T
    gains = jnp.pad(jnp.stack([query_gain, key_gain]), ((0, 0), (0, LANES - head)))
    order = jnp.arange(4, dtype=jnp.int32) ^ me
    places = jnp.stack([patch_rows[0], patch_columns[0]], axis=1).astype(F32)
    places = jnp.take(places.reshape(4, rows, 2), order, axis=0).reshape(full, 2)
    ends = jnp.cumsum(item_lengths[0])
    share, order, places, ends = sync(share, order, places, ends)
    shares = [share, flip(share, 1), flip(share, 2), flip(share, 3)]
    side = kernel_call(
        functools.partial(setup_kernel, head, items, spans),
        [out for n in sizes for out in (like(5, n, LANES), like(n, LANES))],
        ends, item_condition[0], order, places,
        scalars=3, name="setup", us=3.0, hbm=(0, 2, 4),
    )
    order, *both = sync(order, *shares, *side)
    shares, side, pick = both[:4], both[4::2], both[5::2]
    (table,) = kernel_call(
        functools.partial(columns_kernel, 4),
        [like(12, width)],
        order, *[in_hbm(share) for share in shares], offsets,
        scalars=1, name="columns",
    )
    x_halves = halves(x_one, x_two)
    x_one, x_two, dy, table, *x_halves = sync(x_one, x_two, dy, table, *x_halves)

    x_far = flip(x_halves[0], 2), flip(x_halves[1], 1)
    x_parts = [[x], [x_one, x_two], list(x_far)]

    def enter(k, parts):
        n = sizes[k]
        return kernel_call(
            functools.partial(enter_kernel, head, len(parts)),
            [
                like(n, width, dtype=BF),
                like(n, padded, dtype=BF),
                like(n, padded, dtype=BF),
                like(n, padded, dtype=BF),
                like(n, 2 * part, dtype=BF),
            ],
            *parts, side[k], pick[k], table, gains, inward_rows,
            name="enter", hbm=(0, 1, 4) if k == 0 else (0, 4), us=3.3 * n / rows,
        )

    entered = [None, list(enter(1, x_parts[1]))]
    x_far, dy, entered[1][1], x_own = sync(x_far, dy, entered[1][1], x)
    dy_one, dy_two = flip(dy, 1), flip(dy, 2)
    entered[0] = list(enter(0, [x_own]))
    x_far = list(x_far)
    x_parts[2] = x_far

    entered.append(enter(2, x_far))
    first_in, queries, keys, values, raws = zip(*entered)

    def attend(k, query):
        n = sizes[k]
        return kernel_call(
            functools.partial(forward_kernel, head, 3),
            [like(n, width, dtype=BF), like(n, part, dtype=BF), like(n, padded, dtype=BF)],
            query, *keys, *values, outward_rows,
            name="attend", hbm=(1, 2) if k == 2 else (), us=2.0 * n / rows,
        )

    attended = [None, None, attend(2, queries[2])]
    far, query_near = sync(attended[2][0], queries[1])

    got = scatter_first(far)
    attended[1] = attend(1, query_near)
    near, query_own, dy_one, dy_two = sync(attended[1][0], queries[0], dy_one, dy_two)
    dy_halves = halves(dy_one, dy_two)
    near, query_own, got, dy_halves = sync(near, query_own, got, dy_halves)

    sums = scatter_second(near, got)
    attended[0] = attend(0, query_own)
    own, dy_halves, expansion = sync(attended[0][0], dy_halves, expansion)
    expansion_flat = expansion.reshape(width, 2 * units)
    dy_far = [flip(dy_halves[0], 2), flip(dy_halves[1], 1)]
    own, cond_low, sums, dy_far, expansion_flat = sync(own, cond_low, sums, dy_far, expansion_flat)

    attended_own, middle, second = kernel_call(
        middle_kernel,
        [like(rows, width, dtype=BF), like(rows, width), like(rows, width, dtype=BF)],
        x, own, *sums, pick[0], table,
        name="middle", hbm=(0, 1),
    )
    second, cond_low, dy, dy_one, dy_two = sync(second, cond_low, dy, dy_one, dy_two)
    second_one, second_two = flip(second, 1), flip(second, 2)
    dy_parts = [[dy], [dy_one, dy_two], dy_far]
    fed_grad, hidden_grad = [], []
    for k in range(3):
        outs = kernel_call(
            functools.partial(hidden_grad_kernel, len(dy_parts[k])),
            [like(sizes[k], width, dtype=BF), like(sizes[k], units)],
            *dy_parts[k], pick[k], table, contraction,
            name="hidden_grad", us=0.8 * sizes[k] / rows,
        )
        fed_grad.append(outs[0])
        hidden_grad.append(outs[1])
    conds = jnp.transpose(gather_small(cond_low, dp), (1, 0, 2)).reshape(2 * dp, width)
    conds = lax.dynamic_slice_in_dim(conds, dp_me * lanes, lanes, 1).astype(F32)
    second_one, second_two, conds, *hidden_grad = sync(second_one, second_two, conds, *hidden_grad)

    second_far = relay(second_one, second_two)
    second_parts = [[second], [second_one, second_two], list(second_far)]

    def through(k, parts):
        n = sizes[k]
        return kernel_call(
            functools.partial(units_kernel, len(parts)),
            [
                like(n, units, dtype=BF),
                like(n, 2 * units, dtype=BF),
                like(n, width, dtype=BF),
            ],
            *parts, hidden_grad[k], expansion_flat,
            name="units", hbm=() if k == 2 else (2,), us=2.5 * n / rows,
        )

    passed = [through(0, second_parts[0]), through(1, second_parts[1])]
    *second_far, near, own = sync(*second_far, passed[1][2], passed[0][2])
    second_parts[2] = second_far
    passed.append(through(2, second_far))
    hidden, widening, back = zip(*passed)
    far, hidden_far = sync(back[2], hidden[2])

    got = scatter_first(far)
    wide = weights_call(
        [
            (sum(second_parts, []), widening),
            (fed_grad, [*hidden[:2], hidden_far]),
        ],
        dp,
        "wide",
        6.0,
        18,
    )
    wide, near, hidden_far, got = sync(wide, near, hidden_far, got)

    sums = scatter_second(in_hbm(near), [in_hbm(g) for g in got])
    wide = sum_start(wide)
    fed_parts, fed_slots = [None] * 3, [None] * 3
    for k, source in ((1, hidden[1]), (2, hidden_far), (0, hidden[0])):
        if k == 2:
            fed_parts[1], wide, source = sync(fed_parts[1], wide, source)
            wide = sum_merge(wide, "merge")
        if k == 0:
            fed_parts[2], wide, source = sync(fed_parts[2], wide, source)
            wide[3] = swap(wide[3], 2)
        fed_parts[k], fed_slots[k] = kernel_call(
            functools.partial(fed_part_kernel, len(dy_parts[k])),
            [like(sizes[k], width, dtype=BF), like(2, width)],
            *dy_parts[k], source, pick[k], contraction,
            name="fed_part", hbm=(0, 1), us=1.0 * sizes[k] / rows,
        )
    own, sums, fed_parts[0] = sync(own, sums, fed_parts[0])

    middle_grad, send, slots_two = kernel_call(
        middle_back_kernel,
        [like(rows, width), like(rows, width, dtype=BF), like(6, width)],
        own, *sums, middle, attended_own, dy, pick[0], table,
        name="middle_back", hbm=(0, 2), us=1.7,
    )
    send_one, send_two = flip(send, 1), flip(send, 2)

    def attend_back(k, parts, sums):
        n = sizes[k]
        given = (*parts, outward_rows, attended[k][1], attended[k][2], *keys, *values)
        out = kernel_call(
            functools.partial(backward_kernel, head, 3, not sums, len(parts)),
            [like(n, padded)] + [like(a.shape[0], padded) for a in keys + values],
            *given, *sums,
            aliases={len(given) + i: 1 + i for i in range(len(sums))},
            name="attend_back", us=4.3 * n / rows, mib=16,
        )
        return out[0], tuple(out[1:])

    query_grads = [None] * 3
    query_grads[0], totals = attend_back(0, [send], ())
    totals, wide = sync(totals, wide)
    wide[2] = swap(plus(wide[2], wide[3]), 4)
    send_one, send_two, totals = sync(send_one, send_two, totals)

    send_far = relay(send_one, send_two)
    query_grads[1], totals = attend_back(1, [send_one, send_two], totals)
    send_far, totals, fed_far, wide[1] = sync(send_far, totals, fed_parts[2], wide[1])

    fed_got = scatter_first(fed_far)
    wide[1] = swap(wide[1], 2)
    send_parts = [[send], [send_one, send_two], list(send_far)]
    query_grads[2], totals = attend_back(2, send_far, totals)
    key_grads, value_grads = totals[:3], totals[3:]

    def leave(k, query_grad):
        n = sizes[k]
        return kernel_call(
            functools.partial(leave_kernel, head, len(x_parts[k])),
            [
                like(n, 3 * part, dtype=BF),
                like(n, width, dtype=BF),
                like(4, width),
                like(1, 2 * head),
            ],
            *x_parts[k], query_grad, key_grads[k], value_grads[k], raws[k], side[k], pick[k], gains,
            inward_rows,
            name="leave", hbm=(0, 2, 3), us=3.8 * n / rows,
        )

    left = [None, None, leave(2, query_grads[2])]
    far, query_near, fed_near, fed_got = sync(left[2][1], query_grads[1], fed_parts[1], fed_got)

    got = scatter_first(far)
    left[1] = leave(1, query_near)
    near, query_own, got = sync(left[1][1], query_grads[0], got)

    left[0] = sync(*leave(0, query_own))

    parts = left[0][2], left[1][2], left[2][2], slots_two, *fed_slots
    packed = kernel_call(
        pack_kernel,
        [like(2, 37, part)] * 2,
        order, *[in_hbm(v) for v in (*parts, left[0][3], left[1][3], left[2][3])],
        scalars=1, name="pack", us=1.0,
    )
    packed = packed[0] + flip(packed[1], 1)
    narrow = weights_call(
        [
            (first_in, [left[k][0] for k in range(3)]),
            (sum(send_parts, []), [attended[k][1] for k in range(3)]),
        ],
        dp,
        "narrow",
        0.1,
        16,
    )
    narrow, packed, wide[1], wide[2] = sync(narrow, packed, wide[1], wide[2])

    narrow = sum_start(narrow)
    packed = packed[0] + flip(packed[1], 2)
    narrow, packed, near, got, fed_near = sync(narrow, packed, near, got, fed_parts[1])

    narrow = sum_merge(narrow, "merge")
    narrow[3] = swap(narrow[3], 2)
    sums = scatter_second(near, got)
    every = gather_small(packed.astype(BF), dp).astype(F32)
    expansion_gradient, contraction_gradient = spread(
        [2, 1], [like(2, lanes, units), like(1, lanes, units)], wide[:3]
    )
    fed_joined = joined(in_hbm(fed_near), fed_got)
    narrow[1], narrow[2], narrow[3], sums, fed_joined, expansion_gradient, every = sync(
        narrow[1], narrow[2], narrow[3], sums, fed_joined, expansion_gradient, every
    )

    narrow[2] = swap(plus(narrow[2], narrow[3]), 4)
    narrow[1] = swap(narrow[1], 2)
    fed_sums = flip(fed_joined[0], 1), flip(fed_joined[1], 2)
    (token_gradient,) = kernel_call(
        token_kernel,
        [like(rows, width)],
        left[0][1], *sums, x, middle_grad, pick[0], table,
        name="token", us=8.0,
    )
    expansion_gradient = jnp.transpose(expansion_gradient, (1, 0, 2))
    modulator_gradient, bias_gradient, gain_sum = kernel_call(
        slots_kernel,
        [like(6, lanes, part), like(6, width), like(1, part)],
        conds, every,
        name="slots", us=8.0,
    )
    narrow[0], expansion_gradient, token_gradient, modulator_gradient = sync(
        narrow[0], expansion_gradient, token_gradient, modulator_gradient
    )
    parts = [part for part in narrow[:3] if part is not None]
    inward_gradient, outward_gradient, layer_output = kernel_call(
        functools.partial(last_kernel, [3, 1], len(parts)),
        [like(3, lanes, part), like(1, lanes, part), like(rows, width, dtype=BF)],
        *parts, fed_parts[0], *fed_sums, middle, pick[0], table,
        name="last",
    )
    return (
        layer_output[None],
        token_gradient[None],
        jnp.transpose(modulator_gradient, (1, 0, 2)),
        bias_gradient,
        jnp.transpose(inward_gradient, (1, 0, 2)),
        gain_sum[0, :head],
        gain_sum[0, head : 2 * head],
        outward_gradient[0],
        expansion_gradient,
        contraction_gradient[0],
    )


def solution(mesh):
    placed = (
        P("dp", "tp", None),
        P("dp", None),
        P(None, None, "tp"),
        P(),
        P(None, None, "tp"),
        P(),
        P(),
        P(None, "tp"),
        P(None, None, "tp"),
        P(None, "tp"),
        P("dp", None),
        P("dp", None),
        P("dp", None),
        P("dp", None),
        P("dp", "tp", None),
    )
    return jax.shard_map(
        shards,
        mesh=mesh,
        in_specs=placed,
        out_specs=(
            P("dp", "tp", None),
            P("dp", "tp", None),
            P("dp", None, "tp"),
            P(),
            P("dp", None, "tp"),
            P(),
            P(),
            P("dp", "tp"),
            P("dp", None, "tp"),
            P("dp", "tp"),
        ),
        check_vma=False,
    )
```

```python
import functools
import math

import jax
import jax.numpy as jnp
from jax import lax
from jax.experimental import pallas as pl
from jax.experimental.pallas import tpu as pltpu
from jax.sharding import PartitionSpec as P

BF = jnp.bfloat16
F32 = jnp.float32
LANES = 128
EPS = 1e-06
NN = ((1,), (0,))
NT = ((1,), (1,))
TN = ((0,), (0,))
MASKED = -30000.0


def dot(left, right, dims):
    return lax.dot_general(left, right, (dims, ((), ())), preferred_element_type=F32)


def flip(value, by):
    return lax.ppermute(value, "tp", [(i, i ^ by) for i in range(4)])


def halves(one, two):
    half = one.shape[0] // 2
    return one[:half], two[half:]


def relay(one, two):
    low, high = halves(one, two)
    return flip(low, 2), flip(high, 1)


def scatter_first(far):
    half = far.shape[0] // 2
    return flip(far[:half], 1), flip(far[half:], 2)


def total(*refs):
    return sum(ref[...].astype(F32) for ref in refs)


def join_kernel(near_ref, via_one_ref, via_two_ref, one_ref, two_ref):
    rows = one_ref.shape[0]
    half = rows // 2
    one_ref[:half, :] = near_ref[:half, :]
    one_ref[half:, :] = near_ref[half:rows, :] + via_two_ref[...]
    two_ref[:half, :] = near_ref[rows : rows + half, :] + via_one_ref[...]
    two_ref[half:, :] = near_ref[rows + half :, :]


def joined(near, got):
    out = like(near.shape[0] // 2, near.shape[1], dtype=near.dtype)
    return kernel_call(join_kernel, [out, out], near, *got, name="join")


def scatter_second(near, got):
    one, two = joined(near, got)
    return flip(one, 1), flip(two, 2)


def gather_core(own, dp):
    return jnp.stack([own, swap(own, 1)]) if dp == 8 else own


def gather_chips(pair, dp):
    if dp != 8:
        return lax.all_gather(pair, "dp", axis=0)
    four = jnp.concatenate([pair, swap(pair, 2)], axis=0)
    return jnp.concatenate([four, swap(four, 4)], axis=0)


def gather_small(own, dp):
    return gather_chips(gather_core(own, dp), dp)


def pack_kernel(order_ref, *refs):
    first, two_ref, fed, gains, out_refs = refs[:3], refs[3], refs[4:7], refs[7:10], refs[10:]
    cut = out_refs[0].shape[-1]
    tall = jnp.concatenate([total(*first), two_ref[...], total(*fed)], axis=0)
    gain = total(*gains)
    gain = jnp.concatenate([gain, jnp.zeros((1, cut - gain.shape[1]), F32)], axis=1)
    parts = [tall[:, j * cut : (j + 1) * cut] for j in range(4)]
    bias = []
    for part in parts:
        bias += [part[2 * j : 2 * j + 1] + part[2 * j + 1 : 2 * j + 2] for j in range(6)]
    below = jnp.concatenate([gain, *bias], axis=0)
    for k in range(4):
        part = parts[0]
        for j in range(1, 4):
            part = jnp.where(order_ref[k] == j, parts[j], part)
        out_refs[k % 2][k // 2] = jnp.concatenate([part, below], axis=0)


def slots_kernel(conds_ref, every_ref, grad_ref, bias_ref, gain_ref):
    conds = conds_ref[...]
    cut = every_ref.shape[2]
    gain_ref[...] = jnp.sum(every_ref[:, 12, :], axis=0, keepdims=True)
    for j in range(6):
        both = [every_ref[:, 2 * j + c, :] for c in range(2)]
        grad_ref[j] = lax.dot_general(
            conds,
            jnp.concatenate(both, axis=0),
            (TN, ((), ())),
            precision=lax.Precision.HIGHEST,
            preferred_element_type=F32,
        )
        for q in range(4):
            own = every_ref[:, 13 + 6 * q + j, :]
            bias_ref[j : j + 1, q * cut : (q + 1) * cut] = jnp.sum(own, axis=0, keepdims=True)


def columns_kernel(pieces, order_ref, *refs):
    add_ref, out_ref = refs[pieces:]
    stacked = jnp.stack([ref[...] for ref in refs[:pieces]])
    parts = []
    for j in range(pieces):
        part = stacked[0]
        for k in range(1, pieces):
            part = jnp.where(order_ref[j] == k, stacked[k], part)
        parts.append(part)
    out = jnp.concatenate(parts, axis=1)
    add = add_ref[...]
    if add.shape[0] < out.shape[0]:
        add = jnp.concatenate([add, add], axis=0)
    out_ref[...] = out + add


def gather_tp_columns(own, add):
    order = jnp.arange(4, dtype=jnp.int32) ^ lax.axis_index("tp")
    (out,) = kernel_call(
        functools.partial(columns_kernel, 4),
        [like(own.shape[0], 4 * own.shape[1])],
        order, own, flip(own, 1), flip(own, 2), flip(own, 3), add,
        scalars=1,
        name="columns",
    )
    return out


def kernel_call(body, outs, *args, aliases=None, name=None, scalars=0, us=1.0, mib=16, hbm=()):
    spec = pl.BlockSpec(memory_space=pltpu.VMEM)
    given = [pl.BlockSpec(memory_space=pltpu.SMEM)] * scalars + [spec] * (len(args) - scalars)
    return pl.pallas_call(
        body,
        out_shape=[pltpu.HBM(o.shape, o.dtype) if i in hbm else o for i, o in enumerate(outs)],
        in_specs=given,
        out_specs=[spec] * len(outs),
        input_output_aliases=aliases or {},
        compiler_params=pltpu.CompilerParams(vmem_limit_bytes=mib * 1024 * 1024),
        cost_estimate=pl.CostEstimate(flops=int(us * 1.15e9), bytes_accessed=1, transcendentals=0),
        name=name,
    )(*args)


def like(*shape, dtype=F32):
    return jax.ShapeDtypeStruct(shape, dtype)


def norm(values):
    count = values.shape[-1]
    center = values - jnp.sum(values, axis=-1, keepdims=True) * (1.0 / count)
    inverse = lax.rsqrt(jnp.sum(center * center, axis=-1, keepdims=True) * (1.0 / count) + EPS)
    return center * inverse, inverse


def norm_back(grad, normed, inverse):
    count = grad.shape[-1]
    middle = jnp.sum(grad, axis=-1, keepdims=True) * (1.0 / count)
    slope = jnp.sum(grad * normed, axis=-1, keepdims=True) * (1.0 / count)
    return inverse * (grad - middle - normed * slope)


def choose(pick, table_ref, column):
    return jnp.where(pick, table_ref[6 + column : 7 + column, :], table_ref[column : column + 1, :])


def slot_sums(pick, values):
    zero = jnp.zeros_like(values)
    return [
        jnp.sum(jnp.where(pick, zero, values), axis=0, keepdims=True),
        jnp.sum(jnp.where(pick, values, zero), axis=0, keepdims=True),
    ]


def picks(pick_ref, width):
    return jnp.broadcast_to(pick_ref[:, 0:1], (pick_ref.shape[0], width)) > 0.5


def lane_sums(values):
    ones = jnp.ones((values.shape[1], values.shape[1]), BF)
    high = values.astype(BF)
    low = (values - high.astype(F32)).astype(BF)
    return dot(high, ones, NN) + dot(low, ones, NN)


def square_sums(values):
    ones = jnp.ones((values.shape[1], values.shape[1]), BF)
    return dot((values * values).astype(BF), ones, NN)


def widen(values):
    return jnp.concatenate(
        [values, jnp.zeros((values.shape[0], LANES - values.shape[1]), values.dtype)], axis=1
    )


def stack_rows(refs):
    return refs[0][...] if len(refs) == 1 else jnp.concatenate([ref[...] for ref in refs], axis=0)


def setup_kernel(head, items, spans, ends_ref, conds_ref, order_ref, places_ref, *out_refs):
    rows = places_ref.shape[0] // 4
    quarter = head // 4
    for s, (low, high) in enumerate(spans):
        count = high - low
        shape = (count, LANES)
        lane = lax.broadcasted_iota(jnp.int32, shape, 1)
        row = lax.broadcasted_iota(jnp.int32, shape, 0)
        start = jnp.full(shape, order_ref[low // rows] * rows, jnp.int32)
        if count > rows:
            start = jnp.where(row >= rows, order_ref[low // rows + 1] * rows - rows, start)
        token = start + row
        owner = jnp.zeros(shape, jnp.int32)
        for j in range(items):
            owner = owner + (token >= ends_ref[j]).astype(jnp.int32)
        pick = jnp.zeros(shape, jnp.int32)
        for j in range(items):
            pick = jnp.where(owner == j, conds_ref[j], pick)
        place = jnp.where(
            lane < 2 * quarter,
            jnp.broadcast_to(places_ref[low:high, 0:1], shape),
            jnp.broadcast_to(places_ref[low:high, 1:2], shape),
        )
        phase = lane
        for j in range(1, 4):
            phase = jnp.where(lane >= j * quarter, lane - j * quarter, phase)
        angles = place * jnp.exp(phase.astype(F32) * (-math.log(10000.0) / quarter))
        real = lane < head
        sine = jnp.sin(angles)
        lower = (lane < quarter) | ((lane >= 2 * quarter) & (lane < 3 * quarter))
        zero = jnp.zeros(shape, F32)
        out_ref, pick_ref = out_refs[2 * s : 2 * s + 2]
        out_ref[0] = jnp.where(real, jnp.cos(angles), zero)
        out_ref[1] = jnp.where(real & lower, -sine, zero)
        out_ref[2] = jnp.where(real & ~lower, sine, zero)
        base = head + 8
        mine = jnp.where(lane == owner + base, 1.0, 0.0)
        out_ref[3] = mine
        marks = jnp.where((lane >= head + 4) & (lane < head + 7), 1.0, zero)
        slots = (lane >= base) & (lane < base + items)
        out_ref[4] = jnp.where(slots, MASKED * (1.0 - mine), marks)
        pick_ref[...] = pick.astype(F32)


def enter_kernel(head, count, *refs):
    x = stack_rows(refs[:count])
    side_ref, pick_ref, table_ref, gain_ref, weight_ref = refs[count : count + 5]
    first_ref, query_ref, key_ref, value_ref, raw_ref = refs[count + 5 :]
    rows, width = x.shape
    part = weight_ref.shape[0] // 3
    heads = part // head
    pick = picks(pick_ref, width)
    normed, _ = norm(x.astype(F32))
    low = (normed * (1.0 + choose(pick, table_ref, 1)) + choose(pick, table_ref, 0)).astype(BF)
    first_ref[...] = low
    raw = dot(low, weight_ref[...], NT)
    raw_ref[...] = raw[:, : 2 * part].astype(BF)
    cosine, near, far = side_ref[0], side_ref[1], side_ref[2]
    scale = math.log2(math.e) / math.sqrt(head)
    for kind in range(2):
        gain = gain_ref[kind : kind + 1, :]
        if kind == 0:
            gain = gain * scale
        target = (query_ref, key_ref)[kind]
        for h in range(heads):
            at = kind * part + h * head
            own = widen(raw[:, at : at + head])
            inverse = lax.rsqrt(square_sums(own) * (1.0 / head) + EPS)
            own = own * inverse * gain
            turned = (
                own * cosine
                + pltpu.roll(own, LANES - head // 4, 1) * near
                + pltpu.roll(own, head // 4, 1) * far
            )
            target[:, pl.ds(h * LANES, LANES)] = (turned + side_ref[3 + kind]).astype(BF)
    lane = lax.broadcasted_iota(jnp.int32, (rows, LANES), 1)
    ones = ((lane >= head) & (lane < head + 3)).astype(F32)
    for h in range(heads):
        at = 2 * part + h * head
        value_ref[:, pl.ds(h * LANES, LANES)] = (widen(raw[:, at : at + head]) + ones).astype(BF)


def split_three(value):
    one = value.astype(BF).astype(F32)
    rest = value - one
    two = rest.astype(BF).astype(F32)
    return one, two, rest - two


def forward_kernel(head, pieces, query_ref, *refs):
    keys, values = refs[:pieces], refs[pieces : 2 * pieces]
    outward_ref, partial_ref, mixed_ref, again_ref = refs[2 * pieces :]
    rows = query_ref.shape[0]
    heads = query_ref.shape[1] // LANES
    lane = lax.broadcasted_iota(jnp.int32, (rows, LANES), 1)
    mixed = []
    for h in range(heads):
        place = pl.ds(h * LANES, LANES)
        query = query_ref[:, place]
        out = None
        for key_ref, value_ref in zip(keys, values):
            weights = jnp.exp2(dot(query, key_ref[:, place], NT)).astype(BF)
            term = dot(weights, value_ref[:, place], NN)
            out = term if out is None else out + term
        total = out[:, head : head + 1]
        mixed.append((out[:, :head] * (1.0 / total)).astype(BF))
        one, two, three = split_three(-jnp.log2(total))
        marks = jnp.where(lane == head + 4, one, 0.0)
        marks = jnp.where(lane == head + 5, two, marks)
        marks = jnp.where(lane == head + 6, three, marks)
        again_ref[:, place] = (query.astype(F32) + marks).astype(BF)
    mixed = jnp.concatenate(mixed, axis=1)
    mixed_ref[...] = mixed
    partial_ref[...] = dot(mixed, outward_ref[...], NN).astype(partial_ref.dtype)


def backward_kernel(head, pieces, first, count, *refs):
    sent = stack_rows(refs[:count])
    outward_ref, mixed_ref, query_ref = refs[count : count + 3]
    refs = refs[count + 3 :]
    keys, values = refs[:pieces], refs[pieces : 2 * pieces]
    refs = refs[2 * pieces :]
    if not first:
        key_in, value_in = refs[:pieces], refs[pieces : 2 * pieces]
        refs = refs[2 * pieces :]
    query_out = refs[0]
    key_out, value_out = refs[1 : 1 + pieces], refs[1 + pieces :]
    rows = query_ref.shape[0]
    heads = query_ref.shape[1] // LANES
    lane = lax.broadcasted_iota(jnp.int32, (rows, LANES), 1)
    grads = dot(sent, outward_ref[...], NT).astype(BF).astype(F32)
    mixed = mixed_ref[...].astype(F32)
    for h in range(heads):
        place = pl.ds(h * LANES, LANES)
        cut = slice(h * head, (h + 1) * head)
        grad = grads[:, cut]
        centre = jnp.sum(grad * mixed[:, cut], axis=-1, keepdims=True)
        one, two, three = split_three(-centre)
        grad = widen(grad)
        grad = jnp.where(lane == head, one, grad)
        grad = jnp.where(lane == head + 1, two, grad)
        grad = jnp.where(lane == head + 2, three, grad).astype(BF)
        query = query_ref[:, place]
        query_grad = None
        for j in range(pieces):
            key, value = keys[j][:, place], values[j][:, place]
            weights = jnp.exp2(dot(key, query, NT))
            score_grad = (weights * dot(value, grad, NT)).astype(BF)
            value_grad = dot(weights.astype(BF), grad, NN)
            key_grad = dot(score_grad, query, NN)
            if not first:
                value_grad += value_in[j][:, place]
                key_grad += key_in[j][:, place]
            value_out[j][:, place] = value_grad
            key_out[j][:, place] = key_grad
            term = dot(key, score_grad, TN)
            query_grad = term if query_grad is None else query_grad + term
        query_out[:, place] = query_grad.T


def leave_kernel(head, count, *refs):
    x = stack_rows(refs[:count])
    query_grad_ref, key_grad_ref, value_grad_ref, raw_ref, side_ref, pick_ref = refs[count : count + 6]
    gain_ref, weight_ref, projected_ref, partial_ref, slots_ref, gains_ref = refs[count + 6 :]
    rows, width = x.shape
    part = weight_ref.shape[0] // 3
    heads = part // head
    cosine, near, far = side_ref[0], side_ref[1], side_ref[2]
    raw = raw_ref[...].astype(F32)
    pieces = []
    gain_grads = []
    for kind in range(2):
        gain = gain_ref[kind : kind + 1, :]
        source = (query_grad_ref, key_grad_ref)[kind]
        scale = (1.0 / math.sqrt(head), math.log(2.0))[kind]
        gain_grad = None
        for h in range(heads):
            grad = source[:, pl.ds(h * LANES, LANES)] * scale
            grad = (
                grad * cosine
                + pltpu.roll(grad * near, head // 4, 1)
                + pltpu.roll(grad * far, LANES - head // 4, 1)
            )
            at = kind * part + h * head
            own = widen(raw[:, at : at + head])
            inverse = lax.rsqrt(square_sums(own) * (1.0 / head) + EPS)
            own = own * inverse
            term = grad * own
            gain_grad = term if gain_grad is None else gain_grad + term
            slope = lane_sums(term * gain) * (1.0 / head)
            pieces.append((inverse * (grad * gain - own * slope))[:, :head].astype(BF))
        gain_grad = jnp.sum(gain_grad, axis=0, keepdims=True)
        gain_grads.append(gain_grad[:, :head])
    gains_ref[...] = jnp.concatenate(gain_grads, axis=1)
    for h in range(heads):
        pieces.append(value_grad_ref[:, pl.ds(h * LANES, head)].astype(BF))
    projected = jnp.concatenate(pieces, axis=1)
    projected_ref[...] = projected
    grad = dot(projected, weight_ref[...], NN)
    partial_ref[...] = grad.astype(partial_ref.dtype)
    pick = picks(pick_ref, width)
    normed, _ = norm(x.astype(F32))
    slots_ref[...] = jnp.concatenate(slot_sums(pick, grad) + slot_sums(pick, grad * normed), axis=0)


def middle_kernel(x_ref, own_ref, one_ref, two_ref, side_ref, table_ref,
                  attended_ref, middle_ref, second_ref):
    attended = total(own_ref, one_ref, two_ref)
    attended_ref[...] = attended.astype(BF)
    pick = picks(side_ref, x_ref.shape[1])
    middle = x_ref[...].astype(F32) + choose(pick, table_ref, 2) * attended
    middle_ref[...] = middle
    normed, _ = norm(middle)
    second_ref[...] = (
        normed * (1.0 + choose(pick, table_ref, 4)) + choose(pick, table_ref, 3)
    ).astype(BF)


def units_kernel(count, *refs):
    second = stack_rows(refs[:count])
    grad_ref, weight_ref, hidden_ref, widening_ref, partial_ref = refs[count:]
    units = grad_ref.shape[1]
    both = dot(second, weight_ref[...], NN)
    gate, up = both[:, :units], both[:, units:]
    sigmoid = 1.0 / (1.0 + jnp.exp(-gate))
    active = gate * sigmoid
    hidden_ref[...] = (active * up).astype(BF)
    grad = grad_ref[...]
    gate_grad = (grad * up * (sigmoid + active * (1.0 - sigmoid))).astype(BF)
    widening = jnp.concatenate([gate_grad, (grad * active).astype(BF)], axis=1)
    widening_ref[...] = widening
    partial_ref[...] = dot(widening, weight_ref[...], NT).astype(partial_ref.dtype)


def hidden_grad_kernel(count, *refs):
    dy = stack_rows(refs[:count])
    side_ref, table_ref, weight_ref, fed_ref, out_ref = refs[count:]
    pick = picks(side_ref, dy.shape[1])
    fed = (choose(pick, table_ref, 5) * dy.astype(F32)).astype(BF)
    fed_ref[...] = fed
    out_ref[...] = dot(fed, weight_ref[...], NN)


def fed_part_kernel(count, *refs):
    dy = stack_rows(refs[:count])
    hidden_ref, side_ref, weight_ref, out_ref, slots_ref = refs[count:]
    fed = dot(hidden_ref[...], weight_ref[...], NT)
    out_ref[...] = fed.astype(BF)
    slots_ref[...] = jnp.concatenate(
        slot_sums(picks(side_ref, dy.shape[1]), dy.astype(F32) * fed), axis=0
    )


def weights_kernel(counts, cuts, core_ref, *refs):
    *refs, room_ref, sems = refs
    pairs = []
    for lefts, rights in counts:
        pairs.append((refs[:lefts], stack_rows(refs[lefts : lefts + rights])))
        refs = refs[lefts + rights :]
    outs = refs
    height = room_ref.shape[0]
    blocks = len(outs) * outs[0].shape[0]
    size = height // blocks
    copies = []
    step = height // cuts
    for low in range(0, height, step):
        at = 0
        for lefts, right in pairs:
            left = [ref[:, low : low + step] for ref in lefts]
            left = left[0] if len(left) == 1 else jnp.concatenate(left, axis=0)
            high = at + right.shape[1]
            room_ref[low : low + step, at:high] = dot(left, right, TN).astype(BF)
            at = high
        while len(copies) < blocks and (len(copies) + 1) * size <= low + step:
            j = len(copies)
            rows = room_ref.at[j * size : (j + 1) * size, :]
            to = [pltpu.make_async_copy(rows, out.at[j // len(outs)], sems.at[j]) for out in outs]
            if len(outs) == 1:
                to[0].start()
            else:

                @pl.when(core_ref[0] == j % 2)
                def _(copy=to[0]):
                    copy.start()

                @pl.when(core_ref[0] != j % 2)
                def _(copy=to[1]):
                    copy.start()

            copies.append(to[0])
    for copy in copies:
        copy.wait()


def weights_call(pairs, dp, name, us, mib):
    args, counts = [], []
    for lefts, rights in pairs:
        args += [*lefts, *rights]
        counts.append((len(lefts), len(rights)))
    height = pairs[0][0][0].shape[1]
    wide = sum(rights[0].shape[1] for _, rights in pairs)
    outs = 2 if dp == 8 else 1
    blocks = dp if outs == 2 else 1
    return pl.pallas_call(
        functools.partial(weights_kernel, counts, 3),
        out_shape=[pltpu.HBM((blocks // outs, height // blocks, wide), BF)] * outs,
        in_specs=[pl.BlockSpec(memory_space=pltpu.SMEM)]
        + [pl.BlockSpec(memory_space=pltpu.VMEM)] * len(args),
        out_specs=[pl.BlockSpec(memory_space=pltpu.HBM)] * outs,
        scratch_shapes=[pltpu.VMEM((height, wide), BF), pltpu.SemaphoreType.DMA((blocks,))],
        compiler_params=pltpu.CompilerParams(vmem_limit_bytes=mib * 1024 * 1024),
        cost_estimate=pl.CostEstimate(flops=int(us * 1.15e9), bytes_accessed=1, transcendentals=0),
        name=name,
    )((lax.axis_index("dp") % 2).reshape(1).astype(jnp.int32), *args)


def swap(value, by):
    return None if value is None else lax.ppermute(value, "dp", [(i, i ^ by) for i in range(8)])


def merge_kernel(place_ref, keep_ref, got_ref, *out_refs):
    for k, ref in enumerate(out_refs):
        at = place_ref[0] ^ k
        ref[...] = keep_ref[at] + got_ref[at]


def sum_start(outs):
    if len(outs) == 1:
        total_sum = lax.psum_scatter(outs[0][0], "dp", scatter_dimension=0, tiled=True)
        return [total_sum, None, None, None]
    return [outs[0], swap(outs[1], 1), None, None]


def sum_merge(parts, name):
    if parts[1] is None:
        return parts
    _, size, wide = parts[0].shape
    place = (lax.axis_index("dp") // 2).reshape(1).astype(jnp.int32)
    outs = kernel_call(
        merge_kernel,
        [like(size, wide, dtype=BF)] * 4,
        place, in_hbm(parts[0]), parts[1],
        scalars=1, name=name, us=3.0, hbm=(0,),
    )
    return list(outs)


def plus(left, right):
    return None if left is None else left + right


def spread(groups, outs, parts):
    parts = [part for part in parts if part is not None]
    return kernel_call(
        functools.partial(spread_kernel, groups, len(parts)), outs, *parts, name="spread"
    )


def in_hbm(value):
    return pltpu.with_memory_space_constraint(value, pltpu.HBM)


def middle_back_kernel(own_ref, one_ref, two_ref, middle_ref, attended_ref, dy_ref, side_ref, table_ref,
                       grad_ref, send_ref, slots_ref):
    pick = picks(side_ref, dy_ref.shape[1])
    second_grad = total(own_ref, one_ref, two_ref)
    normed, inverse = norm(middle_ref[...])
    grad = dy_ref[...].astype(F32) + norm_back(
        second_grad * (1.0 + choose(pick, table_ref, 4)), normed, inverse
    )
    grad_ref[...] = grad
    send_ref[...] = (choose(pick, table_ref, 2) * grad).astype(BF)
    slots_ref[...] = jnp.concatenate(
        slot_sums(pick, grad * attended_ref[...].astype(F32))
        + slot_sums(pick, second_grad)
        + slot_sums(pick, second_grad * normed),
        axis=0,
    )


def fed_kernel(own_ref, one_ref, two_ref, middle_ref, side_ref, table_ref, out_ref):
    pick = picks(side_ref, middle_ref.shape[1])
    fed = total(own_ref, one_ref, two_ref)
    out_ref[...] = (middle_ref[...] + choose(pick, table_ref, 5) * fed).astype(BF)


def spread_kernel(groups, count, *refs):
    parts, out_refs = refs[:count], refs[count:]
    at = 0
    for group, ref in zip(groups, out_refs):
        width = ref.shape[-1]
        for j in range(group):
            ref[j] = total(*[part.at[:, at : at + width] for part in parts])
            at += width


def last_kernel(groups, count, *refs):
    outs = len(groups)
    spread_kernel(groups, count, *refs[:count], *refs[count + 6 : count + 6 + outs])
    fed_kernel(*refs[count : count + 6], refs[-1])


def token_kernel(own_ref, one_ref, two_ref, x_ref, grad_ref, side_ref, table_ref, out_ref):
    pick = picks(side_ref, x_ref.shape[1])
    first_grad = total(own_ref, one_ref, two_ref)
    normed, inverse = norm(x_ref[...].astype(F32))
    out_ref[...] = grad_ref[...] + norm_back(
        first_grad * (1.0 + choose(pick, table_ref, 1)), normed, inverse
    )


def sync(*values):
    return lax.optimization_barrier(values)


def shards(
    tokens,
    condition,
    modulator,
    offsets,
    inward,
    query_gain,
    key_gain,
    outward,
    expansion,
    contraction,
    item_lengths,
    item_condition,
    patch_rows,
    patch_columns,
    cotangent,
):
    _, rows, width = tokens.shape
    full = patch_rows.shape[1]
    head = query_gain.shape[0]
    part = inward.shape[2]
    heads = part // head
    units = contraction.shape[1]
    items = item_lengths.shape[1]
    dp = lax.axis_size("dp")
    me = lax.axis_index("tp")
    dp_me = lax.axis_index("dp")
    lanes = width // dp
    padded = heads * LANES
    spans = ((0, rows), (rows, 3 * rows), (3 * rows, full))
    sizes = [high - low for low, high in spans]

    x, dy = tokens[0], cotangent[0]
    x_one, x_two = flip(x, 1), flip(x, 2)
    cond_low = jax.nn.silu(condition.astype(F32)).astype(BF)
    share = dot(cond_low, jnp.transpose(modulator, (1, 2, 0)).reshape(-1, width), NT)
    share = share.reshape(12, part)
    inward_rows = jnp.transpose(inward, (1, 2, 0)).reshape(3 * part, width)
    outward_rows = outward.T
    gains = jnp.pad(jnp.stack([query_gain, key_gain]), ((0, 0), (0, LANES - head)))
    order = jnp.arange(4, dtype=jnp.int32) ^ me
    places = jnp.stack([patch_rows[0], patch_columns[0]], axis=1).astype(F32)
    places = jnp.take(places.reshape(4, rows, 2), order, axis=0).reshape(full, 2)
    ends = jnp.cumsum(item_lengths[0])
    share, order, places, ends = sync(share, order, places, ends)
    shares = [share, flip(share, 1), flip(share, 2), flip(share, 3)]
    side = kernel_call(
        functools.partial(setup_kernel, head, items, spans),
        [out for n in sizes for out in (like(5, n, LANES), like(n, LANES))],
        ends, item_condition[0], order, places,
        scalars=3, name="setup", us=3.0, hbm=(0, 2, 4),
    )
    order, *both = sync(order, *shares, *side)
    shares, side, pick = both[:4], both[4::2], both[5::2]
    (table,) = kernel_call(
        functools.partial(columns_kernel, 4),
        [like(12, width)],
        order, *[in_hbm(share) for share in shares], offsets,
        scalars=1, name="columns",
    )
    x_halves = halves(x_one, x_two)
    x_one, x_two, dy, table, *x_halves = sync(x_one, x_two, dy, table, *x_halves)

    x_far = flip(x_halves[0], 2), flip(x_halves[1], 1)
    x_parts = [[x], [x_one, x_two], list(x_far)]

    def enter(k, parts):
        n = sizes[k]
        return kernel_call(
            functools.partial(enter_kernel, head, len(parts)),
            [
                like(n, width, dtype=BF),
                like(n, padded, dtype=BF),
                like(n, padded, dtype=BF),
                like(n, padded, dtype=BF),
                like(n, 2 * part, dtype=BF),
            ],
            *parts, side[k], pick[k], table, gains, inward_rows,
            name="enter", hbm=(0, 1, 4) if k == 0 else (0, 4), us=3.3 * n / rows,
        )

    entered = [None, list(enter(1, x_parts[1]))]
    x_far, dy, entered[1][1], x_own = sync(x_far, dy, entered[1][1], x)
    dy_one, dy_two = flip(dy, 1), flip(dy, 2)
    entered[0] = list(enter(0, [x_own]))
    x_far = list(x_far)
    x_parts[2] = x_far

    entered.append(enter(2, x_far))
    first_in, queries, keys, values, raws = zip(*entered)

    def attend(k, query):
        n = sizes[k]
        return kernel_call(
            functools.partial(forward_kernel, head, 3),
            [like(n, width, dtype=BF), like(n, part, dtype=BF), like(n, padded, dtype=BF)],
            query, *keys, *values, outward_rows,
            name="attend", hbm=(1, 2) if k == 2 else (), us=2.0 * n / rows,
        )

    attended = [None, None, attend(2, queries[2])]
    far, query_near = sync(attended[2][0], queries[1])

    got = scatter_first(far)
    attended[1] = attend(1, query_near)
    near, query_own, dy_one, dy_two = sync(attended[1][0], queries[0], dy_one, dy_two)
    dy_halves = halves(dy_one, dy_two)
    near, query_own, got, dy_halves = sync(near, query_own, got, dy_halves)

    sums = scatter_second(near, got)
    attended[0] = attend(0, query_own)
    own, dy_halves, expansion = sync(attended[0][0], dy_halves, expansion)
    expansion_flat = expansion.reshape(width, 2 * units)
    dy_far = [flip(dy_halves[0], 2), flip(dy_halves[1], 1)]
    own, cond_low, sums, dy_far, expansion_flat = sync(own, cond_low, sums, dy_far, expansion_flat)

    attended_own, middle, second = kernel_call(
        middle_kernel,
        [like(rows, width, dtype=BF), like(rows, width), like(rows, width, dtype=BF)],
        x, own, *sums, pick[0], table,
        name="middle", hbm=(0, 1),
    )
    second, cond_low, dy, dy_one, dy_two = sync(second, cond_low, dy, dy_one, dy_two)
    second_one, second_two = flip(second, 1), flip(second, 2)
    dy_parts = [[dy], [dy_one, dy_two], dy_far]
    fed_grad, hidden_grad = [], []
    for k in range(3):
        outs = kernel_call(
            functools.partial(hidden_grad_kernel, len(dy_parts[k])),
            [like(sizes[k], width, dtype=BF), like(sizes[k], units)],
            *dy_parts[k], pick[k], table, contraction,
            name="hidden_grad", us=0.8 * sizes[k] / rows,
        )
        fed_grad.append(outs[0])
        hidden_grad.append(outs[1])
    conds = jnp.transpose(gather_small(cond_low, dp), (1, 0, 2)).reshape(2 * dp, width)
    conds = lax.dynamic_slice_in_dim(conds, dp_me * lanes, lanes, 1).astype(F32)
    second_one, second_two, conds, *hidden_grad = sync(second_one, second_two, conds, *hidden_grad)

    second_far = relay(second_one, second_two)
    second_parts = [[second], [second_one, second_two], list(second_far)]

    def through(k, parts):
        n = sizes[k]
        return kernel_call(
            functools.partial(units_kernel, len(parts)),
            [
                like(n, units, dtype=BF),
                like(n, 2 * units, dtype=BF),
                like(n, width, dtype=BF),
            ],
            *parts, hidden_grad[k], expansion_flat,
            name="units", hbm=() if k == 2 else (2,), us=2.5 * n / rows,
        )

    passed = [through(0, second_parts[0]), through(1, second_parts[1])]
    *second_far, near, own = sync(*second_far, passed[1][2], passed[0][2])
    second_parts[2] = second_far
    passed.append(through(2, second_far))
    hidden, widening, back = zip(*passed)
    far, hidden_far = sync(back[2], hidden[2])

    got = scatter_first(far)
    wide = weights_call(
        [
            (sum(second_parts, []), widening),
            (fed_grad, [*hidden[:2], hidden_far]),
        ],
        dp,
        "wide",
        6.0,
        18,
    )
    wide, near, hidden_far, got = sync(wide, near, hidden_far, got)

    sums = scatter_second(in_hbm(near), [in_hbm(g) for g in got])
    wide = sum_start(wide)
    fed_parts, fed_slots = [None] * 3, [None] * 3
    for k, source in ((1, hidden[1]), (2, hidden_far), (0, hidden[0])):
        if k == 2:
            fed_parts[1], wide, source = sync(fed_parts[1], wide, source)
            wide = sum_merge(wide, "merge")
        if k == 0:
            fed_parts[2], wide, source = sync(fed_parts[2], wide, source)
            wide[3] = swap(wide[3], 2)
        fed_parts[k], fed_slots[k] = kernel_call(
            functools.partial(fed_part_kernel, len(dy_parts[k])),
            [like(sizes[k], width, dtype=BF), like(2, width)],
            *dy_parts[k], source, pick[k], contraction,
            name="fed_part", hbm=(0, 1), us=1.0 * sizes[k] / rows,
        )
    own, sums, fed_parts[0] = sync(own, sums, fed_parts[0])

    middle_grad, send, slots_two = kernel_call(
        middle_back_kernel,
        [like(rows, width), like(rows, width, dtype=BF), like(6, width)],
        own, *sums, middle, attended_own, dy, pick[0], table,
        name="middle_back", hbm=(0, 2), us=1.7,
    )
    send_one, send_two = flip(send, 1), flip(send, 2)

    def attend_back(k, parts, sums):
        n = sizes[k]
        given = (*parts, outward_rows, attended[k][1], attended[k][2], *keys, *values)
        out = kernel_call(
            functools.partial(backward_kernel, head, 3, not sums, len(parts)),
            [like(n, padded)] + [like(a.shape[0], padded) for a in keys + values],
            *given, *sums,
            aliases={len(given) + i: 1 + i for i in range(len(sums))},
            name="attend_back", us=4.3 * n / rows, mib=16,
        )
        return out[0], tuple(out[1:])

    query_grads = [None] * 3
    query_grads[0], totals = attend_back(0, [send], ())
    totals, wide = sync(totals, wide)
    wide[2] = swap(plus(wide[2], wide[3]), 4)
    send_one, send_two, totals = sync(send_one, send_two, totals)

    send_far = relay(send_one, send_two)
    query_grads[1], totals = attend_back(1, [send_one, send_two], totals)
    send_far, totals, fed_far, wide[1] = sync(send_far, totals, fed_parts[2], wide[1])

    fed_got = scatter_first(fed_far)
    wide[1] = swap(wide[1], 2)
    send_parts = [[send], [send_one, send_two], list(send_far)]
    query_grads[2], totals = attend_back(2, send_far, totals)
    key_grads, value_grads = totals[:3], totals[3:]

    def leave(k, query_grad):
        n = sizes[k]
        return kernel_call(
            functools.partial(leave_kernel, head, len(x_parts[k])),
            [
                like(n, 3 * part, dtype=BF),
                like(n, width, dtype=BF),
                like(4, width),
                like(1, 2 * head),
            ],
            *x_parts[k], query_grad, key_grads[k], value_grads[k], raws[k], side[k], pick[k], gains,
            inward_rows,
            name="leave", hbm=(0, 2, 3), us=3.8 * n / rows,
        )

    left = [None, None, leave(2, query_grads[2])]
    far, query_near, fed_near, fed_got = sync(left[2][1], query_grads[1], fed_parts[1], fed_got)

    got = scatter_first(far)
    left[1] = leave(1, query_near)
    near, query_own, got = sync(left[1][1], query_grads[0], got)

    left[0] = sync(*leave(0, query_own))

    parts = left[0][2], left[1][2], left[2][2], slots_two, *fed_slots
    packed = kernel_call(
        pack_kernel,
        [like(2, 37, part)] * 2,
        order, *[in_hbm(v) for v in (*parts, left[0][3], left[1][3], left[2][3])],
        scalars=1, name="pack", us=1.0,
    )
    packed = packed[0] + flip(packed[1], 1)
    narrow = weights_call(
        [
            (first_in, [left[k][0] for k in range(3)]),
            (sum(send_parts, []), [attended[k][1] for k in range(3)]),
        ],
        dp,
        "narrow",
        0.1,
        16,
    )
    narrow, packed, wide[1], wide[2] = sync(narrow, packed, wide[1], wide[2])

    narrow = sum_start(narrow)
    packed = packed[0] + flip(packed[1], 2)
    narrow, packed, near, got, fed_near = sync(narrow, packed, near, got, fed_parts[1])

    narrow = sum_merge(narrow, "merge")
    narrow[3] = swap(narrow[3], 2)
    sums = scatter_second(near, got)
    every = gather_small(packed.astype(BF), dp).astype(F32)
    expansion_gradient, contraction_gradient = spread(
        [2, 1], [like(2, lanes, units), like(1, lanes, units)], wide[:3]
    )
    fed_joined = joined(in_hbm(fed_near), fed_got)
    narrow[1], narrow[2], narrow[3], sums, fed_joined, expansion_gradient, every = sync(
        narrow[1], narrow[2], narrow[3], sums, fed_joined, expansion_gradient, every
    )

    narrow[2] = swap(plus(narrow[2], narrow[3]), 4)
    narrow[1] = swap(narrow[1], 2)
    fed_sums = flip(fed_joined[0], 1), flip(fed_joined[1], 2)
    (token_gradient,) = kernel_call(
        token_kernel,
        [like(rows, width)],
        left[0][1], *sums, x, middle_grad, pick[0], table,
        name="token", us=8.0,
    )
    expansion_gradient = jnp.transpose(expansion_gradient, (1, 0, 2))
    modulator_gradient, bias_gradient, gain_sum = kernel_call(
        slots_kernel,
        [like(6, lanes, part), like(6, width), like(1, part)],
        conds, every,
        name="slots", us=8.0,
    )
    narrow[0], expansion_gradient, token_gradient, modulator_gradient = sync(
        narrow[0], expansion_gradient, token_gradient, modulator_gradient
    )
    parts = [part for part in narrow[:3] if part is not None]
    inward_gradient, outward_gradient, layer_output = kernel_call(
        functools.partial(last_kernel, [3, 1], len(parts)),
        [like(3, lanes, part), like(1, lanes, part), like(rows, width, dtype=BF)],
        *parts, fed_parts[0], *fed_sums, middle, pick[0], table,
        name="last",
    )
    return (
        layer_output[None],
        token_gradient[None],
        jnp.transpose(modulator_gradient, (1, 0, 2)),
        bias_gradient,
        jnp.transpose(inward_gradient, (1, 0, 2)),
        gain_sum[0, :head],
        gain_sum[0, head : 2 * head],
        outward_gradient[0],
        expansion_gradient,
        contraction_gradient[0],
    )


def solution(mesh):
    placed = (
        P("dp", "tp", None),
        P("dp", None),
        P(None, None, "tp"),
        P(),
        P(None, None, "tp"),
        P(),
        P(),
        P(None, "tp"),
        P(None, None, "tp"),
        P(None, "tp"),
        P("dp", None),
        P("dp", None),
        P("dp", None),
        P("dp", None),
        P("dp", "tp", None),
    )
    return jax.shard_map(
        shards,
        mesh=mesh,
        in_specs=placed,
        out_specs=(
            P("dp", "tp", None),
            P("dp", "tp", None),
            P("dp", None, "tp"),
            P(),
            P("dp", None, "tp"),
            P(),
            P(),
            P("dp", "tp"),
            P("dp", None, "tp"),
            P("dp", "tp"),
        ),
        check_vma=False,
    )
```
